256 devices in a mesh: dp: 16 (over x, y), vocab: 16 (over z, core).
Axes of the slice: x: 4, y: 4, z: 8, core: 2. Of those that a mesh axis runs over, the one named last changes fastest.
Arguments:
- hidden: bfloat16 [2048, 2048], P('dp'), may hold values from -8 to 8
- head_weight: bfloat16 [131072, 2048], P(('dp', 'vocab')), may hold values from -0.397747564 to 0.397747564
- sampled_ids: int32 [2048], replicated, may hold values from 0 to 131071
- advantage: float32 [2048], replicated, may hold values from -4 to 4
Outputs:
- log_prob: float32 [2048], P('dp')
- entropy: float32 [2048], P('dp')
- grad_hidden: float32 [2048, 2048], P('dp', 'vocab')
- grad_weight: float32 [131072, 2048], P(('dp', 'vocab'))
The draws below stay inside these ranges and needn't reach their ends.
All inputs are finite; a program needn't handle non-finite values.
Results may differ from the reference program's by a relative error of at most 0.0028.
Values may be sent and summed in bfloat16 or wider, within the bound.
A program may use at most 128 MiB of HBM per device.

```python
import math
import jax
import jax.numpy as jnp
from jax import lax

D = 2048
ROWS_DEV = 512
TOKENS = 2048
VOCAB = 131072
N_DP = 16
N_VOCAB = 16


def draw_hidden(key, part):
    key = jax.random.fold_in(key, 11)
    values = jnp.clip(jax.random.normal(key, (TOKENS, D), jnp.float32), -8.0, 8.0)
    return values.astype(jnp.bfloat16)


def draw_head_weight(key, part):
    key = jax.random.fold_in(key, 23)
    spread = 3.0 / math.sqrt(D)
    values = jnp.clip(jax.random.normal(key, (VOCAB, D), jnp.float32), -6.0, 6.0) * spread
    return values.astype(jnp.bfloat16)


def plant(drawn, rng, low, top_value):
    index_at = [jax.random.randint(jax.random.fold_in(rng, axis), (), 0, length) for axis, length in enumerate(drawn.shape)]
    longest = drawn.shape.index(max(drawn.shape))
    next_to = index_at[:longest] + [(index_at[longest] + 1) % drawn.shape[longest]] + index_at[longest + 1:]
    return drawn.at[tuple(index_at)].set(low).at[tuple(next_to)].set(top_value)


def centred(rng, shape, scale, reach, held_as=jnp.bfloat16):
    return jnp.clip(scale * jax.random.normal(rng, shape, jnp.float32), -reach, reach).astype(held_as)


def setup_inputs(seed: int = 0) -> dict:
    keys = jax.random.split(jax.random.key(seed), 5)
    return {
        "hidden": draw_hidden(jax.random.fold_in(keys[4], 71), 0),
        "head_weight": draw_head_weight(jax.random.fold_in(keys[4], 71), 0),
        "sampled_ids": plant(jax.random.randint(keys[2], (TOKENS,), 0, VOCAB), jax.random.fold_in(keys[2], 1), 0, VOCAB - 1).astype(jnp.int32),
        "advantage": centred(keys[3], (TOKENS,), 1.0, 4.0, jnp.float32),
    }


entropy_coef = 0.25


def block_logits(hidden, block):
    return lax.dot_general(hidden, block, (((1,), (1,)), ((), ())), preferred_element_type=jnp.float32)


def reference(hidden, head_weight, sampled_ids, advantage):
    span = ROWS_DEV * N_VOCAB
    blocks = head_weight.reshape(N_DP, span, D)
    offsets = (jnp.arange(N_DP) * span).astype(jnp.int32)

    def stats_step(carry, inputs):
        running_max, total, weighted, target = carry
        block, offset = inputs
        logits = block_logits(hidden, block)
        columns = offset + jnp.arange(span).astype(jnp.int32)
        picked = sampled_ids[:, None] == columns[None, :]
        new_max = jnp.maximum(running_max, jnp.max(logits, axis=1))
        shrink = jnp.exp(running_max - new_max)
        expon = jnp.exp(logits - new_max[:, None])
        total = total * shrink + jnp.sum(expon, axis=1)
        weighted = weighted * shrink + jnp.sum(expon * logits, axis=1)
        target = target + jnp.sum(jnp.where(picked, logits, jnp.zeros_like(logits)), axis=1)
        return (new_max, total, weighted, target), None

    start_state = (jnp.full((TOKENS,), -1e30, jnp.float32), jnp.zeros((TOKENS,), jnp.float32),
                   jnp.zeros((TOKENS,), jnp.float32), jnp.zeros((TOKENS,), jnp.float32))
    (running_max, total, weighted, target), _ = lax.scan(stats_step, start_state, (blocks, offsets))
    log_total = running_max + jnp.log(total)
    mean_logit = weighted / total
    log_prob = target - log_total
    entropy = log_total - mean_logit

    def grad_step(carry, inputs):
        block, offset = inputs
        logits = block_logits(hidden, block)
        columns = offset + jnp.arange(span).astype(jnp.int32)
        picked = (sampled_ids[:, None] == columns[None, :]).astype(jnp.float32)
        prob = jnp.exp(logits - log_total[:, None])
        grad_logits = advantage[:, None] * (picked - prob) - entropy_coef * prob * (logits - mean_logit[:, None])
        grad_low = grad_logits.astype(jnp.bfloat16)
        grad_block = lax.dot_general(grad_low, hidden, (((0,), (0,)), ((), ())), preferred_element_type=jnp.float32)
        carry = carry + jnp.dot(grad_low, block, preferred_element_type=jnp.float32)
        return carry, grad_block

    grad_hidden, grad_blocks = lax.scan(grad_step, jnp.zeros((TOKENS, D), jnp.float32), (blocks, offsets))
    grad_weight = grad_blocks.reshape(VOCAB, D)
    return (log_prob, entropy, grad_hidden, grad_weight)
```

```python
import jax
import jax.numpy as jnp
from jax import lax
from jax.experimental import pallas as pl
from jax.experimental.pallas import tpu as pltpu
from jax.sharding import PartitionSpec as P

ENTROPY_COEF = 0.25
MESH = pl.DeviceIdType.MESH
F32, BF16 = jnp.float32, jnp.bfloat16

D = 2048
V = 1024
ROWS = 512
SHARD = 128
RING = 4
NZ = 8
H = 2
R = 16
BLK = 2 * RING * R
HALF = RING * R
NB = RING * H
VC = 512
NC = 512
NSEM = 128


def kernel(hid, w, ids, adv, gw_out, gh_out, lp_out, en_out,
           hall, wall, logits, grad, grad_t, pm, x1, y1, r1, x2, y2, zs, zr, st, sx, sy, sz, fin,
           ids_in, adv_in, rolled, ids_row, adv_row, stat_swap, gw_send, gw_recv, send_sem, recv_sem, z_sem, local_sem):
    dp, vo = lax.axis_index("dp"), lax.axis_index("vocab")
    x, y = lax.div(dp, RING), lax.rem(dp, RING)
    z, core = lax.div(vo, 2), lax.rem(vo, 2)
    pa, pb = x + core * (y - x), y + core * (x - y)
    a_p, a_2, a_m = (lax.rem(pa + k, RING) for k in (1, 2, 3))
    b_p, b_2, b_m = (lax.rem(pb + k, RING) for k in (1, 2, 3))

    def place(a, b):
        first, second = a * RING + b, b * RING + a
        return first + core * (second - first)

    def dev(a, b):
        return {"dp": place(a, b), "vocab": vo}

    def zdev(k):
        return {"dp": dp, "vocab": lax.rem(z + k, NZ) * 2 + core}

    sibling = {"dp": dp, "vocab": vo + 1 - 2 * core}

    copies = []

    def remote(src, dst, device, arrival=None):
        i = len(copies)
        copies.append(pltpu.make_async_remote_copy(
            src_ref=src, dst_ref=dst, send_sem=send_sem.at[i], recv_sem=recv_sem.at[i] if arrival is None else arrival,
            device_id=device, device_id_type=MESH))
        return copies[-1]

    def start(*some):
        for copy in some:
            copy.start()

    def arrive(*some):
        for copy in some:
            copy.wait_recv()

    w_rows = pl.ds(pl.multiple_of(core * ROWS, ROWS), ROWS)
    w_in = pltpu.make_async_copy(w, wall.at[w_rows], local_sem.at[0])
    small_in = [pltpu.make_async_copy(ids, ids_in, local_sem.at[1]),
                pltpu.make_async_copy(adv, adv_in, local_sem.at[2])]
    own_in = [pltpu.make_async_copy(hid.at[core, h], hall.at[h * RING + pb, :, pa], local_sem.at[3 + h])
              for h in range(H)]
    for c in [w_in] + small_in + own_in:
        c.start()

    a_dev = [dev(lax.rem(pa + k, RING), pb) for k in (1, 2, 3)]
    b_dev = [dev(pa, lax.rem(pb + k, RING)) for k in (1, 2, 3)]
    z_dev = [zdev(k) for k in range(1, NZ)]
    ap, _, am = a_dev
    bp, _, bm = b_dev
    barrier = pltpu.get_barrier_semaphore()
    z_both = [[dict(dp=dp, vocab=lax.rem(z + k, NZ) * 2 + f) for f in range(2)] for k in range(1, NZ)]
    peers = a_dev + b_dev + [d for both in z_both for d in both] + [sibling]
    for peer in peers:
        pl.semaphore_signal(barrier, inc=1, device_id=peer, device_id_type=MESH)

    w_swap = remote(wall.at[w_rows], wall.at[w_rows], sibling)

    class Gather:
        def __init__(self, h):
            kp, km, k0 = (h * RING + b for b in (b_p, b_m, pb))
            own, there = hid.at[core, h], hall.at[k0, :, pa]
            self.near = [remote(own, there, d) for d in (ap, am)]
            self.far = [remote(hall.at[k0, 0, a_m], hall.at[k0, 0, a_m], ap),
                        remote(hall.at[k0, 1, a_p], hall.at[k0, 1, a_p], am)]
            self.spread, self.pass_on = {}, {}
            for slot, src in (("own", pa), ("m", a_m), ("p", a_p), ("2", a_2)):
                ref = hall.at[k0, :, src]
                self.spread[slot] = [remote(own if slot == "own" else ref, ref, d) for d in (bp, bm)]
                one, two = hall.at[km, 0, src], hall.at[kp, 1, src]
                self.pass_on[slot] = [remote(one, one, bp), remote(two, two, bm)]

        def ring(self):
            for near, far in zip(self.near, self.far):
                arrive(near)
                start(far)

        def spread_on(self, *slots):
            for slot in slots:
                start(*self.spread[slot])

        def ring_far(self):
            arrive(*self.far)
            start(*self.spread["2"])

        def forward(self, *slots):
            for slot in slots:
                for came, on in zip(self.spread[slot], self.pass_on[slot]):
                    arrive(came)
                    start(on)

        def last(self):
            for on in self.pass_on.values():
                arrive(*on)

    g0, g1 = Gather(0), Gather(1)

    lane = lax.broadcasted_iota(jnp.int32, (8, 128), 1)

    def lanes_of(group):
        return lax.div(lane, R) == group

    def reorder(source, out):
        both = source[...].astype(F32)
        rolled[...] = jnp.where(core == 0, both, pltpu.roll(both, 64, 1))
        for b in range(RING):
            rows = [jnp.broadcast_to(rolled[pl.ds(place(a, b), 1), :], (8, 128)) for a in range(RING)]
            for h in range(H):
                line = jnp.zeros((8, 128), F32)
                for a in range(RING):
                    for s in range(2):
                        group = s * RING + a
                        shift = (group * R - h * 2 * R - s * R) % 128
                        line = jnp.where(lanes_of(group), pltpu.roll(rows[a], shift, 1), line)
                out[h * RING + b] = line[0:1].astype(out.dtype)

    first_row = dp * (2 * ROWS * NZ) + z * (2 * ROWS)

    def stats_blocks(k_one, k_two):
        token_ids = jnp.concatenate([ids_row[k_one], ids_row[k_two]], axis=1) - first_row

        def logits_step(v, peak):
            rows = pl.ds(pl.multiple_of(v * VC, VC), VC)
            tokens = jnp.concatenate([hall[k_one].reshape(BLK, D), hall[k_two].reshape(BLK, D)], axis=0)
            part = lax.dot_general(wall[rows, :], tokens, (((1,), (1,)), ((), ())), preferred_element_type=F32)
            logits[k_one, rows, :] = part[:, :BLK]
            logits[k_two, rows, :] = part[:, BLK:]
            return jnp.maximum(peak, jnp.max(part.reshape(VC // 8, 8, 2 * BLK), axis=0))

        peak = lax.fori_loop(0, V // VC, logits_step, jnp.full((8, 2 * BLK), -3e38, F32))
        peak = jnp.max(peak, axis=0, keepdims=True)
        step_rows = 256

        def sums_step(v, sums):
            start_row = pl.multiple_of(v * step_rows, step_rows)
            rows = pl.ds(start_row, step_rows)
            part = jnp.concatenate([logits[k_one, rows, :], logits[k_two, rows, :]], axis=1)
            expon = jnp.exp(part - peak)
            row = lax.broadcasted_iota(jnp.int32, part.shape, 0)
            picked = jnp.where(row == token_ids - start_row, part, 0.0)
            return tuple(s + jnp.sum(p.reshape(step_rows // 8, 8, 2 * BLK), axis=0)
                         for s, p in zip(sums, (expon, expon * part, picked)))

        zero = jnp.zeros((8, 2 * BLK), F32)
        sums = lax.fori_loop(0, V // step_rows, sums_step, (zero, zero, zero))
        sums = tuple(jnp.sum(s, axis=0, keepdims=True) for s in sums)
        for q, row in enumerate((peak,) + sums):
            st[k_one, pl.ds(q, 1), :] = row[:, :BLK]
            st[k_two, pl.ds(q, 1), :] = row[:, BLK:]

    def stats_merge(ref, slots, sent):
        arrive(*sent)
        parts = [ref[...]] + [slots[i] for i in range(len(sent))]
        peak = parts[0][:, 0:1, :]
        for p in parts[1:]:
            peak = jnp.maximum(peak, p[:, 0:1, :])
        total, weighted, target = 0.0, 0.0, 0.0
        for p in parts:
            scale = jnp.exp(p[:, 0:1, :] - peak)
            total += scale * p[:, 1:2, :]
            weighted += scale * p[:, 2:3, :]
            target += p[:, 3:4, :]
        return peak, total, weighted, target

    class Stats:
        def __init__(self, h):
            blocks = pl.ds(h * RING, RING)
            self.steps = [(st.at[blocks], sx.at[h], fin.at[0, blocks], a_dev),
                          (fin.at[0, blocks], sy.at[h], fin.at[1, blocks], b_dev),
                          (fin.at[1, blocks], sz.at[h], fin.at[2, blocks], z_dev)]
            self.sent = [[remote(ref, slots.at[i], d) for i, d in enumerate(devices)]
                         for ref, slots, _, devices in self.steps]

        def begin(self):
            start(*self.sent[0])

        def step(self, i):
            ref, slots, out, _ = self.steps[i]
            rows = stats_merge(ref, slots, self.sent[i])
            if i == 2:
                peak, total, weighted, target = rows
                rows = (peak + jnp.log(total), weighted / total, target)
            for q, row in enumerate(rows):
                out[:, pl.ds(q, 1), :] = row
            if i < 2:
                start(*self.sent[i + 1])

    s0, s1 = Stats(0), Stats(1)

    order = (b_2, b_m, b_p, pb)

    def grad_chunk(h):
        ks = [h * RING + b for b in order]
        token_ids = jnp.concatenate([ids_row[k] for k in ks], axis=1) - first_row
        advantage = jnp.concatenate([adv_row[k] for k in ks], axis=1)
        log_total = jnp.concatenate([fin[2, k, 0:1, :] for k in ks], axis=1)
        mean = jnp.concatenate([fin[2, k, 1:2, :] for k in ks], axis=1)
        step_rows = 128

        def grad_step(v, carry):
            start_row = pl.multiple_of(v * step_rows, step_rows)
            rows = pl.ds(start_row, step_rows)
            part = jnp.concatenate([logits[k, rows, :] for k in ks], axis=1)
            prob = jnp.exp(part - log_total)
            row = lax.broadcasted_iota(jnp.int32, part.shape, 0)
            onehot = jnp.where(row == token_ids - start_row, 1.0, 0.0)
            low = (advantage * (onehot - prob) - ENTROPY_COEF * prob * (part - mean)).astype(BF16)
            for j, k in enumerate(ks):
                tile = low[:, j * BLK:(j + 1) * BLK]
                grad[k, rows, :] = tile
                grad_t[j * BLK:(j + 1) * BLK, rows] = tile.T
            return carry

        lax.fori_loop(0, V // step_rows, grad_step, 0)

    def product_chunk(h):
        def product_step(n, carry):
            cols = pl.ds(pl.multiple_of(n * NC, NC), NC)
            part = jnp.dot(grad_t[...], wall[:, cols], preferred_element_type=F32)
            two_0, two_1, m_0, m_1, p_0, p_1, own_0, own_1 = (part[i * HALF:(i + 1) * HALF] for i in range(8))
            x1[h, 0, :, cols] = two_0.astype(BF16)
            x1[h, 1, :, cols] = two_1.astype(BF16)
            pm[h, 0, :, cols] = m_0
            x1[h, 2, :, cols] = m_1.astype(BF16)
            x1[h, 3, :, cols] = p_0.astype(BF16)
            pm[h, 1, :, cols] = p_1
            pm[h, 2, :, cols] = own_0
            pm[h, 3, :, cols] = own_1
            return carry

        lax.fori_loop(0, D // NC, product_step, 0)

    def chunked(rows, body):
        def step(n, carry):
            body(pl.ds(pl.multiple_of(n * 16, 16), 16))
            return carry

        lax.fori_loop(0, rows // 16, step, 0)

    def slot(a):
        return pl.ds(pl.multiple_of(a * R, R), R)

    class Reduce:
        def __init__(self, h):
            self.h = h
            self.b = [remote(x1.at[h, i], y1.at[h, i], d) for i, d in enumerate((bm, bp, bm, bp, bm, bp))]
            self.a = [remote(x2.at[h, i], y2.at[h, i], d) for i, d in enumerate(a_dev)]
            self.z = [remote(zs.at[h, z, 1 - core], zr.at[h, core, 0], sibling, z_sem.at[h, 0, core])]
            self.z += [remote(zs.at[h, lax.rem(z + k, NZ), f], zr.at[h, core, k], z_both[k - 1][f], z_sem.at[h, k, core])
                       for k in range(1, NZ) for f in range(2)]
            places = [(1 - core, 0)] + [(c, k) for k in range(1, NZ) for c in range(2)]
            self.z_in = [pltpu.make_async_remote_copy(
                src_ref=zr.at[h, c, k], dst_ref=zr.at[h, c, k], send_sem=send_sem.at[0], recv_sem=z_sem.at[h, k, c],
                device_id=sibling, device_id_type=MESH) for c, k in places]

        def begin(self):
            start(*self.b[:4])

        def relay_b(self):
            h = self.h
            for i in range(2):
                arrive(self.b[i])

                def relay(rows):
                    x1[h, 4 + i, rows, :] = (pm[h, i, rows, :] + y1[h, i, rows, :].astype(F32)).astype(BF16)

                chunked(HALF, relay)
                start(self.b[4 + i])

        def end_b(self):
            h = self.h
            arrive(*self.b[2:])
            for s, (one, two) in enumerate(((3, 4), (2, 5))):

                def total(rows):
                    r1[h, s, rows, :] = (pm[h, 2 + s, rows, :] + y1[h, one, rows, :].astype(F32)
                                         + y1[h, two, rows, :].astype(F32))

                chunked(HALF, total)
            for i, a in enumerate((a_p, a_2, a_m)):
                for s in range(2):
                    x2[h, i, s] = r1[h, s, slot(a), :].astype(BF16)
            start(self.a[1], self.a[0], self.a[2])

        def end_a(self):
            h = self.h
            arrive(*self.a)
            for s in range(2):
                for f in range(2 * NZ):
                    cols = slice(f * 128, f * 128 + 128)
                    zs[h, f // 2, f % 2, s] = r1[h, s, slot(pa), cols] + sum(
                        y2[h, i, s, :, cols].astype(F32) for i in range(RING - 1))
            zr[h, core, 0] = zs[h, z, core]
            start(*self.z)

        def end_z(self):
            h = self.h
            arrive(*self.z_in)
            for c in range(2):
                total = zr[h, c, 0]
                for k in range(1, NZ):
                    total += zr[h, c, k]
                gh_out[c, h] = total

    d0, d1 = Reduce(0), Reduce(1)

    weight_copies = [remote(gw_send.at[n], gw_recv.at[n], sibling) for n in range(D // NC)]

    def weight_part(side, n):
        rows = pl.ds(pl.multiple_of(side * ROWS, ROWS), ROWS)
        cols = pl.ds(pl.multiple_of(n * NC, NC), NC)
        lhs = jnp.concatenate([grad[k, rows, :] for k in range(NB)], axis=1)
        rhs = hall[:, :, :, :, cols].reshape(NB * BLK, NC)
        return jnp.dot(lhs, rhs, preferred_element_type=F32), cols

    def weight_other(n):
        gw_send[n] = weight_part(1 - core, n)[0]

    def weight_own(n):
        part, cols = weight_part(core, n)
        gw_out[:, cols] = part + gw_recv[n]

    stat_copy = remote(stat_swap.at[0], stat_swap.at[1], sibling)

    def own_stats():
        for q in range(2):
            line = jnp.zeros((8, 128), F32)
            for h in range(H):
                k = h * RING + pb
                log_total, mean, target = (fin[2, k, pl.ds(i, 1), :] for i in range(3))
                row = jnp.broadcast_to(target - log_total if q == 0 else log_total - mean, (8, 128))
                for s in range(2):
                    group = (h * 2 + s) + core * 4
                    shift = lax.rem(group * R + 256 - (s * RING + pa) * R, 128)
                    line = jnp.where(lanes_of(group), pltpu.roll(row, shift, 1), line)
            stat_swap[0, q] = line
        start(stat_copy)

    def own_stats_store():
        arrive(stat_copy)
        mine = lax.div(lane, 64) == core
        for q, out in enumerate((lp_out, en_out)):
            out[...] = jnp.where(mine, stat_swap[0, q], stat_swap[1, q])[0:1]

    def staged(count, before, body):
        def step(i, carry):
            for j, action in before.items():
                pl.when(i == j)(action)
            body(i)
            return carry

        lax.fori_loop(0, count, step, 0)

    for c in small_in:
        c.wait()
    reorder(ids_in, ids_row)
    reorder(adv_in, adv_row)
    pl.semaphore_wait(barrier, len(peers))
    start(*g0.near, *g0.spread["own"], *g1.near)
    for c in [w_in] + own_in:
        c.wait()
    start(w_swap)
    g0.ring()
    g0.spread_on("m", "p")
    g0.forward("own")
    g0.ring_far()
    g1.spread_on("own")
    g1.ring()
    g0.forward("m", "p", "2")
    g1.spread_on("m", "p")
    g1.forward("own")
    arrive(w_swap)

    def unit(i):
        half = lax.rem(i, 2)
        k = lax.div(i, 2) * RING
        stats_blocks(k + lax.rem(pb + half, RING), k + lax.rem(pb + 3 - half, RING))

    def before_1():
        g1.ring_far()
        g0.last()

    def before_2():
        s0.begin()
        g1.forward("m", "p")
        s0.step(0)
        g1.forward("2")

    def before_3():
        s0.step(1)
        g1.last()

    staged(4, {1: before_1, 2: before_2, 3: before_3}, unit)
    s1.begin()
    s0.step(2)

    def chunk_step(h):
        grad_chunk(h)

        @pl.when(h == 0)
        def _():
            s1.step(1)

        @pl.when(h == 1)
        def _():
            d0.relay_b()

        product_chunk(h)

    def before_chunk_1():
        d0.begin()
        s1.step(2)

    staged(H, {0: lambda: s1.step(0), 1: before_chunk_1}, chunk_step)
    d1.begin()
    own_stats()
    d0.end_b()

    def send_weight(n, *then):
        def action():
            start(weight_copies[n])
            for step in then:
                step()

        return action

    def take_weight(n, *then):
        def action():
            arrive(weight_copies[n])
            for step in then:
                step()

        return action

    staged(4, {1: send_weight(0), 2: send_weight(1, d1.relay_b), 3: send_weight(2)}, weight_other)
    start(weight_copies[3])
    d0.end_a()
    staged(4, {0: take_weight(0), 1: take_weight(1, d1.end_b), 2: take_weight(2, d0.end_z),
               3: take_weight(3, d1.end_a)}, weight_own)
    own_stats_store()
    d1.end_z()
    for copy in copies:
        copy.wait_send()


def call(hid, w, ids, adv):
    vmem = pl.BlockSpec(memory_space=pltpu.VMEM)
    anywhere = pl.BlockSpec(memory_space=pl.ANY)
    scratch = [
        pltpu.VMEM((NB, 2, RING, R, D), BF16),
        pltpu.VMEM((V, D), BF16),
        pltpu.VMEM((NB, V, BLK), F32),
        pltpu.VMEM((NB, V, BLK), BF16),
        pltpu.VMEM((RING * BLK, V), BF16),
        pltpu.VMEM((H, 4, HALF, D), F32),
        pltpu.VMEM((H, 6, HALF, D), BF16),
        pltpu.VMEM((H, 6, HALF, D), BF16),
        pltpu.VMEM((H, 2, HALF, D), F32),
        pltpu.VMEM((H, RING - 1, 2, R, D), BF16),
        pltpu.VMEM((H, RING - 1, 2, R, D), BF16),
        pltpu.VMEM((H, NZ, 2, 2, R, 128), F32),
        pltpu.VMEM((H, 2, NZ, 2, R, 128), F32),
        pltpu.VMEM((NB, 4, BLK), F32),
        pltpu.VMEM((H, RING - 1, RING, 4, BLK), F32),
        pltpu.VMEM((H, RING - 1, RING, 4, BLK), F32),
        pltpu.VMEM((H, NZ - 1, RING, 4, BLK), F32),
        pltpu.VMEM((3, NB, 4, BLK), F32),
        pltpu.VMEM((16, 128), jnp.int32),
        pltpu.VMEM((16, 128), F32),
        pltpu.VMEM((16, 128), F32),
        pltpu.VMEM((NB, 1, BLK), jnp.int32),
        pltpu.VMEM((NB, 1, BLK), F32),
        pltpu.VMEM((2, 2, 8, 128), F32),
        pltpu.VMEM((D // NC, ROWS, NC), F32),
        pltpu.VMEM((D // NC, ROWS, NC), F32),
        pltpu.SemaphoreType.DMA((NSEM,)),
        pltpu.SemaphoreType.DMA((NSEM,)),
        pltpu.SemaphoreType.DMA((H, NZ, 2)),
        pltpu.SemaphoreType.DMA((3 + H,)),
    ]
    return pl.pallas_call(
        kernel,
        out_shape=(
            pltpu.VMEM((ROWS, D), F32),
            pltpu.VMEM((2, H, 2, R, 128), F32),
            pltpu.VMEM((1, SHARD), F32),
            pltpu.VMEM((1, SHARD), F32),
        ),
        in_specs=[anywhere] * 4,
        out_specs=(vmem, vmem, vmem, vmem),
        scratch_shapes=scratch,
        compiler_params=pltpu.CompilerParams(
            collective_id=0, has_side_effects=True, vmem_limit_bytes=50 * 2**20),
    )(hid, w, ids, adv)


def shards(hidden, head_weight, sampled_ids, advantage):
    hid = hidden.reshape(2, H, 2, R, D)
    grad_weight, grad_hidden, log_prob, entropy = call(
        hid, head_weight, sampled_ids.reshape(16, 128), advantage.reshape(16, 128))
    return (log_prob.reshape(SHARD), entropy.reshape(SHARD), grad_hidden.reshape(SHARD, 128), grad_weight)


def solution(mesh):
    placed = (P("dp", None), P(("dp", "vocab"), None), P(), P())
    return jax.shard_map(
        shards,
        mesh=mesh,
        in_specs=placed,
        out_specs=(P("dp"), P("dp"), P("dp", "vocab"), P(("dp", "vocab"), None)),
        check_vma=False,
    )
```

```python
import jax
import jax.numpy as jnp
from jax import lax
from jax.experimental import pallas as pl
from jax.experimental.pallas import tpu as pltpu
from jax.sharding import PartitionSpec as P

ENTROPY_COEF = 0.25
MESH = pl.DeviceIdType.MESH
F32, BF16 = jnp.float32, jnp.bfloat16

D = 2048
V = 1024
ROWS = 512
SHARD = 128
RING = 4
NZ = 8
H = 2
R = 16
BLK = 2 * RING * R
HALF = RING * R
NB = RING * H
VC = 512
NC = 512
DC = D // 2
NSEM = 144


def kernel(hid, w, ids, adv, gw_out, gh_out, lp_out, en_out,
           hall, wall, logits, grad, grad_t, pm, x1, y1, r1, x2, y2, zs, zr, st, sx, sy, sz, fin,
           ids_in, adv_in, rolled, ids_row, adv_row, stat_swap, gw_send, gw_recv, send_sem, recv_sem, z_sem, local_sem):
    dp, vo = lax.axis_index("dp"), lax.axis_index("vocab")
    x, y = lax.div(dp, RING), lax.rem(dp, RING)
    z, core = lax.div(vo, 2), lax.rem(vo, 2)
    pa, pb = x + core * (y - x), y + core * (x - y)
    a_p, a_2, a_m = (lax.rem(pa + k, RING) for k in (1, 2, 3))
    b_p, b_2, b_m = (lax.rem(pb + k, RING) for k in (1, 2, 3))

    def place(a, b):
        first, second = a * RING + b, b * RING + a
        return first + core * (second - first)

    def dev(a, b):
        return {"dp": place(a, b), "vocab": vo}

    def zdev(k):
        return {"dp": dp, "vocab": lax.rem(z + k, NZ) * 2 + core}

    sibling = {"dp": dp, "vocab": vo + 1 - 2 * core}

    copies = []

    def remote(src, dst, device, arrival=None):
        i = len(copies)
        copies.append(pltpu.make_async_remote_copy(
            src_ref=src, dst_ref=dst, send_sem=send_sem.at[i], recv_sem=recv_sem.at[i] if arrival is None else arrival,
            device_id=device, device_id_type=MESH))
        return copies[-1]

    def start(*some):
        for copy in some:
            copy.start()

    def arrive(*some):
        for copy in some:
            copy.wait_recv()

    w_rows = pl.ds(pl.multiple_of(core * ROWS, ROWS), ROWS)
    w_in = pltpu.make_async_copy(w, wall.at[w_rows], local_sem.at[0])
    small_in = [pltpu.make_async_copy(ids, ids_in, local_sem.at[1]),
                pltpu.make_async_copy(adv, adv_in, local_sem.at[2])]
    own_in = [pltpu.make_async_copy(hid.at[core, h], hall.at[h * RING + pb, :, pa], local_sem.at[3 + h])
              for h in range(H)]
    for c in [w_in] + small_in + own_in:
        c.start()

    a_dev = [dev(lax.rem(pa + k, RING), pb) for k in (1, 2, 3)]
    b_dev = [dev(pa, lax.rem(pb + k, RING)) for k in (1, 2, 3)]
    z_dev = [zdev(k) for k in range(1, NZ)]
    ap, _, am = a_dev
    bp, _, bm = b_dev
    barrier = pltpu.get_barrier_semaphore()
    z_both = [[dict(dp=dp, vocab=lax.rem(z + k, NZ) * 2 + f) for f in range(2)] for k in range(1, NZ)]
    peers = a_dev + b_dev + [d for both in z_both for d in both] + [sibling]
    for peer in peers:
        pl.semaphore_signal(barrier, inc=1, device_id=peer, device_id_type=MESH)

    w_swap = remote(wall.at[w_rows], wall.at[w_rows], sibling)

    class Gather:
        def __init__(self, h):
            kp, km, k0 = (h * RING + b for b in (b_p, b_m, pb))
            own, there = hid.at[core, h], hall.at[k0, :, pa]
            self.near = [remote(own, there, d) for d in (ap, am)]
            self.far = [remote(hall.at[k0, 0, a_m], hall.at[k0, 0, a_m], ap),
                        remote(hall.at[k0, 1, a_p], hall.at[k0, 1, a_p], am)]
            self.spread, self.pass_on = {}, {}
            for slot, src in (("own", pa), ("m", a_m), ("p", a_p), ("2", a_2)):
                ref = hall.at[k0, :, src]
                self.spread[slot] = [remote(own if slot == "own" else ref, ref, d) for d in (bp, bm)]
                one, two = hall.at[km, 0, src], hall.at[kp, 1, src]
                self.pass_on[slot] = [remote(one, one, bp), remote(two, two, bm)]

        def ring(self):
            for near, far in zip(self.near, self.far):
                arrive(near)
                start(far)

        def spread_on(self, *slots):
            for slot in slots:
                start(*self.spread[slot])

        def ring_far(self):
            arrive(*self.far)
            start(*self.spread["2"])

        def forward(self, *slots):
            for slot in slots:
                for came, on in zip(self.spread[slot], self.pass_on[slot]):
                    arrive(came)
                    start(on)

        def last(self):
            for on in self.pass_on.values():
                arrive(*on)

    g0, g1 = Gather(0), Gather(1)

    lane = lax.broadcasted_iota(jnp.int32, (8, 128), 1)

    def lanes_of(group):
        return lax.div(lane, R) == group

    def reorder(source, out):
        both = source[...].astype(F32)
        rolled[...] = jnp.where(core == 0, both, pltpu.roll(both, 64, 1))
        for b in range(RING):
            rows = [jnp.broadcast_to(rolled[pl.ds(place(a, b), 1), :], (8, 128)) for a in range(RING)]
            for h in range(H):
                line = jnp.zeros((8, 128), F32)
                for a in range(RING):
                    for s in range(2):
                        group = s * RING + a
                        shift = (group * R - h * 2 * R - s * R) % 128
                        line = jnp.where(lanes_of(group), pltpu.roll(rows[a], shift, 1), line)
                out[h * RING + b] = line[0:1].astype(out.dtype)

    first_row = dp * (2 * ROWS * NZ) + z * (2 * ROWS)

    def stats_blocks(k_one, k_two):
        token_ids = jnp.concatenate([ids_row[k_one], ids_row[k_two]], axis=1) - first_row

        def logits_step(v, peak):
            rows = pl.ds(pl.multiple_of(v * VC, VC), VC)
            tokens = jnp.concatenate([hall[k_one].reshape(BLK, D), hall[k_two].reshape(BLK, D)], axis=0)
            part = lax.dot_general(wall[rows, :], tokens, (((1,), (1,)), ((), ())), preferred_element_type=F32)
            logits[k_one, rows, :] = part[:, :BLK]
            logits[k_two, rows, :] = part[:, BLK:]
            return jnp.maximum(peak, jnp.max(part.reshape(VC // 8, 8, 2 * BLK), axis=0))

        peak = lax.fori_loop(0, V // VC, logits_step, jnp.full((8, 2 * BLK), -3e38, F32))
        peak = jnp.max(peak, axis=0, keepdims=True)
        step_rows = 256

        def sums_step(v, sums):
            start_row = pl.multiple_of(v * step_rows, step_rows)
            rows = pl.ds(start_row, step_rows)
            part = jnp.concatenate([logits[k_one, rows, :], logits[k_two, rows, :]], axis=1)
            expon = jnp.exp(part - peak)
            row = lax.broadcasted_iota(jnp.int32, part.shape, 0)
            picked = jnp.where(row == token_ids - start_row, part, 0.0)
            return tuple(s + jnp.sum(p.reshape(step_rows // 8, 8, 2 * BLK), axis=0)
                         for s, p in zip(sums, (expon, expon * part, picked)))

        zero = jnp.zeros((8, 2 * BLK), F32)
        sums = lax.fori_loop(0, V // step_rows, sums_step, (zero, zero, zero))
        sums = tuple(jnp.sum(s, axis=0, keepdims=True) for s in sums)
        for q, row in enumerate((peak,) + sums):
            st[k_one, pl.ds(q, 1), :] = row[:, :BLK]
            st[k_two, pl.ds(q, 1), :] = row[:, BLK:]

    def stats_merge(ref, slots, sent):
        arrive(*sent)
        parts = [ref[...]] + [slots[i] for i in range(len(sent))]
        peak = parts[0][:, 0:1, :]
        for p in parts[1:]:
            peak = jnp.maximum(peak, p[:, 0:1, :])
        total, weighted, target = 0.0, 0.0, 0.0
        for p in parts:
            scale = jnp.exp(p[:, 0:1, :] - peak)
            total += scale * p[:, 1:2, :]
            weighted += scale * p[:, 2:3, :]
            target += p[:, 3:4, :]
        return peak, total, weighted, target

    class Stats:
        def __init__(self, h):
            blocks = pl.ds(h * RING, RING)
            self.steps = [(st.at[blocks], sz.at[h], fin.at[0, blocks], z_dev),
                          (fin.at[0, blocks], sx.at[h], fin.at[1, blocks], a_dev),
                          (fin.at[1, blocks], sy.at[h], fin.at[2, blocks], b_dev)]
            self.sent = [[remote(ref, slots.at[i], d) for i, d in enumerate(devices)]
                         for ref, slots, _, devices in self.steps]

        def begin(self):
            start(*self.sent[0])

        def step(self, i):
            ref, slots, out, _ = self.steps[i]
            rows = stats_merge(ref, slots, self.sent[i])
            if i == 2:
                peak, total, weighted, target = rows
                rows = (peak + jnp.log(total), weighted / total, target)
            for q, row in enumerate(rows):
                out[:, pl.ds(q, 1), :] = row
            if i < 2:
                start(*self.sent[i + 1])

    s0, s1 = Stats(0), Stats(1)

    order = (b_2, b_m, b_p, pb)

    def grad_chunk(h):
        ks = [h * RING + b for b in order]
        token_ids = jnp.concatenate([ids_row[k] for k in ks], axis=1) - first_row
        advantage = jnp.concatenate([adv_row[k] for k in ks], axis=1)
        log_total = jnp.concatenate([fin[2, k, 0:1, :] for k in ks], axis=1)
        mean = jnp.concatenate([fin[2, k, 1:2, :] for k in ks], axis=1)
        step_rows = 128

        def grad_step(v, carry):
            start_row = pl.multiple_of(v * step_rows, step_rows)
            rows = pl.ds(start_row, step_rows)
            part = jnp.concatenate([logits[k, rows, :] for k in ks], axis=1)
            prob = jnp.exp(part - log_total)
            row = lax.broadcasted_iota(jnp.int32, part.shape, 0)
            onehot = jnp.where(row == token_ids - start_row, 1.0, 0.0)
            low = (advantage * (onehot - prob) - ENTROPY_COEF * prob * (part - mean)).astype(BF16)
            for j, k in enumerate(ks):
                tile = low[:, j * BLK:(j + 1) * BLK]
                grad[k, rows, :] = tile
                grad_t[j * BLK:(j + 1) * BLK, rows] = tile.T
            return carry

        lax.fori_loop(0, V // step_rows, grad_step, 0)

    def product_half(h, c):
        def product_step(n, carry):
            start_col = pl.multiple_of(n * NC, NC)
            cols = pl.ds(start_col, NC)
            part = jnp.dot(grad_t[...], wall[:, pl.ds(pl.multiple_of(c * DC + start_col, NC), NC)],
                           preferred_element_type=F32)
            two_0, two_1, m_0, m_1, p_0, p_1, own_0, own_1 = (part[i * HALF:(i + 1) * HALF] for i in range(8))
            x1[h, c, 0, :, cols] = two_0.astype(BF16)
            x1[h, c, 1, :, cols] = two_1.astype(BF16)
            pm[h, c, 0, :, cols] = m_0
            x1[h, c, 2, :, cols] = m_1.astype(BF16)
            x1[h, c, 3, :, cols] = p_0.astype(BF16)
            pm[h, c, 1, :, cols] = p_1
            pm[h, c, 2, :, cols] = own_0
            pm[h, c, 3, :, cols] = own_1
            return carry

        lax.fori_loop(0, DC // NC, product_step, 0)

    def chunked(rows, body):
        def step(n, carry):
            body(pl.ds(pl.multiple_of(n * 16, 16), 16))
            return carry

        lax.fori_loop(0, rows // 16, step, 0)

    def slot(a):
        return pl.ds(pl.multiple_of(a * R, R), R)

    class Reduce:
        def __init__(self, h, c):
            self.at = h, c
            self.b = [remote(x1.at[h, c, i], y1.at[h, c, i], d) for i, d in enumerate((bm, bp, bm, bp, bm, bp))]
            self.a = [remote(x2.at[h, c, i], y2.at[h, c, i], d) for i, d in enumerate(a_dev)]

        def begin(self):
            start(*self.b[:4])

        def relay_b(self):
            h, c = self.at
            for i in range(2):
                arrive(self.b[i])

                def relay(rows):
                    x1[h, c, 4 + i, rows, :] = (
                        pm[h, c, i, rows, :] + y1[h, c, i, rows, :].astype(F32)).astype(BF16)

                chunked(HALF, relay)
                start(self.b[4 + i])

        def end_b(self):
            h, c = self.at
            arrive(*self.b[2:])
            for s, (one, two) in enumerate(((3, 4), (2, 5))):

                def total(rows):
                    r1[h, c, s, rows, :] = (pm[h, c, 2 + s, rows, :] + y1[h, c, one, rows, :].astype(F32)
                                            + y1[h, c, two, rows, :].astype(F32))

                chunked(HALF, total)
            for i in (1, 0, 2):
                for s in range(2):
                    x2[h, c, i, s] = r1[h, c, s, slot((a_p, a_2, a_m)[i]), :].astype(BF16)
                start(self.a[i])

        def end_a(self):
            h, c = self.at
            arrive(*self.a)
            for s in range(2):
                for f in range(DC // 128):
                    cols = slice(f * 128, f * 128 + 128)
                    zs[h, c * (NZ // 2) + f // 2, f % 2, s] = r1[h, c, s, slot(pa), cols] + sum(
                        y2[h, c, i, s, :, cols].astype(F32) for i in range(RING - 1))

    class Reduce_z:
        def __init__(self, h):
            self.h = h
            self.sibling = remote(zs.at[h, z, 1 - core], zr.at[h, core, 0], sibling, z_sem.at[h, 0, core])
            self.others = [[remote(zs.at[h, lax.rem(z + k, NZ), f], zr.at[h, core, k], z_both[k - 1][f],
                                   z_sem.at[h, k, core]) for f in range(2)] for k in range(1, NZ)]
            places = [(1 - core, 0)] + [(c, k) for k in range(1, NZ) for c in range(2)]
            self.arrivals = [pltpu.make_async_remote_copy(
                src_ref=zr.at[h, c, k], dst_ref=zr.at[h, c, k], send_sem=send_sem.at[0], recv_sem=z_sem.at[h, k, c],
                device_id=sibling, device_id_type=MESH) for c, k in places]

        def send(self, c):
            @pl.when(lax.div(z, NZ // 2) == c)
            def _():
                zr[self.h, core, 0] = zs[self.h, z, core]
                start(self.sibling)

            for k in range(1, NZ):

                @pl.when(lax.div(lax.rem(z + k, NZ), NZ // 2) == c)
                def _():
                    start(*self.others[k - 1])

        def end(self):
            h = self.h
            arrive(*self.arrivals)
            for c in range(2):
                total = zr[h, c, 0]
                for k in range(1, NZ):
                    total += zr[h, c, k]
                gh_out[c, h] = total

    d00, d01, d10, d11 = (Reduce(h, c) for h in range(H) for c in range(2))
    z0, z1 = Reduce_z(0), Reduce_z(1)

    weight_copies = [remote(gw_send.at[n], gw_recv.at[n], sibling) for n in range(D // NC)]

    def weight_part(side, n):
        rows = pl.ds(pl.multiple_of(side * ROWS, ROWS), ROWS)
        cols = pl.ds(pl.multiple_of(n * NC, NC), NC)
        lhs = jnp.concatenate([grad[k, rows, :] for k in range(NB)], axis=1)
        rhs = hall[:, :, :, :, cols].reshape(NB * BLK, NC)
        return jnp.dot(lhs, rhs, preferred_element_type=F32), cols

    def weight_other(n):
        gw_send[n] = weight_part(1 - core, n)[0]

    def weight_own(n):
        part, cols = weight_part(core, n)
        gw_out[:, cols] = part + gw_recv[n]

    stat_copy = remote(stat_swap.at[0], stat_swap.at[1], sibling)

    def own_stats():
        for q in range(2):
            line = jnp.zeros((8, 128), F32)
            for h in range(H):
                k = h * RING + pb
                log_total, mean, target = (fin[2, k, pl.ds(i, 1), :] for i in range(3))
                row = jnp.broadcast_to(target - log_total if q == 0 else log_total - mean, (8, 128))
                for s in range(2):
                    group = (h * 2 + s) + core * 4
                    shift = lax.rem(group * R + 256 - (s * RING + pa) * R, 128)
                    line = jnp.where(lanes_of(group), pltpu.roll(row, shift, 1), line)
            stat_swap[0, q] = line
        start(stat_copy)

    def own_stats_store():
        arrive(stat_copy)
        mine = lax.div(lane, 64) == core
        for q, out in enumerate((lp_out, en_out)):
            out[...] = jnp.where(mine, stat_swap[0, q], stat_swap[1, q])[0:1]

    def staged(count, before, body):
        def step(i, carry):
            for j, action in before.items():
                pl.when(i == j)(action)
            body(i)
            return carry

        lax.fori_loop(0, count, step, 0)

    for c in small_in:
        c.wait()
    reorder(ids_in, ids_row)
    reorder(adv_in, adv_row)
    pl.semaphore_wait(barrier, len(peers))
    start(*g0.near, *g0.spread["own"], *g1.near)
    for c in [w_in] + own_in:
        c.wait()
    start(w_swap)
    g0.ring()
    g0.spread_on("m", "p")
    g0.forward("own")
    g0.ring_far()
    g0.forward("m", "p", "2")
    g1.spread_on("own")
    g1.ring()
    g1.spread_on("m", "p")
    arrive(w_swap)

    def unit(i):
        half = lax.rem(i, 2)
        k = lax.div(i, 2) * RING
        stats_blocks(k + lax.rem(pb + half, RING), k + lax.rem(pb + 3 - half, RING))

    def before_1():
        g1.forward("own")
        g0.last()

    def before_2():
        s0.begin()
        g1.ring_far()
        g1.forward("m", "p")
        s0.step(0)
        g1.forward("2")

    def before_3():
        s0.step(1)
        g1.last()

    staged(4, {1: before_1, 2: before_2, 3: before_3}, unit)
    s1.begin()
    s0.step(2)

    def half_step(i):
        h, c = lax.div(i, 2), lax.rem(i, 2)

        @pl.when(c == 0)
        def _():
            grad_chunk(h)

        pl.when(i == 2)(d01.relay_b)
        product_half(h, c)

    def before_half_1():
        d00.begin()
        s1.step(0)

    def before_half_2():
        d01.begin()
        s1.step(1)
        d00.relay_b()
        s1.step(2)

    staged(4, {1: before_half_1, 2: before_half_2, 3: d10.begin}, half_step)
    d11.begin()
    own_stats()
    d00.end_b()

    def weight_sent(n, *then):
        def action():
            start(weight_copies[n])
            for step in then:
                step()

        return action

    def weight_came(n, *then):
        def action():
            arrive(weight_copies[n])
            for step in then:
                step()

        return action

    staged(4, {1: weight_sent(0, d01.end_b), 2: weight_sent(1, d10.relay_b), 3: weight_sent(2)}, weight_other)
    start(weight_copies[3])
    d11.relay_b()

    def before_own_1():
        d00.end_a()
        z0.send(0)
        d10.end_b()

    def before_own_2():
        d01.end_a()
        z0.send(1)

    staged(4, {0: weight_came(0), 1: weight_came(1, before_own_1), 2: weight_came(2, before_own_2),
               3: weight_came(3, d11.end_b)}, weight_own)
    d10.end_a()
    z1.send(0)
    z0.end()
    own_stats_store()
    d11.end_a()
    z1.send(1)
    z1.end()
    for copy in copies:
        copy.wait_send()


def call(hid, w, ids, adv):
    vmem = pl.BlockSpec(memory_space=pltpu.VMEM)
    anywhere = pl.BlockSpec(memory_space=pl.ANY)
    scratch = [
        pltpu.VMEM((NB, 2, RING, R, D), BF16),
        pltpu.VMEM((V, D), BF16),
        pltpu.VMEM((NB, V, BLK), F32),
        pltpu.VMEM((NB, V, BLK), BF16),
        pltpu.VMEM((RING * BLK, V), BF16),
        pltpu.VMEM((H, 2, 4, HALF, DC), F32),
        pltpu.VMEM((H, 2, 6, HALF, DC), BF16),
        pltpu.VMEM((H, 2, 6, HALF, DC), BF16),
        pltpu.VMEM((H, 2, 2, HALF, DC), F32),
        pltpu.VMEM((H, 2, RING - 1, 2, R, DC), BF16),
        pltpu.VMEM((H, 2, RING - 1, 2, R, DC), BF16),
        pltpu.VMEM((H, NZ, 2, 2, R, 128), F32),
        pltpu.VMEM((H, 2, NZ, 2, R, 128), F32),
        pltpu.VMEM((NB, 4, BLK), F32),
        pltpu.VMEM((H, RING - 1, RING, 4, BLK), F32),
        pltpu.VMEM((H, RING - 1, RING, 4, BLK), F32),
        pltpu.VMEM((H, NZ - 1, RING, 4, BLK), F32),
        pltpu.VMEM((3, NB, 4, BLK), F32),
        pltpu.VMEM((16, 128), jnp.int32),
        pltpu.VMEM((16, 128), F32),
        pltpu.VMEM((16, 128), F32),
        pltpu.VMEM((NB, 1, BLK), jnp.int32),
        pltpu.VMEM((NB, 1, BLK), F32),
        pltpu.VMEM((2, 2, 8, 128), F32),
        pltpu.VMEM((D // NC, ROWS, NC), F32),
        pltpu.VMEM((D // NC, ROWS, NC), F32),
        pltpu.SemaphoreType.DMA((NSEM,)),
        pltpu.SemaphoreType.DMA((NSEM,)),
        pltpu.SemaphoreType.DMA((H, NZ, 2)),
        pltpu.SemaphoreType.DMA((3 + H,)),
    ]
    return pl.pallas_call(
        kernel,
        out_shape=(
            pltpu.VMEM((ROWS, D), F32),
            pltpu.VMEM((2, H, 2, R, 128), F32),
            pltpu.VMEM((1, SHARD), F32),
            pltpu.VMEM((1, SHARD), F32),
        ),
        in_specs=[anywhere] * 4,
        out_specs=(vmem, vmem, vmem, vmem),
        scratch_shapes=scratch,
        compiler_params=pltpu.CompilerParams(
            collective_id=0, has_side_effects=True, vmem_limit_bytes=50 * 2**20),
    )(hid, w, ids, adv)


def store_kernel(*refs):
    count = len(refs) // 2
    moves = [pltpu.make_async_copy(refs[i], refs[count + i], refs[-1].at[i]) for i in range(count)]
    for move in moves:
        move.start()
    for move in moves:
        move.wait()


def store(*arrays):
    return pl.pallas_call(
        store_kernel,
        out_shape=[jax.ShapeDtypeStruct(a.shape, a.dtype) for a in arrays],
        in_specs=[pl.BlockSpec(memory_space=pltpu.VMEM)] * len(arrays),
        out_specs=[pl.BlockSpec(memory_space=pl.ANY)] * len(arrays),
        scratch_shapes=[pltpu.SemaphoreType.DMA((len(arrays),))],
        compiler_params=pltpu.CompilerParams(vmem_limit_bytes=4 * 2**20),
    )(*arrays)


def shards(hidden, head_weight, sampled_ids, advantage):
    hid = hidden.reshape(2, H, 2, R, D)
    grad_weight, grad_hidden, log_prob, entropy = store(*call(
        hid, head_weight, sampled_ids.reshape(16, 128), advantage.reshape(16, 128)))
    return (log_prob.reshape(SHARD), entropy.reshape(SHARD), grad_hidden.reshape(SHARD, 128), grad_weight)


def solution(mesh):
    placed = (P("dp", None), P(("dp", "vocab"), None), P(), P())
    return jax.shard_map(
        shards,
        mesh=mesh,
        in_specs=placed,
        out_specs=(P("dp"), P("dp"), P("dp", "vocab"), P(("dp", "vocab"), None)),
        check_vma=False,
    )
```

```python
import jax
import jax.numpy as jnp
from jax import lax
from jax.experimental import pallas as pl
from jax.experimental.pallas import tpu as pltpu
from jax.sharding import PartitionSpec as P

ENTROPY_COEF = 0.25
MESH = pl.DeviceIdType.MESH
F32, BF16 = jnp.float32, jnp.bfloat16

D = 2048
V = 1024
ROWS = 512
SHARD = 128
RING = 4
NZ = 8
H = 2
R = 16
BLK = 2 * RING * R
HALF = RING * R
NB = RING * H
VC = 256
NC = 512
DC = D // 2
NSEM = 144


def kernel(hid, w, ids, adv, gw_out, gh_out, lp_out, en_out,
           hall, wall, logits, grad, grad_t, pm, x1, y1, r1, x2, y2, zs, zr, st, sx, sy, sz, fin,
           ids_in, adv_in, rolled, ids_row, adv_row, stat_swap, gw_send, gw_recv, send_sem, recv_sem, z_sem, local_sem):
    dp, vo = lax.axis_index("dp"), lax.axis_index("vocab")
    x, y = lax.div(dp, RING), lax.rem(dp, RING)
    z, core = lax.div(vo, 2), lax.rem(vo, 2)
    pa, pb = x + core * (y - x), y + core * (x - y)
    a_p, a_2, a_m = (lax.rem(pa + k, RING) for k in (1, 2, 3))
    b_p, b_2, b_m = (lax.rem(pb + k, RING) for k in (1, 2, 3))

    def place(a, b):
        first, second = a * RING + b, b * RING + a
        return first + core * (second - first)

    def dev(a, b):
        return {"dp": place(a, b), "vocab": vo}

    def zdev(k):
        return {"dp": dp, "vocab": lax.rem(z + k, NZ) * 2 + core}

    sibling = {"dp": dp, "vocab": vo + 1 - 2 * core}

    copies = []

    def remote(src, dst, device, arrival=None):
        i = len(copies)
        copies.append(pltpu.make_async_remote_copy(
            src_ref=src, dst_ref=dst, send_sem=send_sem.at[i], recv_sem=recv_sem.at[i] if arrival is None else arrival,
            device_id=device, device_id_type=MESH))
        return copies[-1]

    def start(*some):
        for copy in some:
            copy.start()

    def arrive(*some):
        for copy in some:
            copy.wait_recv()

    w_rows = pl.ds(pl.multiple_of(core * ROWS, ROWS), ROWS)
    w_in = pltpu.make_async_copy(w, wall.at[w_rows], local_sem.at[0])
    small_in = [pltpu.make_async_copy(ids, ids_in, local_sem.at[1]),
                pltpu.make_async_copy(adv, adv_in, local_sem.at[2])]
    own_in = [pltpu.make_async_copy(hid.at[core, h], hall.at[h * RING + pb, :, pa], local_sem.at[3 + h])
              for h in range(H)]
    for c in [w_in] + small_in + own_in:
        c.start()

    a_dev = [dev(lax.rem(pa + k, RING), pb) for k in (1, 2, 3)]
    b_dev = [dev(pa, lax.rem(pb + k, RING)) for k in (1, 2, 3)]
    z_dev = [zdev(k) for k in range(1, NZ)]
    ap, _, am = a_dev
    bp, _, bm = b_dev
    barrier = pltpu.get_barrier_semaphore()
    z_both = [[dict(dp=dp, vocab=lax.rem(z + k, NZ) * 2 + f) for f in range(2)] for k in range(1, NZ)]
    peers = a_dev + b_dev + [d for both in z_both for d in both] + [sibling]
    for peer in peers:
        pl.semaphore_signal(barrier, inc=1, device_id=peer, device_id_type=MESH)

    w_swap = remote(wall.at[w_rows], wall.at[w_rows], sibling)

    class Gather:
        def __init__(self, h):
            kp, km, k0 = (h * RING + b for b in (b_p, b_m, pb))
            own, there = hid.at[core, h], hall.at[k0, :, pa]
            self.near = [remote(own, there, d) for d in (ap, am)]
            self.far = [remote(hall.at[k0, 0, a_m], hall.at[k0, 0, a_m], ap),
                        remote(hall.at[k0, 1, a_p], hall.at[k0, 1, a_p], am)]
            halves = [hall.at[k0, s] for s in range(2)]
            self.first = [remote(halves[0], halves[0], bp), remote(halves[1], halves[1], bm)]
            self.second = [remote(halves[1], halves[1], bp), remote(halves[0], halves[0], bm)]
            self.on = [remote(hall.at[km, 0], hall.at[km, 0], bp), remote(hall.at[kp, 1], hall.at[kp, 1], bm)]

        def ring(self):
            for near, far in zip(self.near, self.far):
                arrive(near)
                start(far)

        def spread(self):
            arrive(*self.far)
            start(*self.first, *self.second)

        def pass_on(self):
            for first, on in zip(self.first, self.on):
                arrive(first)
                start(on)

    g0, g1 = Gather(0), Gather(1)

    lane = lax.broadcasted_iota(jnp.int32, (8, 128), 1)

    def lanes_of(group):
        return lax.div(lane, R) == group

    def reorder(source, out):
        both = source[...].astype(F32)
        rolled[...] = jnp.where(core == 0, both, pltpu.roll(both, 64, 1))
        for b in range(RING):
            rows = [jnp.broadcast_to(rolled[pl.ds(place(a, b), 1), :], (8, 128)) for a in range(RING)]
            for h in range(H):
                line = jnp.zeros((8, 128), F32)
                for a in range(RING):
                    for s in range(2):
                        group = s * RING + a
                        shift = (group * R - h * 2 * R - s * R) % 128
                        line = jnp.where(lanes_of(group), pltpu.roll(rows[a], shift, 1), line)
                out[h * RING + b] = line[0:1].astype(out.dtype)

    first_row = dp * (2 * ROWS * NZ) + z * (2 * ROWS)

    def stats_blocks(k_one, k_two):
        token_ids = jnp.concatenate([ids_row[k_one], ids_row[k_two]], axis=1) - first_row

        def product(v):
            tokens = jnp.concatenate([hall[k_one].reshape(BLK, D), hall[k_two].reshape(BLK, D)], axis=0)
            part = lax.dot_general(wall[v * VC:(v + 1) * VC, :], tokens, (((1,), (1,)), ((), ())),
                                   preferred_element_type=F32)
            logits[k_one, v * VC:(v + 1) * VC, :] = part[:, :BLK]
            logits[k_two, v * VC:(v + 1) * VC, :] = part[:, BLK:]

        def add_sums(v, peak, sums):
            rows = slice(v * VC, (v + 1) * VC)
            part = jnp.concatenate([logits[k_one, rows, :], logits[k_two, rows, :]], axis=1)
            above = jnp.max(part, axis=0, keepdims=True)
            new_peak = above if peak is None else jnp.maximum(peak, above)
            expon = jnp.exp(part - new_peak)
            row = lax.broadcasted_iota(jnp.int32, part.shape, 0)
            picked = jnp.where(row == token_ids - v * VC, part, 0.0)
            more = [jnp.sum(p, axis=0, keepdims=True) for p in (expon, expon * part, picked)]
            if peak is not None:
                scale = jnp.exp(peak - new_peak)
                more = [m + s * f for m, s, f in zip(more, sums, (scale, scale, 1.0))]
            return new_peak, more

        peak, sums = None, None
        product(0)
        for v in range(1, V // VC):
            product(v)
            peak, sums = add_sums(v - 1, peak, sums)
        peak, sums = add_sums(V // VC - 1, peak, sums)
        for q, row in enumerate([peak] + sums):
            st[k_one, pl.ds(q, 1), :] = row[:, :BLK]
            st[k_two, pl.ds(q, 1), :] = row[:, BLK:]

    def stats_merge(ref, slots, sent):
        arrive(*sent)
        parts = [ref[...]] + [slots[i] for i in range(len(sent))]
        peak = parts[0][:, 0:1, :]
        for p in parts[1:]:
            peak = jnp.maximum(peak, p[:, 0:1, :])
        total, weighted, target = 0.0, 0.0, 0.0
        for p in parts:
            scale = jnp.exp(p[:, 0:1, :] - peak)
            total += scale * p[:, 1:2, :]
            weighted += scale * p[:, 2:3, :]
            target += p[:, 3:4, :]
        return peak, total, weighted, target

    class Stats:
        def __init__(self, h):
            blocks = pl.ds(h * RING, RING)
            self.steps = [(st.at[blocks], sz.at[h], fin.at[0, blocks], z_dev),
                          (fin.at[0, blocks], sx.at[h], fin.at[1, blocks], a_dev),
                          (fin.at[1, blocks], sy.at[h], fin.at[2, blocks], b_dev)]
            self.sent = [[remote(ref, slots.at[i], d) for i, d in enumerate(devices)]
                         for ref, slots, _, devices in self.steps]

        def begin(self):
            start(*self.sent[0])

        def step(self, i):
            ref, slots, out, _ = self.steps[i]
            rows = stats_merge(ref, slots, self.sent[i])
            if i == 2:
                peak, total, weighted, target = rows
                rows = (peak + jnp.log(total), weighted / total, target)
            for q, row in enumerate(rows):
                out[:, pl.ds(q, 1), :] = row
            if i < 2:
                start(*self.sent[i + 1])

    s0, s1 = Stats(0), Stats(1)

    order = (b_2, b_m, b_p, pb)

    def grad_chunk(h):
        ks = [h * RING + b for b in order]
        token_ids = jnp.concatenate([ids_row[k] for k in ks], axis=1) - first_row
        advantage = jnp.concatenate([adv_row[k] for k in ks], axis=1)
        log_total = jnp.concatenate([fin[2, k, 0:1, :] for k in ks], axis=1)
        mean = jnp.concatenate([fin[2, k, 1:2, :] for k in ks], axis=1)
        level = advantage - ENTROPY_COEF * mean
        step_rows = 128

        def grad_step(v, carry):
            start_row = pl.multiple_of(v * step_rows, step_rows)
            rows = pl.ds(start_row, step_rows)
            part = jnp.concatenate([logits[k, rows, :] for k in ks], axis=1)
            prob = jnp.exp(part - log_total)
            row = lax.broadcasted_iota(jnp.int32, part.shape, 0)
            chosen = jnp.where(row == token_ids - start_row, advantage, 0.0)
            low = (chosen - prob * (level + ENTROPY_COEF * part)).astype(BF16)
            for j, k in enumerate(ks):
                tile = low[:, j * BLK:(j + 1) * BLK]
                grad[k, rows, :] = tile
                grad_t[j * BLK:(j + 1) * BLK, rows] = tile.T
            return carry

        lax.fori_loop(0, V // step_rows, grad_step, 0)

    def product_half(h, c):
        def product_step(n, carry):
            start_col = pl.multiple_of(n * NC, NC)
            cols = pl.ds(start_col, NC)
            part = jnp.dot(grad_t[...], wall[:, pl.ds(pl.multiple_of(c * DC + start_col, NC), NC)],
                           preferred_element_type=F32)
            two_0, two_1, m_0, m_1, p_0, p_1, own_0, own_1 = (part[i * HALF:(i + 1) * HALF] for i in range(8))
            x1[h, c, 0, :, cols] = two_0.astype(BF16)
            x1[h, c, 1, :, cols] = m_1.astype(BF16)
            x1[h, c, 2, :, cols] = two_1.astype(BF16)
            x1[h, c, 3, :, cols] = p_0.astype(BF16)
            pm[h, c, 0, :, cols] = m_0
            pm[h, c, 1, :, cols] = p_1
            pm[h, c, 2, :, cols] = own_0
            pm[h, c, 3, :, cols] = own_1
            return carry

        lax.fori_loop(0, DC // NC, product_step, 0)

    def chunked(rows, body):
        def step(n, carry):
            body(pl.ds(pl.multiple_of(n * 32, 32), 32))
            return carry

        lax.fori_loop(0, rows // 32, step, 0)

    def slot(a):
        return pl.ds(pl.multiple_of(a * R, R), R)

    class Reduce:
        def __init__(self, h, c):
            self.at = h, c
            self.b = [remote(x1.at[h, c, i:i + 2], y1.at[h, c, i:i + 2], d) for i, d in ((0, bm), (2, bp))]
            self.b += [remote(x1.at[h, c, i], y1.at[h, c, i], d) for i, d in ((4, bm), (5, bp))]
            self.a = [remote(x2.at[h, c, i], y2.at[h, c, i], d) for i, d in enumerate(a_dev)]

        def begin(self):
            start(*self.b[:2])

        def relay_b(self):
            h, c = self.at
            for i in range(2):
                arrive(self.b[i])

                def relay(rows):
                    x1[h, c, 4 + i, rows, :] = (
                        pm[h, c, i, rows, :] + y1[h, c, 2 * i, rows, :].astype(F32)).astype(BF16)

                chunked(HALF, relay)
                start(self.b[2 + i])

        def end_b(self):
            h, c = self.at
            arrive(*self.b[2:])
            for s, (one, two) in enumerate(((3, 4), (1, 5))):

                def total(rows):
                    r1[h, c, s, rows, :] = (pm[h, c, 2 + s, rows, :] + y1[h, c, one, rows, :].astype(F32)
                                            + y1[h, c, two, rows, :].astype(F32))

                chunked(HALF, total)
            for i in (1, 0, 2):
                for s in range(2):
                    x2[h, c, i, s] = r1[h, c, s, slot((a_p, a_2, a_m)[i]), :].astype(BF16)
                start(self.a[i])

        def end_a(self):
            h, c = self.at
            arrive(*self.a)
            for s in range(2):
                for f in range(DC // 128):
                    cols = slice(f * 128, f * 128 + 128)
                    zs[h, c * (NZ // 2) + f // 2, f % 2, s] = r1[h, c, s, slot(pa), cols] + sum(
                        y2[h, c, i, s, :, cols].astype(F32) for i in range(RING - 1))

    class Reduce_z:
        def __init__(self, h):
            self.h = h
            self.sibling = remote(zs.at[h, z, 1 - core], zr.at[h, core, 0], sibling, z_sem.at[h, 0, core])
            self.others = [[remote(zs.at[h, lax.rem(z + k, NZ), f], zr.at[h, core, k], z_both[k - 1][f],
                                   z_sem.at[h, k, core]) for f in range(2)] for k in range(1, NZ)]
            places = [(1 - core, 0)] + [(c, k) for k in range(1, NZ) for c in range(2)]
            self.arrivals = [pltpu.make_async_remote_copy(
                src_ref=zr.at[h, c, k], dst_ref=zr.at[h, c, k], send_sem=send_sem.at[0], recv_sem=z_sem.at[h, k, c],
                device_id=sibling, device_id_type=MESH) for c, k in places]

        def send(self, c):
            @pl.when(lax.div(z, NZ // 2) == c)
            def _():
                zr[self.h, core, 0] = zs[self.h, z, core]
                start(self.sibling)

            for k in range(1, NZ):

                @pl.when(lax.div(lax.rem(z + k, NZ), NZ // 2) == c)
                def _():
                    start(*self.others[k - 1])

        def end(self):
            h = self.h
            arrive(*self.arrivals)
            for c in range(2):
                total = zr[h, c, 0]
                for k in range(1, NZ):
                    total += zr[h, c, k]
                gh_out[c, h] = total

    d00, d01, d10, d11 = (Reduce(h, c) for h in range(H) for c in range(2))
    z0, z1 = Reduce_z(0), Reduce_z(1)

    weight_copies = [remote(gw_send.at[n], gw_recv.at[n], sibling) for n in range(D // NC)]

    def weight_part(side, n):
        rows = pl.ds(pl.multiple_of(side * ROWS, ROWS), ROWS)
        cols = pl.ds(pl.multiple_of(n * NC, NC), NC)
        lhs = jnp.concatenate([grad[k, rows, :] for k in range(NB)], axis=1)
        rhs = hall[:, :, :, :, cols].reshape(NB * BLK, NC)
        return jnp.dot(lhs, rhs, preferred_element_type=F32), cols

    def weight_other(n):
        gw_send[n] = weight_part(1 - core, n)[0]

    def weight_own(n):
        part, cols = weight_part(core, n)
        gw_out[:, cols] = part + gw_recv[n]

    stat_copy = remote(stat_swap.at[0], stat_swap.at[1], sibling)

    def own_stats():
        for q in range(2):
            line = jnp.zeros((8, 128), F32)
            for h in range(H):
                k = h * RING + pb
                log_total, mean, target = (fin[2, k, pl.ds(i, 1), :] for i in range(3))
                row = jnp.broadcast_to(target - log_total if q == 0 else log_total - mean, (8, 128))
                for s in range(2):
                    group = (h * 2 + s) + core * 4
                    shift = lax.rem(group * R + 256 - (s * RING + pa) * R, 128)
                    line = jnp.where(lanes_of(group), pltpu.roll(row, shift, 1), line)
            stat_swap[0, q] = line
        start(stat_copy)

    def own_stats_store():
        arrive(stat_copy)
        mine = lax.div(lane, 64) == core
        for q, out in enumerate((lp_out, en_out)):
            out[...] = jnp.where(mine, stat_swap[0, q], stat_swap[1, q])[0:1]

    def staged(count, before, body):
        def step(i, carry):
            for j, action in before.items():
                pl.when(i == j)(action)
            body(i)
            return carry

        lax.fori_loop(0, count, step, 0)

    for c in small_in:
        c.wait()
    reorder(ids_in, ids_row)
    reorder(adv_in, adv_row)
    pl.semaphore_wait(barrier, len(peers))
    start(*g0.near, *g1.near)
    for c in [w_in] + own_in:
        c.wait()
    start(w_swap)
    g0.ring()
    g1.ring()
    g0.spread()
    g0.pass_on()
    g1.spread()
    arrive(w_swap, *g0.second)

    def unit(i):
        half = lax.rem(i, 2)
        k = lax.div(i, 2) * RING
        stats_blocks(k + lax.rem(pb + half, RING), k + lax.rem(pb + 3 - half, RING))

    def before_1():
        arrive(*g0.on)

    def before_2():
        s0.begin()
        g1.pass_on()
        s0.step(0)
        arrive(*g1.second)

    def before_3():
        s0.step(1)
        arrive(*g1.on)

    staged(4, {1: before_1, 2: before_2, 3: before_3}, unit)
    s1.begin()
    s0.step(2)

    def half_step(i):
        h, c = lax.div(i, 2), lax.rem(i, 2)

        @pl.when(c == 0)
        def _():
            grad_chunk(h)

        pl.when(i == 2)(d01.relay_b)
        product_half(h, c)

    def before_half_1():
        d00.begin()
        s1.step(0)

    def before_half_2():
        d01.begin()
        s1.step(1)
        d00.relay_b()
        s1.step(2)

    staged(4, {1: before_half_1, 2: before_half_2, 3: d10.begin}, half_step)
    d11.begin()
    own_stats()
    d00.end_b()

    def weight_sent(n, *then):
        def action():
            start(weight_copies[n])
            for step in then:
                step()

        return action

    def weight_came(n, *then):
        def action():
            arrive(weight_copies[n])
            for step in then:
                step()

        return action

    staged(4, {1: weight_sent(0, d01.end_b), 2: weight_sent(1, d10.relay_b), 3: weight_sent(2)}, weight_other)
    start(weight_copies[3])
    d11.relay_b()

    def before_own_1():
        d00.end_a()
        z0.send(0)
        d10.end_b()

    def before_own_2():
        d01.end_a()
        z0.send(1)

    staged(4, {0: weight_came(0), 1: weight_came(1, before_own_1), 2: weight_came(2, before_own_2),
               3: weight_came(3, d11.end_b)}, weight_own)
    d10.end_a()
    z1.send(0)
    z0.end()
    own_stats_store()
    d11.end_a()
    z1.send(1)
    last = [z1.sibling] + [copy for both in z1.others for copy in both]
    for copy in copies:
        if not any(copy is other for other in last):
            copy.wait_send()
    z1.end()
    for copy in last:
        copy.wait_send()


def call(hid, w, ids, adv):
    vmem = pl.BlockSpec(memory_space=pltpu.VMEM)
    anywhere = pl.BlockSpec(memory_space=pl.ANY)
    scratch = [
        pltpu.VMEM((NB, 2, RING, R, D), BF16),
        pltpu.VMEM((V, D), BF16),
        pltpu.VMEM((NB, V, BLK), F32),
        pltpu.VMEM((NB, V, BLK), BF16),
        pltpu.VMEM((RING * BLK, V), BF16),
        pltpu.VMEM((H, 2, 4, HALF, DC), F32),
        pltpu.VMEM((H, 2, 6, HALF, DC), BF16),
        pltpu.VMEM((H, 2, 6, HALF, DC), BF16),
        pltpu.VMEM((H, 2, 2, HALF, DC), F32),
        pltpu.VMEM((H, 2, RING - 1, 2, R, DC), BF16),
        pltpu.VMEM((H, 2, RING - 1, 2, R, DC), BF16),
        pltpu.VMEM((H, NZ, 2, 2, R, 128), F32),
        pltpu.VMEM((H, 2, NZ, 2, R, 128), F32),
        pltpu.VMEM((NB, 4, BLK), F32),
        pltpu.VMEM((H, RING - 1, RING, 4, BLK), F32),
        pltpu.VMEM((H, RING - 1, RING, 4, BLK), F32),
        pltpu.VMEM((H, NZ - 1, RING, 4, BLK), F32),
        pltpu.VMEM((3, NB, 4, BLK), F32),
        pltpu.VMEM((16, 128), jnp.int32),
        pltpu.VMEM((16, 128), F32),
        pltpu.VMEM((16, 128), F32),
        pltpu.VMEM((NB, 1, BLK), jnp.int32),
        pltpu.VMEM((NB, 1, BLK), F32),
        pltpu.VMEM((2, 2, 8, 128), F32),
        pltpu.VMEM((D // NC, ROWS, NC), F32),
        pltpu.VMEM((D // NC, ROWS, NC), F32),
        pltpu.SemaphoreType.DMA((NSEM,)),
        pltpu.SemaphoreType.DMA((NSEM,)),
        pltpu.SemaphoreType.DMA((H, NZ, 2)),
        pltpu.SemaphoreType.DMA((3 + H,)),
    ]
    return pl.pallas_call(
        kernel,
        out_shape=(
            pltpu.VMEM((ROWS, D), F32),
            pltpu.VMEM((2, H, 2, R, 128), F32),
            pltpu.VMEM((1, SHARD), F32),
            pltpu.VMEM((1, SHARD), F32),
        ),
        in_specs=[anywhere] * 4,
        out_specs=(vmem, vmem, vmem, vmem),
        scratch_shapes=scratch,
        compiler_params=pltpu.CompilerParams(
            collective_id=0, has_side_effects=True, vmem_limit_bytes=50 * 2**20),
    )(hid, w, ids, adv)


def store_kernel(*refs):
    count = len(refs) // 2
    moves = [pltpu.make_async_copy(refs[i], refs[count + i], refs[-1].at[i]) for i in range(count)]
    for move in moves:
        move.start()
    for move in moves:
        move.wait()


def store(*arrays):
    return pl.pallas_call(
        store_kernel,
        out_shape=[jax.ShapeDtypeStruct(a.shape, a.dtype) for a in arrays],
        in_specs=[pl.BlockSpec(memory_space=pltpu.VMEM)] * len(arrays),
        out_specs=[pl.BlockSpec(memory_space=pl.ANY)] * len(arrays),
        scratch_shapes=[pltpu.SemaphoreType.DMA((len(arrays),))],
        compiler_params=pltpu.CompilerParams(vmem_limit_bytes=4 * 2**20),
    )(*arrays)


def shards(hidden, head_weight, sampled_ids, advantage):
    hid = hidden.reshape(2, H, 2, R, D)
    grad_weight, grad_hidden, log_prob, entropy = store(*call(
        hid, head_weight, sampled_ids.reshape(16, 128), advantage.reshape(16, 128)))
    return (log_prob.reshape(SHARD), entropy.reshape(SHARD), grad_hidden.reshape(SHARD, 128), grad_weight)


def solution(mesh):
    placed = (P("dp", None), P(("dp", "vocab"), None), P(), P())
    return jax.shard_map(
        shards,
        mesh=mesh,
        in_specs=placed,
        out_specs=(P("dp"), P("dp"), P("dp", "vocab"), P(("dp", "vocab"), None)),
        check_vma=False,
    )
```

```python
import jax
import jax.numpy as jnp
from jax import lax
from jax.experimental import pallas as pl
from jax.experimental.pallas import tpu as pltpu
from jax.sharding import PartitionSpec as P

ENTROPY_COEF = 0.25
MESH = pl.DeviceIdType.MESH
F32, BF16 = jnp.float32, jnp.bfloat16

D = 2048
V = 1024
ROWS = 512
SHARD = 128
RING = 4
NZ = 8
H = 2
R = 16
BLK = 2 * RING * R
HALF = RING * R
NB = RING * H
VC = 256
NC = 512
DC = D // 2
NSEM = 144


def kernel(hid, w, ids, adv, gw_out, gh_out, lp_out, en_out,
           hall, wall, logits, grad, grad_t, pm, x1, y1, r1, x2, y2, zs, zr, st, sx, sy, sz, fin,
           ids_in, adv_in, rolled, ids_row, adv_row, stat_swap, gw_send, gw_recv, send_sem, recv_sem, z_sem, local_sem):
    dp, vo = lax.axis_index("dp"), lax.axis_index("vocab")
    x, y = lax.div(dp, RING), lax.rem(dp, RING)
    z, core = lax.div(vo, 2), lax.rem(vo, 2)
    pa, pb = x + core * (y - x), y + core * (x - y)
    a_p, a_2, a_m = (lax.rem(pa + k, RING) for k in (1, 2, 3))
    b_p, b_2, b_m = (lax.rem(pb + k, RING) for k in (1, 2, 3))

    def place(a, b):
        first, second = a * RING + b, b * RING + a
        return first + core * (second - first)

    def dev(a, b):
        return {"dp": place(a, b), "vocab": vo}

    def zdev(k):
        return {"dp": dp, "vocab": lax.rem(z + k, NZ) * 2 + core}

    sibling = {"dp": dp, "vocab": vo + 1 - 2 * core}

    copies = []

    def remote(src, dst, device, arrival=None):
        i = len(copies)
        copies.append(pltpu.make_async_remote_copy(
            src_ref=src, dst_ref=dst, send_sem=send_sem.at[i], recv_sem=recv_sem.at[i] if arrival is None else arrival,
            device_id=device, device_id_type=MESH))
        return copies[-1]

    def start(*some):
        for copy in some:
            copy.start()

    def arrive(*some):
        for copy in some:
            copy.wait_recv()

    w_rows = pl.ds(pl.multiple_of(core * ROWS, ROWS), ROWS)
    w_in = pltpu.make_async_copy(w, wall.at[w_rows], local_sem.at[0])
    small_in = [pltpu.make_async_copy(ids, ids_in, local_sem.at[1]),
                pltpu.make_async_copy(adv, adv_in, local_sem.at[2])]
    own_in = [pltpu.make_async_copy(hid.at[core, h], hall.at[h * RING + pb, :, pa], local_sem.at[3 + h])
              for h in range(H)]
    for c in [w_in] + small_in + own_in:
        c.start()

    a_dev = [dev(lax.rem(pa + k, RING), pb) for k in (1, 2, 3)]
    b_dev = [dev(pa, lax.rem(pb + k, RING)) for k in (1, 2, 3)]
    z_dev = [zdev(k) for k in range(1, NZ)]
    ap, _, am = a_dev
    bp, _, bm = b_dev
    barrier = pltpu.get_barrier_semaphore()
    z_both = [[dict(dp=dp, vocab=lax.rem(z + k, NZ) * 2 + f) for f in range(2)] for k in range(1, NZ)]
    peers = a_dev + b_dev + [d for both in z_both for d in both] + [sibling]
    for peer in peers:
        pl.semaphore_signal(barrier, inc=1, device_id=peer, device_id_type=MESH)

    w_swap = remote(wall.at[w_rows], wall.at[w_rows], sibling)

    class Gather:
        def __init__(self, h):
            kp, km, k0 = (h * RING + b for b in (b_p, b_m, pb))
            own, there = hid.at[core, h], hall.at[k0, :, pa]
            self.near = [remote(own, there, d) for d in (ap, am)]
            self.far = [remote(hall.at[k0, 0, a_m], hall.at[k0, 0, a_m], ap),
                        remote(hall.at[k0, 1, a_p], hall.at[k0, 1, a_p], am)]
            halves = [hall.at[k0, s] for s in range(2)]
            self.first = [remote(halves[0], halves[0], bp), remote(halves[1], halves[1], bm)]
            self.second = [remote(halves[1], halves[1], bp), remote(halves[0], halves[0], bm)]
            self.on = [remote(hall.at[km, 0], hall.at[km, 0], bp), remote(hall.at[kp, 1], hall.at[kp, 1], bm)]

        def ring(self):
            for near, far in zip(self.near, self.far):
                arrive(near)
                start(far)

        def spread(self):
            start(*self.first, *self.second)

        def pass_on(self):
            for first, on in zip(self.first, self.on):
                arrive(first)
                start(on)

    g0, g1 = Gather(0), Gather(1)

    lane = lax.broadcasted_iota(jnp.int32, (8, 128), 1)

    def lanes_of(group):
        return lax.div(lane, R) == group

    def reorder(source, out):
        both = source[...].astype(F32)
        rolled[...] = jnp.where(core == 0, both, pltpu.roll(both, 64, 1))
        for b in range(RING):
            rows = [jnp.broadcast_to(rolled[pl.ds(place(a, b), 1), :], (8, 128)) for a in range(RING)]
            for h in range(H):
                line = jnp.zeros((8, 128), F32)
                for a in range(RING):
                    for s in range(2):
                        group = s * RING + a
                        shift = (group * R - h * 2 * R - s * R) % 128
                        line = jnp.where(lanes_of(group), pltpu.roll(rows[a], shift, 1), line)
                out[h * RING + b] = line[0:1].astype(out.dtype)

    first_row = dp * (2 * ROWS * NZ) + z * (2 * ROWS)

    def stats_blocks(*ks):
        token_ids = jnp.concatenate([ids_row[k] for k in ks], axis=1) - first_row

        def product(v):
            tokens = jnp.concatenate([hall[k].reshape(BLK, D) for k in ks], axis=0)
            part = lax.dot_general(wall[v * VC:(v + 1) * VC, :], tokens, (((1,), (1,)), ((), ())),
                                   preferred_element_type=F32)
            for j, k in enumerate(ks):
                logits[k, v * VC:(v + 1) * VC, :] = part[:, j * BLK:(j + 1) * BLK]

        def add_sums(v, peak, sums):
            rows = slice(v * VC, (v + 1) * VC)
            part = jnp.concatenate([logits[k, rows, :] for k in ks], axis=1)
            above = jnp.max(part, axis=0, keepdims=True)
            new_peak = above if peak is None else jnp.maximum(peak, above)
            expon = jnp.exp(part - new_peak)
            row = lax.broadcasted_iota(jnp.int32, part.shape, 0)
            picked = jnp.where(row == token_ids - v * VC, part, 0.0)
            more = [jnp.sum(p, axis=0, keepdims=True) for p in (expon, expon * part, picked)]
            if peak is not None:
                scale = jnp.exp(peak - new_peak)
                more = [m + s * f for m, s, f in zip(more, sums, (scale, scale, 1.0))]
            return new_peak, more

        peak, sums = None, None
        product(0)
        for v in range(1, V // VC):
            product(v)
            peak, sums = add_sums(v - 1, peak, sums)
        peak, sums = add_sums(V // VC - 1, peak, sums)
        for q, row in enumerate([peak] + sums):
            for j, k in enumerate(ks):
                st[k, pl.ds(q, 1), :] = row[:, j * BLK:(j + 1) * BLK]

    def stats_merge(ref, slots, sent):
        arrive(*sent)
        parts = [ref[...]] + [slots[i] for i in range(len(sent))]
        peak = parts[0][:, 0:1, :]
        for p in parts[1:]:
            peak = jnp.maximum(peak, p[:, 0:1, :])
        total, weighted, target = 0.0, 0.0, 0.0
        for p in parts:
            scale = jnp.exp(p[:, 0:1, :] - peak)
            total += scale * p[:, 1:2, :]
            weighted += scale * p[:, 2:3, :]
            target += p[:, 3:4, :]
        return peak, total, weighted, target

    class Stats:
        def __init__(self, h):
            blocks = pl.ds(h * RING, RING)
            self.steps = [(st.at[blocks], sz.at[h], fin.at[0, blocks], z_dev),
                          (fin.at[0, blocks], sx.at[h], fin.at[1, blocks], a_dev),
                          (fin.at[1, blocks], sy.at[h], fin.at[2, blocks], b_dev)]
            self.sent = [[remote(ref, slots.at[i], d) for i, d in enumerate(devices)]
                         for ref, slots, _, devices in self.steps]

        def begin(self):
            start(*self.sent[0])

        def step(self, i):
            ref, slots, out, _ = self.steps[i]
            rows = stats_merge(ref, slots, self.sent[i])
            if i == 2:
                peak, total, weighted, target = rows
                rows = (peak + jnp.log(total), weighted / total, target)
            for q, row in enumerate(rows):
                out[:, pl.ds(q, 1), :] = row
            if i < 2:
                start(*self.sent[i + 1])

    s0, s1 = Stats(0), Stats(1)

    order = (b_2, b_m, b_p, pb)

    def grad_chunk(h):
        ks = [h * RING + b for b in order]
        token_ids = jnp.concatenate([ids_row[k] for k in ks], axis=1) - first_row
        advantage = jnp.concatenate([adv_row[k] for k in ks], axis=1)
        log_total = jnp.concatenate([fin[2, k, 0:1, :] for k in ks], axis=1)
        mean = jnp.concatenate([fin[2, k, 1:2, :] for k in ks], axis=1)
        level = advantage - ENTROPY_COEF * mean
        step_rows = 128

        def grad_step(v, carry):
            start_row = pl.multiple_of(v * step_rows, step_rows)
            rows = pl.ds(start_row, step_rows)
            part = jnp.concatenate([logits[k, rows, :] for k in ks], axis=1)
            prob = jnp.exp(part - log_total)
            row = lax.broadcasted_iota(jnp.int32, part.shape, 0)
            chosen = jnp.where(row == token_ids - start_row, advantage, 0.0)
            low = (chosen - prob * (level + ENTROPY_COEF * part)).astype(BF16)
            for j, k in enumerate(ks):
                tile = low[:, j * BLK:(j + 1) * BLK]
                grad[k, rows, :] = tile
                grad_t[j * BLK:(j + 1) * BLK, rows] = tile.T
            return carry

        lax.fori_loop(0, V // step_rows, grad_step, 0)

    def product_half(h, c):
        def product_step(n, carry):
            cols = pl.ds(pl.multiple_of(n * NC, NC), NC)
            rhs = [wall[:, pl.ds(pl.multiple_of((n * (NC // 128) + j) * 256 + c * 128, 128), 128)] for j in range(NC // 128)]
            part = jnp.dot(grad_t[...], jnp.concatenate(rhs, axis=1), preferred_element_type=F32)
            two_0, two_1, m_0, m_1, p_0, p_1, own_0, own_1 = (part[i * HALF:(i + 1) * HALF] for i in range(8))
            x1[h, c, 0, :, cols] = two_0.astype(BF16)
            x1[h, c, 1, :, cols] = m_1.astype(BF16)
            x1[h, c, 2, :, cols] = two_1.astype(BF16)
            x1[h, c, 3, :, cols] = p_0.astype(BF16)
            pm[h, c, 0, :, cols] = m_0
            pm[h, c, 1, :, cols] = p_1
            pm[h, c, 2, :, cols] = own_0
            pm[h, c, 3, :, cols] = own_1
            return carry

        lax.fori_loop(0, DC // NC, product_step, 0)

    def chunked(rows, body):
        def step(n, carry):
            body(pl.ds(pl.multiple_of(n * 32, 32), 32))
            return carry

        lax.fori_loop(0, rows // 32, step, 0)

    def slot(a):
        return pl.ds(pl.multiple_of(a * R, R), R)

    class Reduce:
        def __init__(self, h, c):
            self.at = h, c
            self.b = [remote(x1.at[h, c, i:i + 2], y1.at[h, c, i:i + 2], d) for i, d in ((0, bm), (2, bp))]
            self.b += [remote(x1.at[h, c, i], y1.at[h, c, i], d) for i, d in ((4, bm), (5, bp))]
            self.a = [remote(x2.at[h, c, i], y2.at[h, c, i], d) for i, d in enumerate(a_dev)]

        def begin(self):
            start(*self.b[:2])

        def relay_b(self):
            h, c = self.at
            for i in range(2):
                arrive(self.b[i])

                def relay(rows):
                    x1[h, c, 4 + i, rows, :] = (
                        pm[h, c, i, rows, :] + y1[h, c, 2 * i, rows, :].astype(F32)).astype(BF16)

                chunked(HALF, relay)
                start(self.b[2 + i])

        def end_b(self):
            h, c = self.at
            arrive(*self.b[2:])
            for s, (one, two) in enumerate(((3, 4), (1, 5))):

                def total(rows):
                    r1[h, c, s, rows, :] = (pm[h, c, 2 + s, rows, :] + y1[h, c, one, rows, :].astype(F32)
                                            + y1[h, c, two, rows, :].astype(F32))

                chunked(HALF, total)
            for i in (1, 0, 2):
                for s in range(2):
                    x2[h, c, i, s] = r1[h, c, s, slot((a_p, a_2, a_m)[i]), :].astype(BF16)
                start(self.a[i])

        def end_a(self):
            h, c = self.at
            arrive(*self.a)
            for s in range(2):
                for j in range(NZ):
                    cols = slice(j * 128, j * 128 + 128)
                    zs[h, j, c, s] = r1[h, c, s, slot(pa), cols] + sum(
                        y2[h, c, i, s, :, cols].astype(F32) for i in range(RING - 1))

    class Reduce_z:
        def __init__(self, h):
            self.h = h
            self.sibling = remote(zs.at[h, z, 1 - core], zr.at[h, core, 0], sibling, z_sem.at[h, 0, core])
            self.others = [[remote(zs.at[h, lax.rem(z + k, NZ), f], zr.at[h, core, k], z_both[k - 1][f],
                                   z_sem.at[h, k, core]) for f in range(2)] for k in range(1, NZ)]
            places = [(1 - core, 0)] + [(c, k) for k in range(1, NZ) for c in range(2)]
            self.arrivals = [pltpu.make_async_remote_copy(
                src_ref=zr.at[h, c, k], dst_ref=zr.at[h, c, k], send_sem=send_sem.at[0], recv_sem=z_sem.at[h, k, c],
                device_id=sibling, device_id_type=MESH) for c, k in places]

        def send(self, c):
            start(*[both[c] for both in self.others])

            @pl.when(core == c)
            def _():
                zr[self.h, core, 0] = zs[self.h, z, core]

            @pl.when(core != c)
            def _():
                start(self.sibling)

        def end(self):
            h = self.h
            arrive(*self.arrivals)
            for c in range(2):
                total = zr[h, c, 0]
                for k in range(1, NZ):
                    total += zr[h, c, k]
                gh_out[c, h] = total

    d00, d01, d10, d11 = (Reduce(h, c) for h in range(H) for c in range(2))
    z0, z1 = Reduce_z(0), Reduce_z(1)

    weight_copies = [remote(gw_send.at[n], gw_recv.at[n], sibling) for n in range(D // NC)]

    def weight_part(side, n):
        rows = pl.ds(pl.multiple_of(side * ROWS, ROWS), ROWS)
        cols = pl.ds(pl.multiple_of(n * NC, NC), NC)
        lhs = jnp.concatenate([grad[k, rows, :] for k in range(NB)], axis=1)
        rhs = hall[:, :, :, :, cols].reshape(NB * BLK, NC)
        return jnp.dot(lhs, rhs, preferred_element_type=F32), cols

    def weight_other(n):
        gw_send[n] = weight_part(1 - core, n)[0]

    def weight_own(n):
        part, cols = weight_part(core, n)
        gw_out[:, cols] = part + gw_recv[n]

    stat_copy = remote(stat_swap.at[0], stat_swap.at[1], sibling)

    def own_stats():
        for q in range(2):
            line = jnp.zeros((8, 128), F32)
            for h in range(H):
                k = h * RING + pb
                log_total, mean, target = (fin[2, k, pl.ds(i, 1), :] for i in range(3))
                row = jnp.broadcast_to(target - log_total if q == 0 else log_total - mean, (8, 128))
                for s in range(2):
                    group = (h * 2 + s) + core * 4
                    shift = lax.rem(group * R + 256 - (s * RING + pa) * R, 128)
                    line = jnp.where(lanes_of(group), pltpu.roll(row, shift, 1), line)
            stat_swap[0, q] = line
        start(stat_copy)

    def own_stats_store():
        arrive(stat_copy)
        mine = lax.div(lane, 64) == core
        for q, out in enumerate((lp_out, en_out)):
            out[...] = jnp.where(mine, stat_swap[0, q], stat_swap[1, q])[0:1]

    def staged(count, before, body):
        def step(i, carry):
            for j, action in before.items():
                pl.when(i == j)(action)
            body(i)
            return carry

        lax.fori_loop(0, count, step, 0)

    pl.semaphore_wait(barrier, len(peers))
    start(*g0.near, *g1.near)
    w_in.wait()
    start(w_swap)
    for c in small_in + own_in:
        c.wait()
    reorder(ids_in, ids_row)
    reorder(adv_in, adv_row)
    g0.ring()
    g1.ring()
    arrive(*g0.far)
    g0.spread()
    arrive(*g1.far, w_swap)
    stats_blocks(pb, RING + pb)
    g0.pass_on()
    g1.spread()
    arrive(*g0.second)
    stats_blocks(b_m, b_p)
    arrive(*g0.on)
    stats_blocks(b_2)
    s0.begin()
    g1.pass_on()
    s0.step(0)
    s0.step(1)
    arrive(*g1.second)
    stats_blocks(RING + b_m, RING + b_p)
    s0.step(2)

    def half_step(i):
        h, c = lax.div(i, 2), lax.rem(i, 2)

        @pl.when(c == 0)
        def _():
            grad_chunk(h)

        pl.when(i == 2)(d00.end_b)
        product_half(h, c)

    def before_half_1():
        d00.begin()
        arrive(*g1.on)
        stats_blocks(RING + b_2)
        s1.begin()

    def before_half_2():
        d01.begin()
        s1.step(0)
        d00.relay_b()
        s1.step(1)
        d01.relay_b()
        s1.step(2)

    def before_half_3():
        d10.begin()
        d01.end_b()

    staged(4, {1: before_half_1, 2: before_half_2, 3: before_half_3}, half_step)
    d11.begin()
    own_stats()

    def weight_sent(n, *then):
        def action():
            start(weight_copies[n])
            for step in then:
                step()

        return action

    def weight_came(n, *then):
        def action():
            arrive(weight_copies[n])
            for step in then:
                step()

        return action

    def z0_first():
        d00.end_a()
        z0.send(0)

    staged(4, {1: weight_sent(0), 2: weight_sent(1, z0_first), 3: weight_sent(2, d10.relay_b)}, weight_other)
    start(weight_copies[3])
    d01.end_a()
    z0.send(1)
    staged(4, {0: weight_came(0), 1: weight_came(1), 2: weight_came(2, d11.relay_b), 3: weight_came(3)}, weight_own)
    d10.end_b()
    z0.end()
    own_stats_store()
    d11.end_b()
    d10.end_a()
    z1.send(0)
    d11.end_a()
    z1.send(1)
    last = [z1.sibling] + [copy for both in z1.others for copy in both]
    for copy in copies:
        if not any(copy is other for other in last):
            copy.wait_send()
    z1.end()
    for copy in last:
        copy.wait_send()


def call(hid, w, ids, adv):
    vmem = pl.BlockSpec(memory_space=pltpu.VMEM)
    anywhere = pl.BlockSpec(memory_space=pl.ANY)
    scratch = [
        pltpu.VMEM((NB, 2, RING, R, D), BF16),
        pltpu.VMEM((V, D), BF16),
        pltpu.VMEM((NB, V, BLK), F32),
        pltpu.VMEM((NB, V, BLK), BF16),
        pltpu.VMEM((RING * BLK, V), BF16),
        pltpu.VMEM((H, 2, 4, HALF, DC), F32),
        pltpu.VMEM((H, 2, 6, HALF, DC), BF16),
        pltpu.VMEM((H, 2, 6, HALF, DC), BF16),
        pltpu.VMEM((H, 2, 2, HALF, DC), F32),
        pltpu.VMEM((H, 2, RING - 1, 2, R, DC), BF16),
        pltpu.VMEM((H, 2, RING - 1, 2, R, DC), BF16),
        pltpu.VMEM((H, NZ, 2, 2, R, 128), F32),
        pltpu.VMEM((H, 2, NZ, 2, R, 128), F32),
        pltpu.VMEM((NB, 4, BLK), F32),
        pltpu.VMEM((H, RING - 1, RING, 4, BLK), F32),
        pltpu.VMEM((H, RING - 1, RING, 4, BLK), F32),
        pltpu.VMEM((H, NZ - 1, RING, 4, BLK), F32),
        pltpu.VMEM((3, NB, 4, BLK), F32),
        pltpu.VMEM((16, 128), jnp.int32),
        pltpu.VMEM((16, 128), F32),
        pltpu.VMEM((16, 128), F32),
        pltpu.VMEM((NB, 1, BLK), jnp.int32),
        pltpu.VMEM((NB, 1, BLK), F32),
        pltpu.VMEM((2, 2, 8, 128), F32),
        pltpu.VMEM((D // NC, ROWS, NC), F32),
        pltpu.VMEM((D // NC, ROWS, NC), F32),
        pltpu.SemaphoreType.DMA((NSEM,)),
        pltpu.SemaphoreType.DMA((NSEM,)),
        pltpu.SemaphoreType.DMA((H, NZ, 2)),
        pltpu.SemaphoreType.DMA((3 + H,)),
    ]
    return pl.pallas_call(
        kernel,
        out_shape=(
            pltpu.VMEM((ROWS, D), F32),
            pltpu.VMEM((2, H, 2, R, 128), F32),
            pltpu.VMEM((1, SHARD), F32),
            pltpu.VMEM((1, SHARD), F32),
        ),
        in_specs=[anywhere] * 4,
        out_specs=(vmem, vmem, vmem, vmem),
        scratch_shapes=scratch,
        compiler_params=pltpu.CompilerParams(
            collective_id=0, has_side_effects=True, vmem_limit_bytes=50 * 2**20),
    )(hid, w, ids, adv)


def store_kernel(*refs):
    count = len(refs) // 2
    moves = [pltpu.make_async_copy(refs[i], refs[count + i], refs[-1].at[i]) for i in range(count)]
    for move in moves:
        move.start()
    for move in moves:
        move.wait()


def store(*arrays):
    return pl.pallas_call(
        store_kernel,
        out_shape=[jax.ShapeDtypeStruct(a.shape, a.dtype) for a in arrays],
        in_specs=[pl.BlockSpec(memory_space=pltpu.VMEM)] * len(arrays),
        out_specs=[pl.BlockSpec(memory_space=pl.ANY)] * len(arrays),
        scratch_shapes=[pltpu.SemaphoreType.DMA((len(arrays),))],
        compiler_params=pltpu.CompilerParams(vmem_limit_bytes=4 * 2**20),
    )(*arrays)


def shards(hidden, head_weight, sampled_ids, advantage):
    hid = hidden.reshape(2, H, 2, R, D)
    grad_weight, grad_hidden, log_prob, entropy = store(*call(
        hid, head_weight, sampled_ids.reshape(16, 128), advantage.reshape(16, 128)))
    return (log_prob.reshape(SHARD), entropy.reshape(SHARD), grad_hidden.reshape(SHARD, 128), grad_weight)


def solution(mesh):
    placed = (P("dp", None), P(("dp", "vocab"), None), P(), P())
    return jax.shard_map(
        shards,
        mesh=mesh,
        in_specs=placed,
        out_specs=(P("dp"), P("dp"), P("dp", "vocab"), P(("dp", "vocab"), None)),
        check_vma=False,
    )
```

```python
import jax
import jax.numpy as jnp
from jax import lax
from jax.experimental import pallas as pl
from jax.experimental.pallas import tpu as pltpu
from jax.sharding import PartitionSpec as P

ENTROPY_COEF = 0.25
MESH = pl.DeviceIdType.MESH
F32, BF16 = jnp.float32, jnp.bfloat16

D = 2048
V = 1024
ROWS = 512
SHARD = 128
RING = 4
NZ = 8
H = 2
R = 16
BLK = 2 * RING * R
HALF = RING * R
NB = RING * H
VC = 256
NC = 512
DC = D // 2
NSEM = 144


def kernel(hid, w, ids, adv, gw_out, gh_out, lp_out, en_out,
           hall, wall, logits, grad, grad_t, pm, x1, y1, r1, x2, y2, zs, zr, st, sx, sy, sz, fin,
           ids_in, adv_in, rolled, ids_row, adv_row, stat_swap, gw_send, gw_recv, send_sem, recv_sem, z_sem, local_sem):
    dp, vo = lax.axis_index("dp"), lax.axis_index("vocab")
    x, y = lax.div(dp, RING), lax.rem(dp, RING)
    z, core = lax.div(vo, 2), lax.rem(vo, 2)
    pa, pb = x + core * (y - x), y + core * (x - y)
    a_p, a_2, a_m = (lax.rem(pa + k, RING) for k in (1, 2, 3))
    b_p, b_2, b_m = (lax.rem(pb + k, RING) for k in (1, 2, 3))

    def place(a, b):
        first, second = a * RING + b, b * RING + a
        return first + core * (second - first)

    def dev(a, b):
        return {"dp": place(a, b), "vocab": vo}

    def zdev(k):
        return {"dp": dp, "vocab": lax.rem(z + k, NZ) * 2 + core}

    sibling = {"dp": dp, "vocab": vo + 1 - 2 * core}

    copies = []

    def remote(src, dst, device, arrival=None):
        i = len(copies)
        copies.append(pltpu.make_async_remote_copy(
            src_ref=src, dst_ref=dst, send_sem=send_sem.at[i], recv_sem=recv_sem.at[i] if arrival is None else arrival,
            device_id=device, device_id_type=MESH))
        return copies[-1]

    def start(*some):
        for copy in some:
            copy.start()

    def arrive(*some):
        for copy in some:
            copy.wait_recv()

    w_rows = pl.ds(pl.multiple_of(core * ROWS, ROWS), ROWS)
    w_in = pltpu.make_async_copy(w, wall.at[w_rows], local_sem.at[0])
    small_in = [pltpu.make_async_copy(ids, ids_in, local_sem.at[1]),
                pltpu.make_async_copy(adv, adv_in, local_sem.at[2])]
    own_in = [pltpu.make_async_copy(hid.at[core, h], hall.at[h * RING + pb, :, pa], local_sem.at[3 + h])
              for h in range(H)]
    for c in [w_in] + small_in + own_in:
        c.start()

    a_dev = [dev(lax.rem(pa + k, RING), pb) for k in (1, 2, 3)]
    b_dev = [dev(pa, lax.rem(pb + k, RING)) for k in (1, 2, 3)]
    z_dev = [zdev(k) for k in range(1, NZ)]
    ap, _, am = a_dev
    bp, _, bm = b_dev
    barrier = pltpu.get_barrier_semaphore()
    z_both = [[dict(dp=dp, vocab=lax.rem(z + k, NZ) * 2 + f) for f in range(2)] for k in range(1, NZ)]
    peers = a_dev + b_dev + [d for both in z_both for d in both] + [sibling]
    for peer in peers:
        pl.semaphore_signal(barrier, inc=1, device_id=peer, device_id_type=MESH)

    w_swap = remote(wall.at[w_rows], wall.at[w_rows], sibling)

    class Gather:
        def __init__(self, h):
            kp, km, k0 = (h * RING + b for b in (b_p, b_m, pb))
            own, there = hid.at[core, h], hall.at[k0, :, pa]
            self.near = [remote(own, there, d) for d in (ap, am)]
            self.far = [remote(hall.at[k0, 0, a_m], hall.at[k0, 0, a_m], ap),
                        remote(hall.at[k0, 1, a_p], hall.at[k0, 1, a_p], am)]
            halves = [hall.at[k0, s] for s in range(2)]
            self.first = [remote(halves[0], halves[0], bp), remote(halves[1], halves[1], bm)]
            self.second = [remote(halves[1], halves[1], bp), remote(halves[0], halves[0], bm)]
            self.on = [remote(hall.at[km, 0], hall.at[km, 0], bp), remote(hall.at[kp, 1], hall.at[kp, 1], bm)]

        def ring(self):
            for near, far in zip(self.near, self.far):
                arrive(near)
                start(far)

        def spread(self):
            arrive(*self.far)
            start(*self.first, *self.second)

        def pass_on(self):
            for first, on in zip(self.first, self.on):
                arrive(first)
                start(on)

    g0, g1 = Gather(0), Gather(1)

    lane = lax.broadcasted_iota(jnp.int32, (8, 128), 1)

    def lanes_of(group):
        return lax.div(lane, R) == group

    def reorder(source, out):
        both = source[...].astype(F32)
        rolled[...] = jnp.where(core == 0, both, pltpu.roll(both, 64, 1))
        for b in range(RING):
            rows = [jnp.broadcast_to(rolled[pl.ds(place(a, b), 1), :], (8, 128)) for a in range(RING)]
            for h in range(H):
                line = jnp.zeros((8, 128), F32)
                for a in range(RING):
                    for s in range(2):
                        group = s * RING + a
                        shift = (group * R - h * 2 * R - s * R) % 128
                        line = jnp.where(lanes_of(group), pltpu.roll(rows[a], shift, 1), line)
                out[h * RING + b] = line[0:1].astype(out.dtype)

    first_row = dp * (2 * ROWS * NZ) + z * (2 * ROWS)

    def stats_blocks(k_one, k_two):
        token_ids = jnp.concatenate([ids_row[k_one], ids_row[k_two]], axis=1) - first_row

        def product(v):
            tokens = jnp.concatenate([hall[k_one].reshape(BLK, D), hall[k_two].reshape(BLK, D)], axis=0)
            part = lax.dot_general(wall[v * VC:(v + 1) * VC, :], tokens, (((1,), (1,)), ((), ())),
                                   preferred_element_type=F32)
            logits[k_one, v * VC:(v + 1) * VC, :] = part[:, :BLK]
            logits[k_two, v * VC:(v + 1) * VC, :] = part[:, BLK:]

        def add_sums(v, peak, sums):
            rows = slice(v * VC, (v + 1) * VC)
            part = jnp.concatenate([logits[k_one, rows, :], logits[k_two, rows, :]], axis=1)
            above = jnp.max(part, axis=0, keepdims=True)
            new_peak = above if peak is None else jnp.maximum(peak, above)
            expon = jnp.exp(part - new_peak)
            row = lax.broadcasted_iota(jnp.int32, part.shape, 0)
            picked = jnp.where(row == token_ids - v * VC, part, 0.0)
            more = [jnp.sum(p, axis=0, keepdims=True) for p in (expon, expon * part, picked)]
            if peak is not None:
                scale = jnp.exp(peak - new_peak)
                more = [m + s * f for m, s, f in zip(more, sums, (scale, scale, 1.0))]
            return new_peak, more

        peak, sums = None, None
        product(0)
        for v in range(1, V // VC):
            product(v)
            peak, sums = add_sums(v - 1, peak, sums)
        peak, sums = add_sums(V // VC - 1, peak, sums)
        for q, row in enumerate([peak] + sums):
            st[k_one, pl.ds(q, 1), :] = row[:, :BLK]
            st[k_two, pl.ds(q, 1), :] = row[:, BLK:]

    def stats_merge(ref, slots, sent):
        arrive(*sent)
        parts = [ref[...]] + [slots[i] for i in range(len(sent))]
        peak = parts[0][:, 0:1, :]
        for p in parts[1:]:
            peak = jnp.maximum(peak, p[:, 0:1, :])
        total, weighted, target = 0.0, 0.0, 0.0
        for p in parts:
            scale = jnp.exp(p[:, 0:1, :] - peak)
            total += scale * p[:, 1:2, :]
            weighted += scale * p[:, 2:3, :]
            target += p[:, 3:4, :]
        return peak, total, weighted, target

    class Stats:
        def __init__(self, h):
            blocks = pl.ds(h * RING, RING)
            self.steps = [(st.at[blocks], sz.at[h], fin.at[0, blocks], z_dev),
                          (fin.at[0, blocks], sx.at[h], fin.at[1, blocks], a_dev),
                          (fin.at[1, blocks], sy.at[h], fin.at[2, blocks], b_dev)]
            self.sent = [[remote(ref, slots.at[i], d) for i, d in enumerate(devices)]
                         for ref, slots, _, devices in self.steps]

        def begin(self):
            start(*self.sent[0])

        def step(self, i):
            ref, slots, out, _ = self.steps[i]
            rows = stats_merge(ref, slots, self.sent[i])
            if i == 2:
                peak, total, weighted, target = rows
                rows = (peak + jnp.log(total), weighted / total, target)
            for q, row in enumerate(rows):
                out[:, pl.ds(q, 1), :] = row
            if i < 2:
                start(*self.sent[i + 1])

    s0, s1 = Stats(0), Stats(1)

    order = (b_2, b_m, b_p, pb)
    STEPS = D // NC
    GR = V // STEPS

    def grad_step(h, pair, v):
        ks = [h * RING + b for b in order[2 * pair:2 * pair + 2]]
        token_ids = jnp.concatenate([ids_row[k] for k in ks], axis=1) - first_row
        advantage = jnp.concatenate([adv_row[k] for k in ks], axis=1)
        log_total = jnp.concatenate([fin[2, k, 0:1, :] for k in ks], axis=1)
        mean = jnp.concatenate([fin[2, k, 1:2, :] for k in ks], axis=1)
        level = advantage - ENTROPY_COEF * mean
        start_row = pl.multiple_of(v * GR, GR)
        rows = pl.ds(start_row, GR)
        part = jnp.concatenate([logits[k, rows, :] for k in ks], axis=1)
        prob = jnp.exp(part - log_total)
        row = lax.broadcasted_iota(jnp.int32, part.shape, 0)
        chosen = jnp.where(row == token_ids - start_row, advantage, 0.0)
        low = (chosen - prob * (level + ENTROPY_COEF * part)).astype(BF16)
        for j, k in enumerate(ks):
            tile = low[:, j * BLK:(j + 1) * BLK]
            grad[k, rows, :] = tile
            grad_t[pair, j * BLK:(j + 1) * BLK, rows] = tile.T

    def product_step(h, pair, n):
        c, m = lax.div(n, STEPS // 2), lax.rem(n, STEPS // 2)
        cols = pl.ds(pl.multiple_of(m * NC, NC), NC)
        part = jnp.dot(grad_t[pair], wall[:, pl.ds(pl.multiple_of(n * NC, NC), NC)], preferred_element_type=F32)
        one_0, one_1, two_0, two_1 = (part[i * HALF:(i + 1) * HALF] for i in range(4))
        if pair == 0:
            x1[h, c, 0, :, cols] = one_0.astype(BF16)
            x1[h, c, 2, :, cols] = one_1.astype(BF16)
            pm[h, c, 0, :, cols] = two_0
            x1[h, c, 1, :, cols] = two_1.astype(BF16)
        else:
            x1[h, c, 3, :, cols] = one_0.astype(BF16)
            pm[h, c, 1, :, cols] = one_1
            pm[h, c, 2, :, cols] = two_0
            pm[h, c, 3, :, cols] = two_1

    def each_step(*bodies):
        def step(n, carry):
            for body in bodies:
                body(n)
            return carry

        lax.fori_loop(0, STEPS, step, 0)

    def chunked(rows, body):
        def step(n, carry):
            body(pl.ds(pl.multiple_of(n * 32, 32), 32))
            return carry

        lax.fori_loop(0, rows // 32, step, 0)

    def slot(a):
        return pl.ds(pl.multiple_of(a * R, R), R)

    class Reduce:
        def __init__(self, h, c):
            self.at = h, c
            self.b = [remote(x1.at[h, c, i], y1.at[h, c, i], d)
                      for i, d in ((0, bm), (2, bp), (1, bm), (3, bp), (4, bm), (5, bp))]
            self.a = [remote(x2.at[h, c, i], y2.at[h, c, i], d) for i, d in enumerate(a_dev)]

        def send(self, *which):
            start(*[self.b[i] for i in which])

        def relay_b(self):
            h, c = self.at
            for i in range(2):
                arrive(self.b[i])

                def relay(rows):
                    x1[h, c, 4 + i, rows, :] = (
                        pm[h, c, i, rows, :] + y1[h, c, 2 * i, rows, :].astype(F32)).astype(BF16)

                chunked(HALF, relay)
                start(self.b[4 + i])

        def end_b(self):
            h, c = self.at
            arrive(*self.b[2:])
            for s, (one, two) in enumerate(((3, 4), (1, 5))):

                def total(rows):
                    r1[h, c, s, rows, :] = (pm[h, c, 2 + s, rows, :] + y1[h, c, one, rows, :].astype(F32)
                                            + y1[h, c, two, rows, :].astype(F32))

                chunked(HALF, total)
            for i in (1, 0, 2):
                for s in range(2):
                    x2[h, c, i, s] = r1[h, c, s, slot((a_p, a_2, a_m)[i]), :].astype(BF16)
                start(self.a[i])

        def end_a(self):
            h, c = self.at
            arrive(*self.a)
            for s in range(2):
                for f in range(DC // 128):
                    cols = slice(f * 128, f * 128 + 128)
                    zs[h, c * (NZ // 2) + f // 2, f % 2, s] = r1[h, c, s, slot(pa), cols] + sum(
                        y2[h, c, i, s, :, cols].astype(F32) for i in range(RING - 1))

    class Reduce_z:
        def __init__(self, h):
            self.h = h
            self.sibling = remote(zs.at[h, z, 1 - core], zr.at[h, core, 0], sibling, z_sem.at[h, 0, core])
            self.others = [[remote(zs.at[h, lax.rem(z + k, NZ), f], zr.at[h, core, k], z_both[k - 1][f],
                                   z_sem.at[h, k, core]) for f in range(2)] for k in range(1, NZ)]
            places = [(1 - core, 0)] + [(c, k) for k in range(1, NZ) for c in range(2)]
            self.arrivals = [pltpu.make_async_remote_copy(
                src_ref=zr.at[h, c, k], dst_ref=zr.at[h, c, k], send_sem=send_sem.at[0], recv_sem=z_sem.at[h, k, c],
                device_id=sibling, device_id_type=MESH) for c, k in places]

        def send(self, c):
            @pl.when(lax.div(z, NZ // 2) == c)
            def _():
                zr[self.h, core, 0] = zs[self.h, z, core]
                start(self.sibling)

            for k in range(1, NZ):

                @pl.when(lax.div(lax.rem(z + k, NZ), NZ // 2) == c)
                def _():
                    start(*self.others[k - 1])

        def end(self):
            h = self.h
            arrive(*self.arrivals)
            for c in range(2):
                total = zr[h, c, 0]
                for k in range(1, NZ):
                    total += zr[h, c, k]
                gh_out[c, h] = total

    d00, d01, d10, d11 = (Reduce(h, c) for h in range(H) for c in range(2))
    z0, z1 = Reduce_z(0), Reduce_z(1)

    weight_copies = [remote(gw_send.at[n], gw_recv.at[n], sibling) for n in range(D // NC)]

    def weight_part(side, n):
        rows = pl.ds(pl.multiple_of(side * ROWS, ROWS), ROWS)
        cols = pl.ds(pl.multiple_of(n * NC, NC), NC)
        lhs = jnp.concatenate([grad[k, rows, :] for k in range(NB)], axis=1)
        rhs = hall[:, :, :, :, cols].reshape(NB * BLK, NC)
        return jnp.dot(lhs, rhs, preferred_element_type=F32), cols

    def weight_other(n):
        gw_send[n] = weight_part(1 - core, n)[0]

    def weight_own(n):
        part, cols = weight_part(core, n)
        gw_out[:, cols] = part + gw_recv[n]

    stat_copy = remote(stat_swap.at[0], stat_swap.at[1], sibling)

    def own_stats():
        for q in range(2):
            line = jnp.zeros((8, 128), F32)
            for h in range(H):
                k = h * RING + pb
                log_total, mean, target = (fin[2, k, pl.ds(i, 1), :] for i in range(3))
                row = jnp.broadcast_to(target - log_total if q == 0 else log_total - mean, (8, 128))
                for s in range(2):
                    group = (h * 2 + s) + core * 4
                    shift = lax.rem(group * R + 256 - (s * RING + pa) * R, 128)
                    line = jnp.where(lanes_of(group), pltpu.roll(row, shift, 1), line)
            stat_swap[0, q] = line
        start(stat_copy)

    def own_stats_store():
        arrive(stat_copy)
        mine = lax.div(lane, 64) == core
        for q, out in enumerate((lp_out, en_out)):
            out[...] = jnp.where(mine, stat_swap[0, q], stat_swap[1, q])[0:1]

    def staged(count, before, body):
        def step(i, carry):
            for j, action in before.items():
                pl.when(i == j)(action)
            body(i)
            return carry

        lax.fori_loop(0, count, step, 0)

    for c in small_in:
        c.wait()
    reorder(ids_in, ids_row)
    reorder(adv_in, adv_row)
    pl.semaphore_wait(barrier, len(peers))
    start(*g0.near, *g1.near)
    for c in [w_in] + own_in:
        c.wait()
    start(w_swap)
    g0.ring()
    g1.ring()
    g0.spread()
    g0.pass_on()
    g1.spread()
    arrive(w_swap, *g0.second)

    def unit(i):
        half = lax.rem(i, 2)
        k = lax.div(i, 2) * RING
        stats_blocks(k + lax.rem(pb + half, RING), k + lax.rem(pb + 3 - half, RING))

    def before_1():
        arrive(*g0.on)

    def before_2():
        s0.begin()
        g1.pass_on()
        s0.step(0)
        arrive(*g1.second)

    def before_3():
        s0.step(1)
        arrive(*g1.on)

    staged(4, {1: before_1, 2: before_2, 3: before_3}, unit)
    s1.begin()
    s0.step(2)

    def chunk_step(h):
        each_step(lambda v: grad_step(h, 0, v))
        pl.when(h == 1)(d01.relay_b)
        each_step(lambda n: product_step(h, 0, n), lambda v: grad_step(h, 1, v))

        @pl.when(h == 0)
        def _():
            d00.send(0, 1)
            d01.send(0, 1)
            d00.send(2)
            d01.send(2)
            s1.step(0)

        @pl.when(h == 1)
        def _():
            d10.send(0, 1)
            d11.send(0, 1)
            d10.send(2)
            d11.send(2)
            d00.end_b()

        each_step(lambda n: product_step(h, 1, n))

    def before_chunk_1():
        d00.send(3)
        d01.send(3)
        s1.step(1)
        d00.relay_b()
        s1.step(2)

    staged(H, {1: before_chunk_1}, chunk_step)
    d10.send(3)
    d11.send(3)
    own_stats()

    def weight_sent(n, *then):
        def action():
            start(weight_copies[n])
            for step in then:
                step()

        return action

    def weight_came(n, *then):
        def action():
            arrive(weight_copies[n])
            for step in then:
                step()

        return action

    staged(4, {1: weight_sent(0, d01.end_b), 2: weight_sent(1, d10.relay_b), 3: weight_sent(2)}, weight_other)
    start(weight_copies[3])
    d11.relay_b()

    def before_own_1():
        d00.end_a()
        z0.send(0)
        d10.end_b()

    def before_own_2():
        d01.end_a()
        z0.send(1)

    staged(4, {0: weight_came(0), 1: weight_came(1, before_own_1), 2: weight_came(2, before_own_2),
               3: weight_came(3, d11.end_b)}, weight_own)
    d10.end_a()
    z1.send(0)
    z0.end()
    own_stats_store()
    d11.end_a()
    z1.send(1)
    last = [z1.sibling] + [copy for both in z1.others for copy in both]
    for copy in copies:
        if not any(copy is other for other in last):
            copy.wait_send()
    z1.end()
    for copy in last:
        copy.wait_send()


def call(hid, w, ids, adv):
    vmem = pl.BlockSpec(memory_space=pltpu.VMEM)
    anywhere = pl.BlockSpec(memory_space=pl.ANY)
    scratch = [
        pltpu.VMEM((NB, 2, RING, R, D), BF16),
        pltpu.VMEM((V, D), BF16),
        pltpu.VMEM((NB, V, BLK), F32),
        pltpu.VMEM((NB, V, BLK), BF16),
        pltpu.VMEM((2, 2 * BLK, V), BF16),
        pltpu.VMEM((H, 2, 4, HALF, DC), F32),
        pltpu.VMEM((H, 2, 6, HALF, DC), BF16),
        pltpu.VMEM((H, 2, 6, HALF, DC), BF16),
        pltpu.VMEM((H, 2, 2, HALF, DC), F32),
        pltpu.VMEM((H, 2, RING - 1, 2, R, DC), BF16),
        pltpu.VMEM((H, 2, RING - 1, 2, R, DC), BF16),
        pltpu.VMEM((H, NZ, 2, 2, R, 128), F32),
        pltpu.VMEM((H, 2, NZ, 2, R, 128), F32),
        pltpu.VMEM((NB, 4, BLK), F32),
        pltpu.VMEM((H, RING - 1, RING, 4, BLK), F32),
        pltpu.VMEM((H, RING - 1, RING, 4, BLK), F32),
        pltpu.VMEM((H, NZ - 1, RING, 4, BLK), F32),
        pltpu.VMEM((3, NB, 4, BLK), F32),
        pltpu.VMEM((16, 128), jnp.int32),
        pltpu.VMEM((16, 128), F32),
        pltpu.VMEM((16, 128), F32),
        pltpu.VMEM((NB, 1, BLK), jnp.int32),
        pltpu.VMEM((NB, 1, BLK), F32),
        pltpu.VMEM((2, 2, 8, 128), F32),
        pltpu.VMEM((D // NC, ROWS, NC), F32),
        pltpu.VMEM((D // NC, ROWS, NC), F32),
        pltpu.SemaphoreType.DMA((NSEM,)),
        pltpu.SemaphoreType.DMA((NSEM,)),
        pltpu.SemaphoreType.DMA((H, NZ, 2)),
        pltpu.SemaphoreType.DMA((3 + H,)),
    ]
    return pl.pallas_call(
        kernel,
        out_shape=(
            pltpu.VMEM((ROWS, D), F32),
            pltpu.VMEM((2, H, 2, R, 128), F32),
            pltpu.VMEM((1, SHARD), F32),
            pltpu.VMEM((1, SHARD), F32),
        ),
        in_specs=[anywhere] * 4,
        out_specs=(vmem, vmem, vmem, vmem),
        scratch_shapes=scratch,
        compiler_params=pltpu.CompilerParams(
            collective_id=0, has_side_effects=True, vmem_limit_bytes=50 * 2**20),
    )(hid, w, ids, adv)


def store_kernel(*refs):
    count = len(refs) // 2
    moves = [pltpu.make_async_copy(refs[i], refs[count + i], refs[-1].at[i]) for i in range(count)]
    for move in moves:
        move.start()
    for move in moves:
        move.wait()


def store(*arrays):
    return pl.pallas_call(
        store_kernel,
        out_shape=[jax.ShapeDtypeStruct(a.shape, a.dtype) for a in arrays],
        in_specs=[pl.BlockSpec(memory_space=pltpu.VMEM)] * len(arrays),
        out_specs=[pl.BlockSpec(memory_space=pl.ANY)] * len(arrays),
        scratch_shapes=[pltpu.SemaphoreType.DMA((len(arrays),))],
        compiler_params=pltpu.CompilerParams(vmem_limit_bytes=4 * 2**20),
    )(*arrays)


def shards(hidden, head_weight, sampled_ids, advantage):
    hid = hidden.reshape(2, H, 2, R, D)
    grad_weight, grad_hidden, log_prob, entropy = store(*call(
        hid, head_weight, sampled_ids.reshape(16, 128), advantage.reshape(16, 128)))
    return (log_prob.reshape(SHARD), entropy.reshape(SHARD), grad_hidden.reshape(SHARD, 128), grad_weight)


def solution(mesh):
    placed = (P("dp", None), P(("dp", "vocab"), None), P(), P())
    return jax.shard_map(
        shards,
        mesh=mesh,
        in_specs=placed,
        out_specs=(P("dp"), P("dp"), P("dp", "vocab"), P(("dp", "vocab"), None)),
        check_vma=False,
    )
```

```python
import jax
import jax.numpy as jnp
from jax import lax
from jax.experimental import pallas as pl
from jax.experimental.pallas import tpu as pltpu
from jax.sharding import PartitionSpec as P

ENTROPY_COEF = 0.25
MESH = pl.DeviceIdType.MESH
F32, BF16 = jnp.float32, jnp.bfloat16

D = 2048
V = 1024
ROWS = 512
SHARD = 128
RING = 4
NZ = 8
H = 2
R = 16
BLK = 2 * RING * R
HALF = RING * R
NB = RING * H
VC = 256
NC = 512
DC = D // 2
NSEM = 144


def kernel(hid, w, ids, adv, gw_out, gh_out, lp_out, en_out,
           hall, wall, logits, grad, grad_t, pm, x1, y1, yz, r1, x2, y2, zs, zr, st, sx, sy, sz, fin,
           ids_in, adv_in, rolled, ids_row, adv_row, stat_swap, gw_send, gw_recv, send_sem, recv_sem, z_sem, pass_sem, local_sem):
    dp, vo = lax.axis_index("dp"), lax.axis_index("vocab")
    x, y = lax.div(dp, RING), lax.rem(dp, RING)
    z, core = lax.div(vo, 2), lax.rem(vo, 2)
    pa, pb = x + core * (y - x), y + core * (x - y)
    a_p, a_2, a_m = (lax.rem(pa + k, RING) for k in (1, 2, 3))
    b_p, b_2, b_m = (lax.rem(pb + k, RING) for k in (1, 2, 3))

    def place(a, b):
        first, second = a * RING + b, b * RING + a
        return first + core * (second - first)

    def dev(a, b):
        return {"dp": place(a, b), "vocab": vo}

    def zdev(k):
        return {"dp": dp, "vocab": lax.rem(z + k, NZ) * 2 + core}

    sibling = {"dp": dp, "vocab": vo + 1 - 2 * core}

    copies = []

    def remote(src, dst, device, arrival=None):
        i = len(copies)
        copies.append(pltpu.make_async_remote_copy(
            src_ref=src, dst_ref=dst, send_sem=send_sem.at[i], recv_sem=recv_sem.at[i] if arrival is None else arrival,
            device_id=device, device_id_type=MESH))
        return copies[-1]

    def start(*some):
        for copy in some:
            copy.start()

    def arrive(*some):
        for copy in some:
            copy.wait_recv()

    w_rows = pl.ds(pl.multiple_of(core * ROWS, ROWS), ROWS)
    w_in = pltpu.make_async_copy(w, wall.at[w_rows], local_sem.at[0])
    small_in = [pltpu.make_async_copy(ids, ids_in, local_sem.at[1]),
                pltpu.make_async_copy(adv, adv_in, local_sem.at[2])]
    own_in = [pltpu.make_async_copy(hid.at[core, h], hall.at[h * RING + pb, :, pa], local_sem.at[3 + h])
              for h in range(H)]
    for c in [w_in] + small_in + own_in:
        c.start()

    a_dev = [dev(lax.rem(pa + k, RING), pb) for k in (1, 2, 3)]
    b_dev = [dev(pa, lax.rem(pb + k, RING)) for k in (1, 2, 3)]
    z_dev = [zdev(k) for k in range(1, NZ)]
    ap, _, am = a_dev
    bp, _, bm = b_dev
    barrier = pltpu.get_barrier_semaphore()
    z_both = [[dict(dp=dp, vocab=lax.rem(z + k, NZ) * 2 + f) for f in range(2)] for k in range(1, NZ)]
    peers = a_dev + b_dev + [d for both in z_both for d in both] + [sibling]
    for peer in peers:
        pl.semaphore_signal(barrier, inc=1, device_id=peer, device_id_type=MESH)

    w_swap = remote(wall.at[w_rows], wall.at[w_rows], sibling)

    class Gather:
        def __init__(self, h):
            kp, km, k0 = (h * RING + b for b in (b_p, b_m, pb))
            own, there = hid.at[core, h], hall.at[k0, :, pa]
            self.near = [remote(own, there, d) for d in (ap, am)]
            self.far = [remote(hall.at[k0, 0, a_m], hall.at[k0, 0, a_m], ap),
                        remote(hall.at[k0, 1, a_p], hall.at[k0, 1, a_p], am)]
            halves = [hall.at[k0, s] for s in range(2)]
            self.first = [remote(halves[0], halves[0], bp), remote(halves[1], halves[1], bm)]
            self.second = [remote(halves[1], halves[1], bp), remote(halves[0], halves[0], bm)]
            self.on = [remote(hall.at[km, 0], hall.at[km, 0], bp), remote(hall.at[kp, 1], hall.at[kp, 1], bm)]

        def ring(self):
            for near, far in zip(self.near, self.far):
                arrive(near)
                start(far)

        def spread(self):
            arrive(*self.far)
            start(*self.first, *self.second)

        def pass_on(self):
            for first, on in zip(self.first, self.on):
                arrive(first)
                start(on)

    g0, g1 = Gather(0), Gather(1)

    lane = lax.broadcasted_iota(jnp.int32, (8, 128), 1)

    def lanes_of(group):
        return lax.div(lane, R) == group

    def reorder(source, out):
        both = source[...].astype(F32)
        rolled[...] = jnp.where(core == 0, both, pltpu.roll(both, 64, 1))
        for b in range(RING):
            rows = [jnp.broadcast_to(rolled[pl.ds(place(a, b), 1), :], (8, 128)) for a in range(RING)]
            for h in range(H):
                line = jnp.zeros((8, 128), F32)
                for a in range(RING):
                    for s in range(2):
                        group = s * RING + a
                        shift = (group * R - h * 2 * R - s * R) % 128
                        line = jnp.where(lanes_of(group), pltpu.roll(rows[a], shift, 1), line)
                out[h * RING + b] = line[0:1].astype(out.dtype)

    first_row = dp * (2 * ROWS * NZ) + z * (2 * ROWS)

    def stats_blocks(k_one, k_two):
        token_ids = jnp.concatenate([ids_row[k_one], ids_row[k_two]], axis=1) - first_row

        def product(v):
            tokens = jnp.concatenate([hall[k_one].reshape(BLK, D), hall[k_two].reshape(BLK, D)], axis=0)
            part = lax.dot_general(wall[v * VC:(v + 1) * VC, :], tokens, (((1,), (1,)), ((), ())),
                                   preferred_element_type=F32)
            logits[k_one, v * VC:(v + 1) * VC, :] = part[:, :BLK]
            logits[k_two, v * VC:(v + 1) * VC, :] = part[:, BLK:]

        def add_sums(v, peak, sums):
            rows = slice(v * VC, (v + 1) * VC)
            part = jnp.concatenate([logits[k_one, rows, :], logits[k_two, rows, :]], axis=1)
            above = jnp.max(part, axis=0, keepdims=True)
            new_peak = above if peak is None else jnp.maximum(peak, above)
            expon = jnp.exp(part - new_peak)
            row = lax.broadcasted_iota(jnp.int32, part.shape, 0)
            picked = jnp.where(row == token_ids - v * VC, part, 0.0)
            more = [jnp.sum(p, axis=0, keepdims=True) for p in (expon, expon * part, picked)]
            if peak is not None:
                scale = jnp.exp(peak - new_peak)
                more = [m + s * f for m, s, f in zip(more, sums, (scale, scale, 1.0))]
            return new_peak, more

        peak, sums = None, None
        product(0)
        for v in range(1, V // VC):
            product(v)
            peak, sums = add_sums(v - 1, peak, sums)
        peak, sums = add_sums(V // VC - 1, peak, sums)
        for q, row in enumerate([peak] + sums):
            st[k_one, pl.ds(q, 1), :] = row[:, :BLK]
            st[k_two, pl.ds(q, 1), :] = row[:, BLK:]

    def stats_merge(ref, slots, sent):
        arrive(*sent)
        parts = [ref[...]] + [slots[i] for i in range(len(sent))]
        peak = parts[0][:, 0:1, :]
        for p in parts[1:]:
            peak = jnp.maximum(peak, p[:, 0:1, :])
        total, weighted, target = 0.0, 0.0, 0.0
        for p in parts:
            scale = jnp.exp(p[:, 0:1, :] - peak)
            total += scale * p[:, 1:2, :]
            weighted += scale * p[:, 2:3, :]
            target += p[:, 3:4, :]
        return peak, total, weighted, target

    class Stats:
        def __init__(self, h):
            blocks = pl.ds(h * RING, RING)
            self.steps = [(st.at[blocks], sz.at[h], fin.at[0, blocks], z_dev),
                          (fin.at[0, blocks], sx.at[h], fin.at[1, blocks], a_dev),
                          (fin.at[1, blocks], sy.at[h], fin.at[2, blocks], b_dev)]
            self.sent = [[remote(ref, slots.at[i], d) for i, d in enumerate(devices)]
                         for ref, slots, _, devices in self.steps]

        def begin(self):
            start(*self.sent[0])

        def step(self, i):
            ref, slots, out, _ = self.steps[i]
            rows = stats_merge(ref, slots, self.sent[i])
            if i == 2:
                peak, total, weighted, target = rows
                rows = (peak + jnp.log(total), weighted / total, target)
            for q, row in enumerate(rows):
                out[:, pl.ds(q, 1), :] = row
            if i < 2:
                start(*self.sent[i + 1])

    s0, s1 = Stats(0), Stats(1)

    order = (b_2, b_m, b_p, pb)
    STEPS = D // NC
    GR = V // STEPS

    def grad_step(h, pair, v):
        ks = [h * RING + b for b in order[2 * pair:2 * pair + 2]]
        token_ids = jnp.concatenate([ids_row[k] for k in ks], axis=1) - first_row
        advantage = jnp.concatenate([adv_row[k] for k in ks], axis=1)
        log_total = jnp.concatenate([fin[2, k, 0:1, :] for k in ks], axis=1)
        mean = jnp.concatenate([fin[2, k, 1:2, :] for k in ks], axis=1)
        level = advantage - ENTROPY_COEF * mean
        start_row = pl.multiple_of(v * GR, GR)
        rows = pl.ds(start_row, GR)
        part = jnp.concatenate([logits[k, rows, :] for k in ks], axis=1)
        prob = jnp.exp(part - log_total)
        row = lax.broadcasted_iota(jnp.int32, part.shape, 0)
        chosen = jnp.where(row == token_ids - start_row, advantage, 0.0)
        low = (chosen - prob * (level + ENTROPY_COEF * part)).astype(BF16)
        for j, k in enumerate(ks):
            tile = low[:, j * BLK:(j + 1) * BLK]
            grad[k, rows, :] = tile
            grad_t[pair, j * BLK:(j + 1) * BLK, rows] = tile.T

    def product_step(h, pair, n):
        c, m = lax.div(n, STEPS // 2), lax.rem(n, STEPS // 2)
        cols = pl.ds(pl.multiple_of(m * NC, NC), NC)
        part = jnp.dot(grad_t[pair], wall[:, pl.ds(pl.multiple_of(n * NC, NC), NC)], preferred_element_type=F32)
        one_0, one_1, two_0, two_1 = (part[i * HALF:(i + 1) * HALF] for i in range(4))
        if pair == 0:
            x1[h, c, 0, :, cols] = one_0.astype(BF16)
            x1[h, c, 2, :, cols] = one_1.astype(BF16)
            pm[h, c, 0, :, cols] = two_0
            x1[h, c, 4, :, cols] = two_0.astype(BF16)
            x1[h, c, 1, :, cols] = two_1.astype(BF16)
        else:
            x1[h, c, 3, :, cols] = one_0.astype(BF16)
            pm[h, c, 1, :, cols] = one_1
            x1[h, c, 5, :, cols] = one_1.astype(BF16)
            pm[h, c, 2, :, cols] = two_0
            pm[h, c, 3, :, cols] = two_1

    def each_step(*bodies):
        def step(n, carry):
            for body in bodies:
                body(n)
            return carry

        lax.fori_loop(0, STEPS, step, 0)

    def chunked(rows, body):
        def step(n, carry):
            body(pl.ds(pl.multiple_of(n * 32, 32), 32))
            return carry

        lax.fori_loop(0, rows // 32, step, 0)

    def slot(a):
        return pl.ds(pl.multiple_of(a * R, R), R)

    class Reduce:
        def __init__(self, h, c):
            self.at = h, c
            self.direct = [remote(x1.at[h, c, i], y1.at[h, c, i], d) for i, d in ((1, bm), (3, bp))]
            self.passed = [pltpu.make_async_remote_copy(
                src_ref=x1.at[h, c, 4 + i], dst_ref=y1.at[h, c, 4 + i], send_sem=send_sem.at[0],
                recv_sem=pass_sem.at[h, c, i], device_id=d, device_id_type=MESH) for i, d in enumerate((bm, bp))]
            self.a = [remote(x2.at[h, c, i], y2.at[h, c, i], d) for i, d in enumerate(a_dev)]

        def end_b(self):
            h, c = self.at
            arrive(*self.direct, *self.passed)
            for s, (one, two) in enumerate(((3, 4), (1, 5))):

                def total(rows):
                    r1[h, c, s, rows, :] = (pm[h, c, 2 + s, rows, :] + y1[h, c, one, rows, :].astype(F32)
                                            + y1[h, c, two, rows, :].astype(F32))

                chunked(HALF, total)
            for i in (1, 0, 2):
                for s in range(2):
                    x2[h, c, i, s] = r1[h, c, s, slot((a_p, a_2, a_m)[i]), :].astype(BF16)
                start(self.a[i])

        def end_a(self):
            h, c = self.at
            arrive(*self.a)
            for s in range(2):
                for f in range(DC // 128):
                    cols = slice(f * 128, f * 128 + 128)
                    zs[h, c * (NZ // 2) + f // 2, f % 2, s] = r1[h, c, s, slot(pa), cols] + sum(
                        y2[h, c, i, s, :, cols].astype(F32) for i in range(RING - 1))

    class Reduce_z:
        def __init__(self, h):
            self.h = h
            self.sibling = remote(zs.at[h, z, 1 - core], zr.at[h, core, 0], sibling, z_sem.at[h, 0, core])
            self.others = [[remote(zs.at[h, lax.rem(z + k, NZ), f], zr.at[h, core, k], z_both[k - 1][f],
                                   z_sem.at[h, k, core]) for f in range(2)] for k in range(1, NZ)]
            places = [(1 - core, 0)] + [(c, k) for k in range(1, NZ) for c in range(2)]
            self.arrivals = [pltpu.make_async_remote_copy(
                src_ref=zr.at[h, c, k], dst_ref=zr.at[h, c, k], send_sem=send_sem.at[0], recv_sem=z_sem.at[h, k, c],
                device_id=sibling, device_id_type=MESH) for c, k in places]

        def send(self, c):
            @pl.when(lax.div(z, NZ // 2) == c)
            def _():
                zr[self.h, core, 0] = zs[self.h, z, core]
                start(self.sibling)

            for k in range(1, NZ):

                @pl.when(lax.div(lax.rem(z + k, NZ), NZ // 2) == c)
                def _():
                    start(*self.others[k - 1])

        def end(self):
            h = self.h
            arrive(*self.arrivals)
            for c in range(2):
                total = zr[h, c, 0]
                for k in range(1, NZ):
                    total += zr[h, c, k]
                gh_out[c, h] = total

    kept = lax.rem(z, 2)

    class Far:
        def __init__(self, h):
            self.h = h
            self.swap = [remote(x1.at[h, 1 - kept, 0], yz.at[h, 0], zdev(1)),
                         remote(x1.at[h, 1 - kept, 2], yz.at[h, 1], zdev(NZ - 1))]
            self.far = [remote(x1.at[h, kept, 2 * i], y1.at[h, kept, 2 * i], d) for i, d in enumerate((bm, bp))]
            self.own, self.relayed = ([remote(x1.at[h, half, 4 + i], y1.at[h, half, 4 + i], d, pass_sem.at[h, half, i])
                                       for i, d in enumerate((bm, bp))] for half in (1 - kept, kept))

        def send(self):
            h = self.h
            for i in range(2):
                arrive(self.swap[i])

                def add(rows):
                    x1[h, kept, 2 * i, rows, :] = (
                        x1[h, kept, 2 * i, rows, :].astype(F32) + yz[h, i, rows, :].astype(F32)).astype(BF16)

                chunked(HALF, add)
                start(self.far[i])

        def relay(self):
            h = self.h
            for i in range(2):
                arrive(self.far[i])

                def add(rows):
                    x1[h, kept, 4 + i, rows, :] = (
                        pm[h, kept, i, rows, :] + y1[h, kept, 2 * i, rows, :].astype(F32)).astype(BF16)

                chunked(HALF, add)
                start(self.relayed[i])

    f0, f1 = Far(0), Far(1)
    d00, d01, d10, d11 = (Reduce(h, c) for h in range(H) for c in range(2))
    z0, z1 = Reduce_z(0), Reduce_z(1)

    weight_copies = [remote(gw_send.at[n], gw_recv.at[n], sibling) for n in range(D // NC)]

    def weight_part(side, n):
        rows = pl.ds(pl.multiple_of(side * ROWS, ROWS), ROWS)
        cols = pl.ds(pl.multiple_of(n * NC, NC), NC)
        lhs = jnp.concatenate([grad[k, rows, :] for k in range(NB)], axis=1)
        rhs = hall[:, :, :, :, cols].reshape(NB * BLK, NC)
        return jnp.dot(lhs, rhs, preferred_element_type=F32), cols

    def weight_other(n):
        gw_send[n] = weight_part(1 - core, n)[0]

    def weight_own(n):
        part, cols = weight_part(core, n)
        gw_out[:, cols] = part + gw_recv[n]

    stat_copy = remote(stat_swap.at[0], stat_swap.at[1], sibling)

    def own_stats():
        for q in range(2):
            line = jnp.zeros((8, 128), F32)
            for h in range(H):
                k = h * RING + pb
                log_total, mean, target = (fin[2, k, pl.ds(i, 1), :] for i in range(3))
                row = jnp.broadcast_to(target - log_total if q == 0 else log_total - mean, (8, 128))
                for s in range(2):
                    group = (h * 2 + s) + core * 4
                    shift = lax.rem(group * R + 256 - (s * RING + pa) * R, 128)
                    line = jnp.where(lanes_of(group), pltpu.roll(row, shift, 1), line)
            stat_swap[0, q] = line
        start(stat_copy)

    def own_stats_store():
        arrive(stat_copy)
        mine = lax.div(lane, 64) == core
        for q, out in enumerate((lp_out, en_out)):
            out[...] = jnp.where(mine, stat_swap[0, q], stat_swap[1, q])[0:1]

    def staged(count, before, body):
        def step(i, carry):
            for j, action in before.items():
                pl.when(i == j)(action)
            body(i)
            return carry

        lax.fori_loop(0, count, step, 0)

    for c in small_in:
        c.wait()
    reorder(ids_in, ids_row)
    reorder(adv_in, adv_row)
    pl.semaphore_wait(barrier, len(peers))
    start(*g0.near, *g1.near)
    for c in [w_in] + own_in:
        c.wait()
    start(w_swap)
    g0.ring()
    g1.ring()
    g0.spread()
    g0.pass_on()
    g1.spread()
    arrive(w_swap, *g0.second)

    def unit(i):
        half = lax.rem(i, 2)
        k = lax.div(i, 2) * RING
        stats_blocks(k + lax.rem(pb + half, RING), k + lax.rem(pb + 3 - half, RING))

    def before_1():
        arrive(*g0.on)

    def before_2():
        s0.begin()
        g1.pass_on()
        s0.step(0)
        arrive(*g1.second)

    def before_3():
        s0.step(1)
        arrive(*g1.on)

    staged(4, {1: before_1, 2: before_2, 3: before_3}, unit)
    s1.begin()
    s0.step(2)

    def chunk_step(h):
        each_step(lambda v: grad_step(h, 0, v))
        pl.when(h == 1)(f0.relay)
        each_step(lambda n: product_step(h, 0, n), lambda v: grad_step(h, 1, v))

        @pl.when(h == 0)
        def _():
            start(*f0.swap, d00.direct[0], d01.direct[0], f0.own[0])
            s1.step(0)

        @pl.when(h == 1)
        def _():
            start(*f1.swap, d10.direct[0], d11.direct[0], f1.own[0])

        each_step(lambda n: product_step(h, 1, n))

    def before_chunk_1():
        start(d00.direct[1], d01.direct[1], f0.own[1])
        f0.send()
        s1.step(1)
        s1.step(2)

    staged(H, {1: before_chunk_1}, chunk_step)
    start(d10.direct[1], d11.direct[1], f1.own[1])
    f1.send()
    d00.end_b()
    own_stats()

    def weight_sent(n, *then):
        def action():
            start(weight_copies[n])
            for step in then:
                step()

        return action

    def weight_came(n, *then):
        def action():
            arrive(weight_copies[n])
            for step in then:
                step()

        return action

    staged(4, {1: weight_sent(0, d01.end_b), 2: weight_sent(1, f1.relay), 3: weight_sent(2)}, weight_other)
    start(weight_copies[3])

    def before_own_1():
        d00.end_a()
        z0.send(0)
        d10.end_b()

    def before_own_2():
        d01.end_a()
        z0.send(1)

    staged(4, {0: weight_came(0), 1: weight_came(1, before_own_1), 2: weight_came(2, before_own_2),
               3: weight_came(3, d11.end_b)}, weight_own)
    d10.end_a()
    z1.send(0)
    z0.end()
    own_stats_store()
    d11.end_a()
    z1.send(1)
    last = [z1.sibling] + [copy for both in z1.others for copy in both]
    for copy in copies:
        if not any(copy is other for other in last):
            copy.wait_send()
    z1.end()
    for copy in last:
        copy.wait_send()


def call(hid, w, ids, adv):
    vmem = pl.BlockSpec(memory_space=pltpu.VMEM)
    anywhere = pl.BlockSpec(memory_space=pl.ANY)
    scratch = [
        pltpu.VMEM((NB, 2, RING, R, D), BF16),
        pltpu.VMEM((V, D), BF16),
        pltpu.VMEM((NB, V, BLK), F32),
        pltpu.VMEM((NB, V, BLK), BF16),
        pltpu.VMEM((2, 2 * BLK, V), BF16),
        pltpu.VMEM((H, 2, 4, HALF, DC), F32),
        pltpu.VMEM((H, 2, 6, HALF, DC), BF16),
        pltpu.VMEM((H, 2, 6, HALF, DC), BF16),
        pltpu.VMEM((H, 2, HALF, DC), BF16),
        pltpu.VMEM((H, 2, 2, HALF, DC), F32),
        pltpu.VMEM((H, 2, RING - 1, 2, R, DC), BF16),
        pltpu.VMEM((H, 2, RING - 1, 2, R, DC), BF16),
        pltpu.VMEM((H, NZ, 2, 2, R, 128), F32),
        pltpu.VMEM((H, 2, NZ, 2, R, 128), F32),
        pltpu.VMEM((NB, 4, BLK), F32),
        pltpu.VMEM((H, RING - 1, RING, 4, BLK), F32),
        pltpu.VMEM((H, RING - 1, RING, 4, BLK), F32),
        pltpu.VMEM((H, NZ - 1, RING, 4, BLK), F32),
        pltpu.VMEM((3, NB, 4, BLK), F32),
        pltpu.VMEM((16, 128), jnp.int32),
        pltpu.VMEM((16, 128), F32),
        pltpu.VMEM((16, 128), F32),
        pltpu.VMEM((NB, 1, BLK), jnp.int32),
        pltpu.VMEM((NB, 1, BLK), F32),
        pltpu.VMEM((2, 2, 8, 128), F32),
        pltpu.VMEM((D // NC, ROWS, NC), F32),
        pltpu.VMEM((D // NC, ROWS, NC), F32),
        pltpu.SemaphoreType.DMA((NSEM,)),
        pltpu.SemaphoreType.DMA((NSEM,)),
        pltpu.SemaphoreType.DMA((H, NZ, 2)),
        pltpu.SemaphoreType.DMA((H, 2, 2)),
        pltpu.SemaphoreType.DMA((3 + H,)),
    ]
    return pl.pallas_call(
        kernel,
        out_shape=(
            pltpu.VMEM((ROWS, D), F32),
            pltpu.VMEM((2, H, 2, R, 128), F32),
            pltpu.VMEM((1, SHARD), F32),
            pltpu.VMEM((1, SHARD), F32),
        ),
        in_specs=[anywhere] * 4,
        out_specs=(vmem, vmem, vmem, vmem),
        scratch_shapes=scratch,
        compiler_params=pltpu.CompilerParams(
            collective_id=0, has_side_effects=True, vmem_limit_bytes=50 * 2**20),
    )(hid, w, ids, adv)


def store_kernel(*refs):
    count = len(refs) // 2
    moves = [pltpu.make_async_copy(refs[i], refs[count + i], refs[-1].at[i]) for i in range(count)]
    for move in moves:
        move.start()
    for move in moves:
        move.wait()


def store(*arrays):
    return pl.pallas_call(
        store_kernel,
        out_shape=[jax.ShapeDtypeStruct(a.shape, a.dtype) for a in arrays],
        in_specs=[pl.BlockSpec(memory_space=pltpu.VMEM)] * len(arrays),
        out_specs=[pl.BlockSpec(memory_space=pl.ANY)] * len(arrays),
        scratch_shapes=[pltpu.SemaphoreType.DMA((len(arrays),))],
        compiler_params=pltpu.CompilerParams(vmem_limit_bytes=4 * 2**20),
    )(*arrays)


def shards(hidden, head_weight, sampled_ids, advantage):
    hid = hidden.reshape(2, H, 2, R, D)
    grad_weight, grad_hidden, log_prob, entropy = store(*call(
        hid, head_weight, sampled_ids.reshape(16, 128), advantage.reshape(16, 128)))
    return (log_prob.reshape(SHARD), entropy.reshape(SHARD), grad_hidden.reshape(SHARD, 128), grad_weight)


def solution(mesh):
    placed = (P("dp", None), P(("dp", "vocab"), None), P(), P())
    return jax.shard_map(
        shards,
        mesh=mesh,
        in_specs=placed,
        out_specs=(P("dp"), P("dp"), P("dp", "vocab"), P(("dp", "vocab"), None)),
        check_vma=False,
    )
```

```python
import jax
import jax.numpy as jnp
from jax import lax
from jax.experimental import pallas as pl
from jax.experimental.pallas import tpu as pltpu
from jax.sharding import PartitionSpec as P

ENTROPY_COEF = 0.25
MESH = pl.DeviceIdType.MESH
F32, BF16 = jnp.float32, jnp.bfloat16

D = 2048
V = 1024
ROWS = 512
SHARD = 128
RING = 4
NZ = 8
H = 2
R = 16
BLK = 2 * RING * R
HALF = RING * R
NB = RING * H
VC = 256
NC = 512
DC = D // 2
NSEM = 144


def kernel(hid, w, ids, adv, gw_out, gh_out, lp_out, en_out,
           hall, wall, logits, grad, grad_t, pm, x1, y1, r1, x2, y2, zs, zr, st, sx, sz, fin,
           ids_in, adv_in, rolled, ids_row, adv_row, stat_swap, gw_send, gw_recv, send_sem, recv_sem, z_sem, local_sem):
    dp, vo = lax.axis_index("dp"), lax.axis_index("vocab")
    x, y = lax.div(dp, RING), lax.rem(dp, RING)
    z, core = lax.div(vo, 2), lax.rem(vo, 2)
    pa, pb = x + core * (y - x), y + core * (x - y)
    a_p, a_2, a_m = (lax.rem(pa + k, RING) for k in (1, 2, 3))
    b_p, b_2, b_m = (lax.rem(pb + k, RING) for k in (1, 2, 3))

    def place(a, b):
        first, second = a * RING + b, b * RING + a
        return first + core * (second - first)

    def dev(a, b):
        return {"dp": place(a, b), "vocab": vo}

    def zdev(k):
        return {"dp": dp, "vocab": lax.rem(z + k, NZ) * 2 + core}

    sibling = {"dp": dp, "vocab": vo + 1 - 2 * core}

    copies = []

    def remote(src, dst, device, arrival=None):
        i = len(copies)
        copies.append(pltpu.make_async_remote_copy(
            src_ref=src, dst_ref=dst, send_sem=send_sem.at[i], recv_sem=recv_sem.at[i] if arrival is None else arrival,
            device_id=device, device_id_type=MESH))
        return copies[-1]

    def start(*some):
        for copy in some:
            copy.start()

    def arrive(*some):
        for copy in some:
            copy.wait_recv()

    w_rows = pl.ds(pl.multiple_of(core * ROWS, ROWS), ROWS)
    w_in = pltpu.make_async_copy(w, wall.at[w_rows], local_sem.at[0])
    small_in = [pltpu.make_async_copy(ids, ids_in, local_sem.at[1]),
                pltpu.make_async_copy(adv, adv_in, local_sem.at[2])]
    own_in = [pltpu.make_async_copy(hid.at[core, h], hall.at[h * RING + pb, :, pa], local_sem.at[3 + h])
              for h in range(H)]
    for c in [w_in] + small_in + own_in:
        c.start()

    a_dev = [dev(lax.rem(pa + k, RING), pb) for k in (1, 2, 3)]
    b_dev = [dev(pa, lax.rem(pb + k, RING)) for k in (1, 2, 3)]
    z_dev = [zdev(k) for k in range(1, NZ)]
    ap, _, am = a_dev
    bp, _, bm = b_dev
    barrier = pltpu.get_barrier_semaphore()
    z_both = [[dict(dp=dp, vocab=lax.rem(z + k, NZ) * 2 + f) for f in range(2)] for k in range(1, NZ)]
    xy_dev = [dev(lax.rem(pa + i, RING), lax.rem(pb + j, RING)) for i in range(RING) for j in range(RING) if i or j]
    peers = xy_dev + [d for both in z_both for d in both] + [sibling]
    for peer in peers:
        pl.semaphore_signal(barrier, inc=1, device_id=peer, device_id_type=MESH)

    w_swap = remote(wall.at[w_rows], wall.at[w_rows], sibling)

    class Gather:
        def __init__(self, h):
            kp, km, k0 = (h * RING + b for b in (b_p, b_m, pb))
            own, there = hid.at[core, h], hall.at[k0, :, pa]
            self.ring = [remote(own, there, d) for d in (ap, am, a_dev[1])]
            halves = [hall.at[k0, s] for s in range(2)]
            self.first = [remote(halves[0], halves[0], bp), remote(halves[1], halves[1], bm)]
            self.second = [remote(halves[1], halves[1], bp), remote(halves[0], halves[0], bm)]
            self.on = [remote(hall.at[km, 0], hall.at[km, 0], bp), remote(hall.at[kp, 1], hall.at[kp, 1], bm)]

        def spread(self):
            arrive(*self.ring)
            start(*self.first, *self.second)

        def pass_on(self):
            for first, on in zip(self.first, self.on):
                arrive(first)
                start(on)

    g0, g1 = Gather(0), Gather(1)

    lane = lax.broadcasted_iota(jnp.int32, (8, 128), 1)

    def lanes_of(group):
        return lax.div(lane, R) == group

    def reorder(source, out):
        both = source[...].astype(F32)
        rolled[...] = jnp.where(core == 0, both, pltpu.roll(both, 64, 1))
        for b in range(RING):
            rows = [jnp.broadcast_to(rolled[pl.ds(place(a, b), 1), :], (8, 128)) for a in range(RING)]
            for h in range(H):
                line = jnp.zeros((8, 128), F32)
                for a in range(RING):
                    for s in range(2):
                        group = s * RING + a
                        shift = (group * R - h * 2 * R - s * R) % 128
                        line = jnp.where(lanes_of(group), pltpu.roll(rows[a], shift, 1), line)
                out[h * RING + b] = line[0:1].astype(out.dtype)

    first_row = dp * (2 * ROWS * NZ) + z * (2 * ROWS)

    def stats_blocks(k_one, k_two):
        token_ids = jnp.concatenate([ids_row[k_one], ids_row[k_two]], axis=1) - first_row

        def product(v):
            tokens = jnp.concatenate([hall[k_one].reshape(BLK, D), hall[k_two].reshape(BLK, D)], axis=0)
            part = lax.dot_general(wall[v * VC:(v + 1) * VC, :], tokens, (((1,), (1,)), ((), ())),
                                   preferred_element_type=F32)
            logits[k_one, v * VC:(v + 1) * VC, :] = part[:, :BLK]
            logits[k_two, v * VC:(v + 1) * VC, :] = part[:, BLK:]

        def add_sums(v, peak, sums):
            rows = slice(v * VC, (v + 1) * VC)
            part = jnp.concatenate([logits[k_one, rows, :], logits[k_two, rows, :]], axis=1)
            above = jnp.max(part, axis=0, keepdims=True)
            new_peak = above if peak is None else jnp.maximum(peak, above)
            expon = jnp.exp(part - new_peak)
            row = lax.broadcasted_iota(jnp.int32, part.shape, 0)
            picked = jnp.where(row == token_ids - v * VC, part, 0.0)
            more = [jnp.sum(p, axis=0, keepdims=True) for p in (expon, expon * part, picked)]
            if peak is not None:
                scale = jnp.exp(peak - new_peak)
                more = [m + s * f for m, s, f in zip(more, sums, (scale, scale, 1.0))]
            return new_peak, more

        peak, sums = None, None
        product(0)
        for v in range(1, V // VC):
            product(v)
            peak, sums = add_sums(v - 1, peak, sums)
        peak, sums = add_sums(V // VC - 1, peak, sums)
        for q, row in enumerate([peak] + sums):
            st[k_one, pl.ds(q, 1), :] = row[:, :BLK]
            st[k_two, pl.ds(q, 1), :] = row[:, BLK:]

    def stats_merge(ref, slots, sent):
        arrive(*sent)
        parts = [ref[...]] + [slots[i] for i in range(len(sent))]
        peak = parts[0][:, 0:1, :]
        for p in parts[1:]:
            peak = jnp.maximum(peak, p[:, 0:1, :])
        total, weighted, target = 0.0, 0.0, 0.0
        for p in parts:
            scale = jnp.exp(p[:, 0:1, :] - peak)
            total += scale * p[:, 1:2, :]
            weighted += scale * p[:, 2:3, :]
            target += p[:, 3:4, :]
        return peak, total, weighted, target

    class Stats:
        def __init__(self, h):
            blocks = pl.ds(h * RING, RING)
            self.steps = [(st.at[blocks], sz.at[h], fin.at[0, blocks], z_dev),
                          (fin.at[0, blocks], sx.at[h], fin.at[2, blocks], xy_dev)]
            self.sent = [[remote(ref, slots.at[i], d) for i, d in enumerate(devices)]
                         for ref, slots, _, devices in self.steps]

        def begin(self):
            start(*self.sent[0])

        def step(self, i):
            ref, slots, out, _ = self.steps[i]
            rows = stats_merge(ref, slots, self.sent[i])
            if i == 1:
                peak, total, weighted, target = rows
                rows = (peak + jnp.log(total), weighted / total, target)
            for q, row in enumerate(rows):
                out[:, pl.ds(q, 1), :] = row
            if i < 1:
                start(*self.sent[i + 1])

    s0, s1 = Stats(0), Stats(1)

    order = (b_2, b_m, b_p, pb)
    STEPS = D // NC
    GR = V // STEPS

    def grad_step(h, pair, v):
        ks = [h * RING + b for b in order[2 * pair:2 * pair + 2]]
        token_ids = jnp.concatenate([ids_row[k] for k in ks], axis=1) - first_row
        advantage = jnp.concatenate([adv_row[k] for k in ks], axis=1)
        log_total = jnp.concatenate([fin[2, k, 0:1, :] for k in ks], axis=1)
        mean = jnp.concatenate([fin[2, k, 1:2, :] for k in ks], axis=1)
        level = advantage - ENTROPY_COEF * mean
        start_row = pl.multiple_of(v * GR, GR)
        rows = pl.ds(start_row, GR)
        part = jnp.concatenate([logits[k, rows, :] for k in ks], axis=1)
        prob = jnp.exp(part - log_total)
        row = lax.broadcasted_iota(jnp.int32, part.shape, 0)
        chosen = jnp.where(row == token_ids - start_row, advantage, 0.0)
        low = (chosen - prob * (level + ENTROPY_COEF * part)).astype(BF16)
        for j, k in enumerate(ks):
            tile = low[:, j * BLK:(j + 1) * BLK]
            grad[k, rows, :] = tile
            grad_t[pair, j * BLK:(j + 1) * BLK, rows] = tile.T

    def product_step(h, pair, n):
        c, m = lax.div(n, STEPS // 2), lax.rem(n, STEPS // 2)
        cols = pl.ds(pl.multiple_of(m * NC, NC), NC)
        part = jnp.dot(grad_t[pair], wall[:, pl.ds(pl.multiple_of(n * NC, NC), NC)], preferred_element_type=F32)
        one_0, one_1, two_0, two_1 = (part[i * HALF:(i + 1) * HALF] for i in range(4))
        if pair == 0:
            x1[h, c, 0, :, cols] = one_0.astype(BF16)
            x1[h, c, 2, :, cols] = one_1.astype(BF16)
            pm[h, c, 0, :, cols] = two_0
            x1[h, c, 1, :, cols] = two_1.astype(BF16)
        else:
            x1[h, c, 3, :, cols] = one_0.astype(BF16)
            pm[h, c, 1, :, cols] = one_1
            pm[h, c, 2, :, cols] = two_0
            pm[h, c, 3, :, cols] = two_1

    def each_step(*bodies):
        def step(n, carry):
            for body in bodies:
                body(n)
            return carry

        lax.fori_loop(0, STEPS, step, 0)

    def chunked(rows, body):
        def step(n, carry):
            body(pl.ds(pl.multiple_of(n * 32, 32), 32))
            return carry

        lax.fori_loop(0, rows // 32, step, 0)

    def slot(a):
        return pl.ds(pl.multiple_of(a * R, R), R)

    class Reduce:
        def __init__(self, h, c):
            self.at = h, c
            self.b = [remote(x1.at[h, c, i], y1.at[h, c, i], d)
                      for i, d in ((0, bm), (2, bp), (1, bm), (3, bp), (4, bm), (5, bp))]
            self.a = [remote(x2.at[h, c, i], y2.at[h, c, i], d) for i, d in enumerate(a_dev)]

        def send(self, *which):
            start(*[self.b[i] for i in which])

        def relay_b(self):
            h, c = self.at
            for i in range(2):
                arrive(self.b[i])

                def relay(rows):
                    x1[h, c, 4 + i, rows, :] = (
                        pm[h, c, i, rows, :] + y1[h, c, 2 * i, rows, :].astype(F32)).astype(BF16)

                chunked(HALF, relay)
                start(self.b[4 + i])

        def end_b(self):
            h, c = self.at
            arrive(*self.b[2:])
            for s, (one, two) in enumerate(((3, 4), (1, 5))):

                def total(rows):
                    r1[h, c, s, rows, :] = (pm[h, c, 2 + s, rows, :] + y1[h, c, one, rows, :].astype(F32)
                                            + y1[h, c, two, rows, :].astype(F32))

                chunked(HALF, total)
            for i in (1, 0, 2):
                for s in range(2):
                    x2[h, c, i, s] = r1[h, c, s, slot((a_p, a_2, a_m)[i]), :].astype(BF16)
                start(self.a[i])

        def end_a(self):
            h, c = self.at
            arrive(*self.a)
            for s in range(2):
                for f in range(DC // 128):
                    cols = slice(f * 128, f * 128 + 128)
                    zs[h, c * (NZ // 2) + f // 2, f % 2, s] = r1[h, c, s, slot(pa), cols] + sum(
                        y2[h, c, i, s, :, cols].astype(F32) for i in range(RING - 1))

    class Reduce_z:
        def __init__(self, h):
            self.h = h
            self.sibling = remote(zs.at[h, z, 1 - core], zr.at[h, core, 0], sibling, z_sem.at[h, 0, core])
            self.others = [[remote(zs.at[h, lax.rem(z + k, NZ), f], zr.at[h, core, k], z_both[k - 1][f],
                                   z_sem.at[h, k, core]) for f in range(2)] for k in range(1, NZ)]
            places = [(1 - core, 0)] + [(c, k) for k in range(1, NZ) for c in range(2)]
            self.arrivals = [pltpu.make_async_remote_copy(
                src_ref=zr.at[h, c, k], dst_ref=zr.at[h, c, k], send_sem=send_sem.at[0], recv_sem=z_sem.at[h, k, c],
                device_id=sibling, device_id_type=MESH) for c, k in places]

        def send(self, c):
            @pl.when(lax.div(z, NZ // 2) == c)
            def _():
                zr[self.h, core, 0] = zs[self.h, z, core]
                start(self.sibling)

            for k in range(1, NZ):

                @pl.when(lax.div(lax.rem(z + k, NZ), NZ // 2) == c)
                def _():
                    start(*self.others[k - 1])

        def end(self):
            h = self.h
            arrive(*self.arrivals)
            for c in range(2):
                total = zr[h, c, 0]
                for k in range(1, NZ):
                    total += zr[h, c, k]
                gh_out[c, h] = total

    d00, d01, d10, d11 = (Reduce(h, c) for h in range(H) for c in range(2))
    z0, z1 = Reduce_z(0), Reduce_z(1)

    weight_copies = [remote(gw_send.at[n], gw_recv.at[n], sibling) for n in range(D // NC)]

    def weight_part(side, n):
        rows = pl.ds(pl.multiple_of(side * ROWS, ROWS), ROWS)
        cols = pl.ds(pl.multiple_of(n * NC, NC), NC)
        lhs = jnp.concatenate([grad[k, rows, :] for k in range(NB)], axis=1)
        rhs = hall[:, :, :, :, cols].reshape(NB * BLK, NC)
        return jnp.dot(lhs, rhs, preferred_element_type=F32), cols

    def weight_other(n):
        gw_send[n] = weight_part(1 - core, n)[0]

    def weight_own(n):
        part, cols = weight_part(core, n)
        gw_out[:, cols] = part + gw_recv[n]

    stat_copy = remote(stat_swap.at[0], stat_swap.at[1], sibling)

    def own_stats():
        for q in range(2):
            line = jnp.zeros((8, 128), F32)
            for h in range(H):
                k = h * RING + pb
                log_total, mean, target = (fin[2, k, pl.ds(i, 1), :] for i in range(3))
                row = jnp.broadcast_to(target - log_total if q == 0 else log_total - mean, (8, 128))
                for s in range(2):
                    group = (h * 2 + s) + core * 4
                    shift = lax.rem(group * R + 256 - (s * RING + pa) * R, 128)
                    line = jnp.where(lanes_of(group), pltpu.roll(row, shift, 1), line)
            stat_swap[0, q] = line
        start(stat_copy)

    def own_stats_store():
        arrive(stat_copy)
        mine = lax.div(lane, 64) == core
        for q, out in enumerate((lp_out, en_out)):
            out[...] = jnp.where(mine, stat_swap[0, q], stat_swap[1, q])[0:1]

    def staged(count, before, body):
        def step(i, carry):
            for j, action in before.items():
                pl.when(i == j)(action)
            body(i)
            return carry

        lax.fori_loop(0, count, step, 0)

    for c in small_in:
        c.wait()
    reorder(ids_in, ids_row)
    reorder(adv_in, adv_row)
    pl.semaphore_wait(barrier, len(peers))
    start(*g0.ring, *g1.ring)
    for c in [w_in] + own_in:
        c.wait()
    start(w_swap)
    g0.spread()
    g0.pass_on()
    g1.spread()
    arrive(w_swap, *g0.second)

    def unit(i):
        half = lax.rem(i, 2)
        k = lax.div(i, 2) * RING
        stats_blocks(k + lax.rem(pb + half, RING), k + lax.rem(pb + 3 - half, RING))

    def before_1():
        arrive(*g0.on)

    def before_2():
        s0.begin()
        g1.pass_on()
        s0.step(0)
        arrive(*g1.second)

    def before_3():
        s0.step(1)
        arrive(*g1.on)

    staged(4, {1: before_1, 2: before_2, 3: before_3}, unit)
    s1.begin()

    def chunk_step(h):
        each_step(lambda v: grad_step(h, 0, v))
        pl.when(h == 1)(d01.relay_b)
        each_step(lambda n: product_step(h, 0, n), lambda v: grad_step(h, 1, v))

        @pl.when(h == 0)
        def _():
            d00.send(0, 1)
            d01.send(0, 1)
            d00.send(2)
            d01.send(2)
            s1.step(0)

        @pl.when(h == 1)
        def _():
            d10.send(0, 1)
            d11.send(0, 1)
            d10.send(2)
            d11.send(2)
            d00.end_b()

        each_step(lambda n: product_step(h, 1, n))

    def before_chunk_1():
        d00.send(3)
        d01.send(3)
        s1.step(1)
        d00.relay_b()

    staged(H, {1: before_chunk_1}, chunk_step)
    d10.send(3)
    d11.send(3)
    own_stats()

    def weight_sent(n, *then):
        def action():
            start(weight_copies[n])
            for step in then:
                step()

        return action

    def weight_came(n, *then):
        def action():
            arrive(weight_copies[n])
            for step in then:
                step()

        return action

    staged(4, {1: weight_sent(0, d01.end_b), 2: weight_sent(1, d10.relay_b), 3: weight_sent(2)}, weight_other)
    start(weight_copies[3])
    d11.relay_b()

    def before_own_1():
        d00.end_a()
        z0.send(0)
        d10.end_b()

    def before_own_2():
        d01.end_a()
        z0.send(1)

    staged(4, {0: weight_came(0), 1: weight_came(1, before_own_1), 2: weight_came(2, before_own_2),
               3: weight_came(3, d11.end_b)}, weight_own)
    d10.end_a()
    z1.send(0)
    z0.end()
    own_stats_store()
    d11.end_a()
    z1.send(1)
    last = [z1.sibling] + [copy for both in z1.others for copy in both]
    for copy in copies:
        if not any(copy is other for other in last):
            copy.wait_send()
    z1.end()
    for copy in last:
        copy.wait_send()


def call(hid, w, ids, adv):
    vmem = pl.BlockSpec(memory_space=pltpu.VMEM)
    anywhere = pl.BlockSpec(memory_space=pl.ANY)
    scratch = [
        pltpu.VMEM((NB, 2, RING, R, D), BF16),
        pltpu.VMEM((V, D), BF16),
        pltpu.VMEM((NB, V, BLK), F32),
        pltpu.VMEM((NB, V, BLK), BF16),
        pltpu.VMEM((2, 2 * BLK, V), BF16),
        pltpu.VMEM((H, 2, 4, HALF, DC), F32),
        pltpu.VMEM((H, 2, 6, HALF, DC), BF16),
        pltpu.VMEM((H, 2, 6, HALF, DC), BF16),
        pltpu.VMEM((H, 2, 2, HALF, DC), F32),
        pltpu.VMEM((H, 2, RING - 1, 2, R, DC), BF16),
        pltpu.VMEM((H, 2, RING - 1, 2, R, DC), BF16),
        pltpu.VMEM((H, NZ, 2, 2, R, 128), F32),
        pltpu.VMEM((H, 2, NZ, 2, R, 128), F32),
        pltpu.VMEM((NB, 4, BLK), F32),
        pltpu.VMEM((H, RING * RING - 1, RING, 4, BLK), F32),
        pltpu.VMEM((H, NZ - 1, RING, 4, BLK), F32),
        pltpu.VMEM((3, NB, 4, BLK), F32),
        pltpu.VMEM((16, 128), jnp.int32),
        pltpu.VMEM((16, 128), F32),
        pltpu.VMEM((16, 128), F32),
        pltpu.VMEM((NB, 1, BLK), jnp.int32),
        pltpu.VMEM((NB, 1, BLK), F32),
        pltpu.VMEM((2, 2, 8, 128), F32),
        pltpu.VMEM((D // NC, ROWS, NC), F32),
        pltpu.VMEM((D // NC, ROWS, NC), F32),
        pltpu.SemaphoreType.DMA((NSEM,)),
        pltpu.SemaphoreType.DMA((NSEM,)),
        pltpu.SemaphoreType.DMA((H, NZ, 2)),
        pltpu.SemaphoreType.DMA((3 + H,)),
    ]
    return pl.pallas_call(
        kernel,
        out_shape=(
            pltpu.VMEM((ROWS, D), F32),
            pltpu.VMEM((2, H, 2, R, 128), F32),
            pltpu.VMEM((1, SHARD), F32),
            pltpu.VMEM((1, SHARD), F32),
        ),
        in_specs=[anywhere] * 4,
        out_specs=(vmem, vmem, vmem, vmem),
        scratch_shapes=scratch,
        compiler_params=pltpu.CompilerParams(
            collective_id=0, has_side_effects=True, vmem_limit_bytes=50 * 2**20),
    )(hid, w, ids, adv)


def store_kernel(*refs):
    count = len(refs) // 2
    moves = [pltpu.make_async_copy(refs[i], refs[count + i], refs[-1].at[i]) for i in range(count)]
    for move in moves:
        move.start()
    for move in moves:
        move.wait()


def store(*arrays):
    return pl.pallas_call(
        store_kernel,
        out_shape=[jax.ShapeDtypeStruct(a.shape, a.dtype) for a in arrays],
        in_specs=[pl.BlockSpec(memory_space=pltpu.VMEM)] * len(arrays),
        out_specs=[pl.BlockSpec(memory_space=pl.ANY)] * len(arrays),
        scratch_shapes=[pltpu.SemaphoreType.DMA((len(arrays),))],
        compiler_params=pltpu.CompilerParams(vmem_limit_bytes=4 * 2**20),
    )(*arrays)


def shards(hidden, head_weight, sampled_ids, advantage):
    hid = hidden.reshape(2, H, 2, R, D)
    grad_weight, grad_hidden, log_prob, entropy = store(*call(
        hid, head_weight, sampled_ids.reshape(16, 128), advantage.reshape(16, 128)))
    return (log_prob.reshape(SHARD), entropy.reshape(SHARD), grad_hidden.reshape(SHARD, 128), grad_weight)


def solution(mesh):
    placed = (P("dp", None), P(("dp", "vocab"), None), P(), P())
    return jax.shard_map(
        shards,
        mesh=mesh,
        in_specs=placed,
        out_specs=(P("dp"), P("dp"), P("dp", "vocab"), P(("dp", "vocab"), None)),
        check_vma=False,
    )
```

```python
import jax
import jax.numpy as jnp
from jax import lax
from jax.experimental import pallas as pl
from jax.experimental.pallas import tpu as pltpu
from jax.sharding import PartitionSpec as P

ENTROPY_COEF = 0.25
MESH = pl.DeviceIdType.MESH
F32, BF16 = jnp.float32, jnp.bfloat16

D = 2048
V = 1024
ROWS = 512
SHARD = 128
RING = 4
NZ = 8
H = 2
R = 16
BLK = 2 * RING * R
HALF = RING * R
NB = RING * H
VC = 256
NC = 512
DC = D // 2
NSEM = 144


def kernel(hid, w, ids, adv, gw_out, gh_out, lp_out, en_out,
           hall, wall, logits, grad, grad_t, pm, x1, y1, r1, x2, y2, zs, zr, st, sx, sy, sz, fin,
           ids_in, adv_in, rolled, ids_row, adv_row, stat_swap, gw_send, gw_recv, send_sem, recv_sem, z_sem, local_sem):
    dp, vo = lax.axis_index("dp"), lax.axis_index("vocab")
    x, y = lax.div(dp, RING), lax.rem(dp, RING)
    z, core = lax.div(vo, 2), lax.rem(vo, 2)
    pa, pb = x + core * (y - x), y + core * (x - y)
    a_p, a_2, a_m = (lax.rem(pa + k, RING) for k in (1, 2, 3))
    b_p, b_2, b_m = (lax.rem(pb + k, RING) for k in (1, 2, 3))

    def place(a, b):
        first, second = a * RING + b, b * RING + a
        return first + core * (second - first)

    def dev(a, b):
        return {"dp": place(a, b), "vocab": vo}

    def zdev(k):
        return {"dp": dp, "vocab": lax.rem(z + k, NZ) * 2 + core}

    sibling = {"dp": dp, "vocab": vo + 1 - 2 * core}

    copies = []

    def remote(src, dst, device, arrival=None):
        i = len(copies)
        copies.append(pltpu.make_async_remote_copy(
            src_ref=src, dst_ref=dst, send_sem=send_sem.at[i], recv_sem=recv_sem.at[i] if arrival is None else arrival,
            device_id=device, device_id_type=MESH))
        return copies[-1]

    def start(*some):
        for copy in some:
            copy.start()

    def arrive(*some):
        for copy in some:
            copy.wait_recv()

    w_rows = pl.ds(pl.multiple_of(core * ROWS, ROWS), ROWS)
    w_in = pltpu.make_async_copy(w, wall.at[w_rows], local_sem.at[0])
    small_in = [pltpu.make_async_copy(ids, ids_in, local_sem.at[1]),
                pltpu.make_async_copy(adv, adv_in, local_sem.at[2])]
    own_in = [pltpu.make_async_copy(hid.at[core, h], hall.at[h * RING + pb, :, pa], local_sem.at[3 + h])
              for h in range(H)]
    for c in [w_in] + small_in + own_in:
        c.start()

    a_dev = [dev(lax.rem(pa + k, RING), pb) for k in (1, 2, 3)]
    b_dev = [dev(pa, lax.rem(pb + k, RING)) for k in (1, 2, 3)]
    z_dev = [zdev(k) for k in range(1, NZ)]
    ap, _, am = a_dev
    bp, _, bm = b_dev
    barrier = pltpu.get_barrier_semaphore()
    z_both = [[dict(dp=dp, vocab=lax.rem(z + k, NZ) * 2 + f) for f in range(2)] for k in range(1, NZ)]
    peers = a_dev + b_dev + [d for both in z_both for d in both] + [sibling]
    for peer in peers:
        pl.semaphore_signal(barrier, inc=1, device_id=peer, device_id_type=MESH)

    w_swap = remote(wall.at[w_rows], wall.at[w_rows], sibling)

    class Gather:
        def __init__(self, h):
            kp, km, k0 = (h * RING + b for b in (b_p, b_m, pb))
            own, there = hid.at[core, h], hall.at[k0, :, pa]
            self.near = [remote(own, there, d) for d in (ap, am)]
            self.far = [remote(hall.at[k0, 0, a_m], hall.at[k0, 0, a_m], ap),
                        remote(hall.at[k0, 1, a_p], hall.at[k0, 1, a_p], am)]
            halves = [hall.at[k0, s] for s in range(2)]
            self.first = [remote(halves[0], halves[0], bp), remote(halves[1], halves[1], bm)]
            self.second = [remote(halves[1], halves[1], bp), remote(halves[0], halves[0], bm)]
            self.on = [remote(hall.at[km, 0], hall.at[km, 0], bp), remote(hall.at[kp, 1], hall.at[kp, 1], bm)]

        def ring(self):
            for near, far in zip(self.near, self.far):
                arrive(near)
                start(far)

        def spread(self):
            arrive(*self.far)
            start(*self.first, *self.second)

        def pass_on(self):
            for first, on in zip(self.first, self.on):
                arrive(first)
                start(on)

    g0, g1 = Gather(0), Gather(1)

    lane = lax.broadcasted_iota(jnp.int32, (8, 128), 1)

    def lanes_of(group):
        return lax.div(lane, R) == group

    def reorder(source, out):
        both = source[...].astype(F32)
        rolled[...] = jnp.where(core == 0, both, pltpu.roll(both, 64, 1))
        for b in range(RING):
            rows = [jnp.broadcast_to(rolled[pl.ds(place(a, b), 1), :], (8, 128)) for a in range(RING)]
            for h in range(H):
                line = jnp.zeros((8, 128), F32)
                for a in range(RING):
                    for s in range(2):
                        group = s * RING + a
                        shift = (group * R - h * 2 * R - s * R) % 128
                        line = jnp.where(lanes_of(group), pltpu.roll(rows[a], shift, 1), line)
                out[h * RING + b] = line[0:1].astype(out.dtype)

    first_row = dp * (2 * ROWS * NZ) + z * (2 * ROWS)

    def stats_blocks(k_one, k_two):
        token_ids = jnp.concatenate([ids_row[k_one], ids_row[k_two]], axis=1) - first_row

        def product(v):
            tokens = jnp.concatenate([hall[k_one].reshape(BLK, D), hall[k_two].reshape(BLK, D)], axis=0)
            part = lax.dot_general(wall[v * VC:(v + 1) * VC, :], tokens, (((1,), (1,)), ((), ())),
                                   preferred_element_type=F32)
            logits[k_one, v * VC:(v + 1) * VC, :] = part[:, :BLK]
            logits[k_two, v * VC:(v + 1) * VC, :] = part[:, BLK:]

        def add_sums(v, peak, sums):
            rows = slice(v * VC, (v + 1) * VC)
            part = jnp.concatenate([logits[k_one, rows, :], logits[k_two, rows, :]], axis=1)
            above = jnp.max(part, axis=0, keepdims=True)
            new_peak = above if peak is None else jnp.maximum(peak, above)
            expon = jnp.exp(part - new_peak)
            row = lax.broadcasted_iota(jnp.int32, part.shape, 0)
            picked = jnp.where(row == token_ids - v * VC, part, 0.0)
            more = [jnp.sum(p, axis=0, keepdims=True) for p in (expon, expon * part, picked)]
            if peak is not None:
                scale = jnp.exp(peak - new_peak)
                more = [m + s * f for m, s, f in zip(more, sums, (scale, scale, 1.0))]
            return new_peak, more

        peak, sums = None, None
        product(0)
        for v in range(1, V // VC):
            product(v)
            peak, sums = add_sums(v - 1, peak, sums)
        peak, sums = add_sums(V // VC - 1, peak, sums)
        for q, row in enumerate([peak] + sums):
            st[k_one, pl.ds(q, 1), :] = row[:, :BLK]
            st[k_two, pl.ds(q, 1), :] = row[:, BLK:]

    def stats_merge(ref, slots, sent):
        arrive(*sent)
        parts = [ref[...]] + [slots[i] for i in range(len(sent))]
        peak = parts[0][:, 0:1, :]
        for p in parts[1:]:
            peak = jnp.maximum(peak, p[:, 0:1, :])
        total, weighted, target = 0.0, 0.0, 0.0
        for p in parts:
            scale = jnp.exp(p[:, 0:1, :] - peak)
            total += scale * p[:, 1:2, :]
            weighted += scale * p[:, 2:3, :]
            target += p[:, 3:4, :]
        return peak, total, weighted, target

    class Stats:
        def __init__(self, h):
            blocks = pl.ds(h * RING, RING)
            self.steps = [(st.at[blocks], sz.at[h], fin.at[0, blocks], z_dev),
                          (fin.at[0, blocks], sx.at[h], fin.at[1, blocks], a_dev),
                          (fin.at[1, blocks], sy.at[h], fin.at[2, blocks], b_dev)]
            self.sent = [[remote(ref, slots.at[i], d) for i, d in enumerate(devices)]
                         for ref, slots, _, devices in self.steps]

        def begin(self):
            start(*self.sent[0])

        def step(self, i):
            ref, slots, out, _ = self.steps[i]
            rows = stats_merge(ref, slots, self.sent[i])
            if i == 2:
                peak, total, weighted, target = rows
                rows = (peak + jnp.log(total), weighted / total, target)
            for q, row in enumerate(rows):
                out[:, pl.ds(q, 1), :] = row
            if i < 2:
                start(*self.sent[i + 1])

    s0, s1 = Stats(0), Stats(1)

    order = (b_2, b_m, b_p, pb)
    STEPS = D // NC
    GR = V // STEPS

    def grad_step(h, pair, v):
        ks = [h * RING + b for b in order[2 * pair:2 * pair + 2]]
        token_ids = jnp.concatenate([ids_row[k] for k in ks], axis=1) - first_row
        advantage = jnp.concatenate([adv_row[k] for k in ks], axis=1)
        log_total = jnp.concatenate([fin[2, k, 0:1, :] for k in ks], axis=1)
        mean = jnp.concatenate([fin[2, k, 1:2, :] for k in ks], axis=1)
        level = advantage - ENTROPY_COEF * mean
        start_row = pl.multiple_of(v * GR, GR)
        rows = pl.ds(start_row, GR)
        part = jnp.concatenate([logits[k, rows, :] for k in ks], axis=1)
        prob = jnp.exp(part - log_total)
        row = lax.broadcasted_iota(jnp.int32, part.shape, 0)
        chosen = jnp.where(row == token_ids - start_row, advantage, 0.0)
        low = (chosen - prob * (level + ENTROPY_COEF * part)).astype(BF16)
        for j, k in enumerate(ks):
            tile = low[:, j * BLK:(j + 1) * BLK]
            grad[k, rows, :] = tile
            grad_t[pair, j * BLK:(j + 1) * BLK, rows] = tile.T

    def product_step(h, pair, n):
        c, m = lax.div(n, STEPS // 2), lax.rem(n, STEPS // 2)
        cols = pl.ds(pl.multiple_of(m * NC, NC), NC)
        part = jnp.dot(grad_t[pair], wall[:, pl.ds(pl.multiple_of(n * NC, NC), NC)], preferred_element_type=F32)
        one_0, one_1, two_0, two_1 = (part[i * HALF:(i + 1) * HALF] for i in range(4))
        if pair == 0:
            x1[h, c, 0, :, cols] = one_0.astype(BF16)
            x1[h, c, 2, :, cols] = one_1.astype(BF16)
            pm[h, c, 0, :, cols] = two_0
            x1[h, c, 1, :, cols] = two_1.astype(BF16)
        else:
            x1[h, c, 3, :, cols] = one_0.astype(BF16)
            pm[h, c, 1, :, cols] = one_1
            pm[h, c, 2, :, cols] = two_0
            pm[h, c, 3, :, cols] = two_1

    def each_step(*bodies):
        def step(n, carry):
            for body in bodies:
                body(n)
            return carry

        lax.fori_loop(0, STEPS, step, 0)

    def chunked(rows, body):
        def step(n, carry):
            body(pl.ds(pl.multiple_of(n * 32, 32), 32))
            return carry

        lax.fori_loop(0, rows // 32, step, 0)

    def slot(a):
        return pl.ds(pl.multiple_of(a * R, R), R)

    class Reduce:
        def __init__(self, h, c):
            self.at = h, c
            self.b = [remote(x1.at[h, c, i], y1.at[h, c, i], d)
                      for i, d in ((0, bm), (2, bp), (1, bm), (3, bp), (4, bm), (5, bp))]
            self.a = [remote(x2.at[h, c, i], y2.at[h, c, i], d) for i, d in enumerate(a_dev)]

        def send(self, *which):
            start(*[self.b[i] for i in which])

        def relay_b(self):
            h, c = self.at
            for i in range(2):
                arrive(self.b[i])

                def relay(rows):
                    x1[h, c, 4 + i, rows, :] = (
                        pm[h, c, i, rows, :] + y1[h, c, 2 * i, rows, :].astype(F32)).astype(BF16)

                chunked(HALF, relay)
                start(self.b[4 + i])

        def end_b(self):
            h, c = self.at
            arrive(*self.b[2:])
            for s, (one, two) in enumerate(((3, 4), (1, 5))):

                def total(rows):
                    r1[h, c, s, rows, :] = (pm[h, c, 2 + s, rows, :] + y1[h, c, one, rows, :].astype(F32)
                                            + y1[h, c, two, rows, :].astype(F32))

                chunked(HALF, total)
            for i in (1, 0, 2):
                for s in range(2):
                    x2[h, c, i, s] = r1[h, c, s, slot((a_p, a_2, a_m)[i]), :].astype(BF16)
                start(self.a[i])

        def end_a(self):
            h, c = self.at
            arrive(*self.a)
            for s in range(2):
                for f in range(DC // 128):
                    cols = slice(f * 128, f * 128 + 128)
                    zs[h, c * (NZ // 2) + f // 2, f % 2, s] = r1[h, c, s, slot(pa), cols] + sum(
                        y2[h, c, i, s, :, cols].astype(F32) for i in range(RING - 1))

    class Reduce_z:
        def __init__(self, h):
            self.h = h
            self.sibling = remote(zs.at[h, z, 1 - core], zr.at[h, core, 0], sibling, z_sem.at[h, 0, core])
            self.others = [[remote(zs.at[h, lax.rem(z + k, NZ), f], zr.at[h, core, k], z_both[k - 1][f],
                                   z_sem.at[h, k, core]) for f in range(2)] for k in range(1, NZ)]
            places = [(1 - core, 0)] + [(c, k) for k in range(1, NZ) for c in range(2)]
            self.arrivals = [pltpu.make_async_remote_copy(
                src_ref=zr.at[h, c, k], dst_ref=zr.at[h, c, k], send_sem=send_sem.at[0], recv_sem=z_sem.at[h, k, c],
                device_id=sibling, device_id_type=MESH) for c, k in places]

        def send(self, c):
            @pl.when(lax.div(z, NZ // 2) == c)
            def _():
                zr[self.h, core, 0] = zs[self.h, z, core]
                start(self.sibling)

            for k in range(1, NZ):

                @pl.when(lax.div(lax.rem(z + k, NZ), NZ // 2) == c)
                def _():
                    start(*self.others[k - 1])

        def end(self):
            h = self.h
            arrive(*self.arrivals)
            for c in range(2):
                total = zr[h, c, 0]
                for k in range(1, NZ):
                    total += zr[h, c, k]
                gh_out[c, h] = total

    d00, d01, d10, d11 = (Reduce(h, c) for h in range(H) for c in range(2))
    z0, z1 = Reduce_z(0), Reduce_z(1)

    weight_copies = [remote(gw_send.at[n], gw_recv.at[n], sibling) for n in range(D // NC)]

    def weight_part(side, n):
        rows = pl.ds(pl.multiple_of(side * ROWS, ROWS), ROWS)
        cols = pl.ds(pl.multiple_of(n * NC, NC), NC)
        lhs = jnp.concatenate([grad[k, rows, :] for k in range(NB)], axis=1)
        rhs = hall[:, :, :, :, cols].reshape(NB * BLK, NC)
        return jnp.dot(lhs, rhs, preferred_element_type=F32), cols

    def weight_other(n):
        gw_send[n] = weight_part(1 - core, n)[0]

    def weight_own(n):
        part, cols = weight_part(core, n)
        gw_out[:, cols] = part + gw_recv[n]

    stat_copy = remote(stat_swap.at[0], stat_swap.at[1], sibling)

    def own_stats():
        for q in range(2):
            line = jnp.zeros((8, 128), F32)
            for h in range(H):
                k = h * RING + pb
                log_total, mean, target = (fin[2, k, pl.ds(i, 1), :] for i in range(3))
                row = jnp.broadcast_to(target - log_total if q == 0 else log_total - mean, (8, 128))
                for s in range(2):
                    group = (h * 2 + s) + core * 4
                    shift = lax.rem(group * R + 256 - (s * RING + pa) * R, 128)
                    line = jnp.where(lanes_of(group), pltpu.roll(row, shift, 1), line)
            stat_swap[0, q] = line
        start(stat_copy)

    def own_stats_store():
        arrive(stat_copy)
        mine = lax.div(lane, 64) == core
        for q, out in enumerate((lp_out, en_out)):
            out[...] = jnp.where(mine, stat_swap[0, q], stat_swap[1, q])[0:1]

    def staged(count, before, body):
        def step(i, carry):
            for j, action in before.items():
                pl.when(i == j)(action)
            body(i)
            return carry

        lax.fori_loop(0, count, step, 0)

    for c in small_in:
        c.wait()
    reorder(ids_in, ids_row)
    reorder(adv_in, adv_row)
    pl.semaphore_wait(barrier, len(peers))
    start(*g0.near, *g1.near)
    for c in [w_in] + own_in:
        c.wait()
    start(w_swap)
    g0.ring()
    g1.ring()
    g0.spread()
    g0.pass_on()
    g1.spread()
    arrive(w_swap, *g0.second)

    def unit(i):
        half = lax.rem(i, 2)
        k = lax.div(i, 2) * RING
        stats_blocks(k + lax.rem(pb + half, RING), k + lax.rem(pb + 3 - half, RING))

    def before_1():
        arrive(*g0.on)

    def before_2():
        s0.begin()
        g1.pass_on()
        s0.step(0)
        arrive(*g1.second)

    def before_3():
        s0.step(1)
        arrive(*g1.on)

    staged(4, {1: before_1, 2: before_2, 3: before_3}, unit)
    s1.begin()
    s0.step(2)

    def chunk_step(h):
        each_step(lambda v: grad_step(h, 0, v))
        pl.when(h == 1)(d01.relay_b)
        each_step(lambda n: product_step(h, 0, n), lambda v: grad_step(h, 1, v))

        @pl.when(h == 0)
        def _():
            d00.send(0, 1)
            d01.send(0, 1)
            d00.send(2)
            d01.send(2)
            s1.step(0)

        @pl.when(h == 1)
        def _():
            d10.send(0, 1)
            d11.send(0, 1)
            d10.send(2)
            d11.send(2)
            d00.end_b()

        each_step(lambda n: product_step(h, 1, n))

    def before_chunk_1():
        d00.send(3)
        d01.send(3)
        s1.step(1)
        d00.relay_b()
        s1.step(2)

    staged(H, {1: before_chunk_1}, chunk_step)
    d10.send(3)
    d11.send(3)
    own_stats()

    def weight_sent(n, *then):
        def action():
            start(weight_copies[n])
            for step in then:
                step()

        return action

    def weight_came(n, *then):
        def action():
            arrive(weight_copies[n])
            for step in then:
                step()

        return action

    staged(4, {1: weight_sent(0, d01.end_b), 2: weight_sent(1, d10.relay_b), 3: weight_sent(2)}, weight_other)
    start(weight_copies[3])
    d11.relay_b()

    def before_own_1():
        d00.end_a()
        z0.send(0)

    def before_own_2():
        d01.end_a()
        z0.send(1)

    staged(4, {0: weight_came(0), 1: weight_came(1, before_own_1), 2: weight_came(2, before_own_2),
               3: weight_came(3)}, weight_own)
    d10.end_b()
    d11.end_b()
    d10.end_a()
    z1.send(0)
    z0.end()
    own_stats_store()
    d11.end_a()
    z1.send(1)
    last = [z1.sibling] + [copy for both in z1.others for copy in both]
    for copy in copies:
        if not any(copy is other for other in last):
            copy.wait_send()
    z1.end()
    for copy in last:
        copy.wait_send()


def call(hid, w, ids, adv):
    vmem = pl.BlockSpec(memory_space=pltpu.VMEM)
    anywhere = pl.BlockSpec(memory_space=pl.ANY)
    scratch = [
        pltpu.VMEM((NB, 2, RING, R, D), BF16),
        pltpu.VMEM((V, D), BF16),
        pltpu.VMEM((NB, V, BLK), F32),
        pltpu.VMEM((NB, V, BLK), BF16),
        pltpu.VMEM((2, 2 * BLK, V), BF16),
        pltpu.VMEM((H, 2, 4, HALF, DC), F32),
        pltpu.VMEM((H, 2, 6, HALF, DC), BF16),
        pltpu.VMEM((H, 2, 6, HALF, DC), BF16),
        pltpu.VMEM((H, 2, 2, HALF, DC), F32),
        pltpu.VMEM((H, 2, RING - 1, 2, R, DC), BF16),
        pltpu.VMEM((H, 2, RING - 1, 2, R, DC), BF16),
        pltpu.VMEM((H, NZ, 2, 2, R, 128), F32),
        pltpu.VMEM((H, 2, NZ, 2, R, 128), F32),
        pltpu.VMEM((NB, 4, BLK), F32),
        pltpu.VMEM((H, RING - 1, RING, 4, BLK), F32),
        pltpu.VMEM((H, RING - 1, RING, 4, BLK), F32),
        pltpu.VMEM((H, NZ - 1, RING, 4, BLK), F32),
        pltpu.VMEM((3, NB, 4, BLK), F32),
        pltpu.VMEM((16, 128), jnp.int32),
        pltpu.VMEM((16, 128), F32),
        pltpu.VMEM((16, 128), F32),
        pltpu.VMEM((NB, 1, BLK), jnp.int32),
        pltpu.VMEM((NB, 1, BLK), F32),
        pltpu.VMEM((2, 2, 8, 128), F32),
        pltpu.VMEM((D // NC, ROWS, NC), F32),
        pltpu.VMEM((D // NC, ROWS, NC), F32),
        pltpu.SemaphoreType.DMA((NSEM,)),
        pltpu.SemaphoreType.DMA((NSEM,)),
        pltpu.SemaphoreType.DMA((H, NZ, 2)),
        pltpu.SemaphoreType.DMA((3 + H,)),
    ]
    return pl.pallas_call(
        kernel,
        out_shape=(
            pltpu.VMEM((ROWS, D), F32),
            pltpu.VMEM((2, H, 2, R, 128), F32),
            pltpu.VMEM((1, SHARD), F32),
            pltpu.VMEM((1, SHARD), F32),
        ),
        in_specs=[anywhere] * 4,
        out_specs=(vmem, vmem, vmem, vmem),
        scratch_shapes=scratch,
        compiler_params=pltpu.CompilerParams(
            collective_id=0, has_side_effects=True, vmem_limit_bytes=50 * 2**20),
    )(hid, w, ids, adv)


def store_kernel(*refs):
    count = len(refs) // 2
    moves = [pltpu.make_async_copy(refs[i], refs[count + i], refs[-1].at[i]) for i in range(count)]
    for move in moves:
        move.start()
    for move in moves:
        move.wait()


def store(*arrays):
    return pl.pallas_call(
        store_kernel,
        out_shape=[jax.ShapeDtypeStruct(a.shape, a.dtype) for a in arrays],
        in_specs=[pl.BlockSpec(memory_space=pltpu.VMEM)] * len(arrays),
        out_specs=[pl.BlockSpec(memory_space=pl.ANY)] * len(arrays),
        scratch_shapes=[pltpu.SemaphoreType.DMA((len(arrays),))],
        compiler_params=pltpu.CompilerParams(vmem_limit_bytes=4 * 2**20),
    )(*arrays)


def shards(hidden, head_weight, sampled_ids, advantage):
    hid = hidden.reshape(2, H, 2, R, D)
    grad_weight, grad_hidden, log_prob, entropy = store(*call(
        hid, head_weight, sampled_ids.reshape(16, 128), advantage.reshape(16, 128)))
    return (log_prob.reshape(SHARD), entropy.reshape(SHARD), grad_hidden.reshape(SHARD, 128), grad_weight)


def solution(mesh):
    placed = (P("dp", None), P(("dp", "vocab"), None), P(), P())
    return jax.shard_map(
        shards,
        mesh=mesh,
        in_specs=placed,
        out_specs=(P("dp"), P("dp"), P("dp", "vocab"), P(("dp", "vocab"), None)),
        check_vma=False,
    )
```

```python
import jax
import jax.numpy as jnp
from jax import lax
from jax.experimental import pallas as pl
from jax.experimental.pallas import tpu as pltpu
from jax.sharding import PartitionSpec as P

ENTROPY_COEF = 0.25
MESH = pl.DeviceIdType.MESH
F32, BF16 = jnp.float32, jnp.bfloat16

D = 2048
V = 1024
ROWS = 512
SHARD = 128
RING = 4
NZ = 8
H = 2
R = 16
BLK = 2 * RING * R
HALF = RING * R
NB = RING * H
VC = 256
NC = 512
DC = D // 2
NSEM = 144


def kernel(hid, w, ids, adv, gw_out, gh_out, lp_out, en_out,
           hall, wall, logits, grad, grad_t, pm, x1, y1, r1, x2, y2, zs, zr, st, sx, sy, sz, fin,
           ids_in, adv_in, rolled, ids_row, adv_row, stat_swap, gw_send, gw_recv, send_sem, recv_sem, z_sem, local_sem):
    dp, vo = lax.axis_index("dp"), lax.axis_index("vocab")
    x, y = lax.div(dp, RING), lax.rem(dp, RING)
    z, core = lax.div(vo, 2), lax.rem(vo, 2)
    pa, pb = x + core * (y - x), y + core * (x - y)
    a_p, a_2, a_m = (lax.rem(pa + k, RING) for k in (1, 2, 3))
    b_p, b_2, b_m = (lax.rem(pb + k, RING) for k in (1, 2, 3))

    def place(a, b):
        first, second = a * RING + b, b * RING + a
        return first + core * (second - first)

    def dev(a, b):
        return {"dp": place(a, b), "vocab": vo}

    def zdev(k):
        return {"dp": dp, "vocab": lax.rem(z + k, NZ) * 2 + core}

    sibling = {"dp": dp, "vocab": vo + 1 - 2 * core}

    copies = []

    def remote(src, dst, device, arrival=None):
        i = len(copies)
        copies.append(pltpu.make_async_remote_copy(
            src_ref=src, dst_ref=dst, send_sem=send_sem.at[i], recv_sem=recv_sem.at[i] if arrival is None else arrival,
            device_id=device, device_id_type=MESH))
        return copies[-1]

    def start(*some):
        for copy in some:
            copy.start()

    def arrive(*some):
        for copy in some:
            copy.wait_recv()

    w_rows = pl.ds(pl.multiple_of(core * ROWS, ROWS), ROWS)
    w_in = pltpu.make_async_copy(w, wall.at[w_rows], local_sem.at[0])
    small_in = [pltpu.make_async_copy(ids, ids_in, local_sem.at[1]),
                pltpu.make_async_copy(adv, adv_in, local_sem.at[2])]
    own_in = [pltpu.make_async_copy(hid.at[core, h], hall.at[h * RING + pb, :, pa], local_sem.at[3 + h])
              for h in range(H)]
    for c in [w_in] + small_in + own_in:
        c.start()

    a_dev = [dev(lax.rem(pa + k, RING), pb) for k in (1, 2, 3)]
    b_dev = [dev(pa, lax.rem(pb + k, RING)) for k in (1, 2, 3)]
    z_dev = [zdev(k) for k in range(1, NZ)]
    ap, _, am = a_dev
    bp, _, bm = b_dev
    barrier = pltpu.get_barrier_semaphore()
    z_both = [[dict(dp=dp, vocab=lax.rem(z + k, NZ) * 2 + f) for f in range(2)] for k in range(1, NZ)]
    peers = a_dev + b_dev + [d for both in z_both for d in both] + [sibling]
    for peer in peers:
        pl.semaphore_signal(barrier, inc=1, device_id=peer, device_id_type=MESH)

    w_swap = remote(wall.at[w_rows], wall.at[w_rows], sibling)

    class Gather:
        def __init__(self, h):
            kp, km, k0 = (h * RING + b for b in (b_p, b_m, pb))
            own, there = hid.at[core, h], hall.at[k0, :, pa]
            self.near = [remote(own, there, d) for d in (ap, am)]
            self.far = [remote(hall.at[k0, 0, a_m], hall.at[k0, 0, a_m], ap),
                        remote(hall.at[k0, 1, a_p], hall.at[k0, 1, a_p], am)]
            halves = [hall.at[k0, s] for s in range(2)]
            self.first = [remote(halves[0], halves[0], bp), remote(halves[1], halves[1], bm)]
            self.second = [remote(halves[1], halves[1], bp), remote(halves[0], halves[0], bm)]
            self.on = [remote(hall.at[km, 0], hall.at[km, 0], bp), remote(hall.at[kp, 1], hall.at[kp, 1], bm)]

        def ring(self):
            for near, far in zip(self.near, self.far):
                arrive(near)
                start(far)

        def spread(self):
            arrive(*self.far)
            start(*self.first, *self.second)

        def pass_on(self):
            for first, on in zip(self.first, self.on):
                arrive(first)
                start(on)

    g0, g1 = Gather(0), Gather(1)

    lane = lax.broadcasted_iota(jnp.int32, (8, 128), 1)

    def lanes_of(group):
        return lax.div(lane, R) == group

    def reorder(source, out):
        both = source[...].astype(F32)
        rolled[...] = jnp.where(core == 0, both, pltpu.roll(both, 64, 1))
        for b in range(RING):
            rows = [jnp.broadcast_to(rolled[pl.ds(place(a, b), 1), :], (8, 128)) for a in range(RING)]
            for h in range(H):
                line = jnp.zeros((8, 128), F32)
                for a in range(RING):
                    for s in range(2):
                        group = s * RING + a
                        shift = (group * R - h * 2 * R - s * R) % 128
                        line = jnp.where(lanes_of(group), pltpu.roll(rows[a], shift, 1), line)
                out[h * RING + b] = line[0:1].astype(out.dtype)

    first_row = dp * (2 * ROWS * NZ) + z * (2 * ROWS)

    def stats_blocks(k_one, k_two):
        token_ids = jnp.concatenate([ids_row[k_one], ids_row[k_two]], axis=1) - first_row

        def product(v):
            tokens = jnp.concatenate([hall[k_one].reshape(BLK, D), hall[k_two].reshape(BLK, D)], axis=0)
            part = lax.dot_general(wall[v * VC:(v + 1) * VC, :], tokens, (((1,), (1,)), ((), ())),
                                   preferred_element_type=F32)
            logits[k_one, v * VC:(v + 1) * VC, :] = part[:, :BLK]
            logits[k_two, v * VC:(v + 1) * VC, :] = part[:, BLK:]

        def add_sums(v, peak, sums):
            rows = slice(v * VC, (v + 1) * VC)
            part = jnp.concatenate([logits[k_one, rows, :], logits[k_two, rows, :]], axis=1)
            above = jnp.max(part, axis=0, keepdims=True)
            new_peak = above if peak is None else jnp.maximum(peak, above)
            expon = jnp.exp(part - new_peak)
            row = lax.broadcasted_iota(jnp.int32, part.shape, 0)
            picked = jnp.where(row == token_ids - v * VC, part, 0.0)
            more = [jnp.sum(p, axis=0, keepdims=True) for p in (expon, expon * part, picked)]
            if peak is not None:
                scale = jnp.exp(peak - new_peak)
                more = [m + s * f for m, s, f in zip(more, sums, (scale, scale, 1.0))]
            return new_peak, more

        peak, sums = None, None
        product(0)
        for v in range(1, V // VC):
            product(v)
            peak, sums = add_sums(v - 1, peak, sums)
        peak, sums = add_sums(V // VC - 1, peak, sums)
        for q, row in enumerate([peak] + sums):
            st[k_one, pl.ds(q, 1), :] = row[:, :BLK]
            st[k_two, pl.ds(q, 1), :] = row[:, BLK:]

    def stats_merge(ref, slots, sent):
        arrive(*sent)
        parts = [ref[...]] + [slots[i] for i in range(len(sent))]
        peak = parts[0][:, 0:1, :]
        for p in parts[1:]:
            peak = jnp.maximum(peak, p[:, 0:1, :])
        total, weighted, target = 0.0, 0.0, 0.0
        for p in parts:
            scale = jnp.exp(p[:, 0:1, :] - peak)
            total += scale * p[:, 1:2, :]
            weighted += scale * p[:, 2:3, :]
            target += p[:, 3:4, :]
        return peak, total, weighted, target

    class Stats:
        def __init__(self, h):
            blocks = pl.ds(h * RING, RING)
            self.steps = [(st.at[blocks], sz.at[h], fin.at[0, blocks], z_dev),
                          (fin.at[0, blocks], sx.at[h], fin.at[1, blocks], a_dev),
                          (fin.at[1, blocks], sy.at[h], fin.at[2, blocks], b_dev)]
            self.sent = [[remote(ref, slots.at[i], d) for i, d in enumerate(devices)]
                         for ref, slots, _, devices in self.steps]

        def begin(self):
            start(*self.sent[0])

        def step(self, i):
            ref, slots, out, _ = self.steps[i]
            rows = stats_merge(ref, slots, self.sent[i])
            if i == 2:
                peak, total, weighted, target = rows
                rows = (peak + jnp.log(total), weighted / total, target)
            for q, row in enumerate(rows):
                out[:, pl.ds(q, 1), :] = row
            if i < 2:
                start(*self.sent[i + 1])

    s0, s1 = Stats(0), Stats(1)

    order = (b_2, b_m, b_p, pb)
    STEPS = D // NC
    GR = V // STEPS

    def grad_step(h, pair, v):
        ks = [h * RING + b for b in order[2 * pair:2 * pair + 2]]
        token_ids = jnp.concatenate([ids_row[k] for k in ks], axis=1) - first_row
        advantage = jnp.concatenate([adv_row[k] for k in ks], axis=1)
        log_total = jnp.concatenate([fin[2, k, 0:1, :] for k in ks], axis=1)
        mean = jnp.concatenate([fin[2, k, 1:2, :] for k in ks], axis=1)
        level = advantage - ENTROPY_COEF * mean
        start_row = pl.multiple_of(v * GR, GR)
        rows = pl.ds(start_row, GR)
        part = jnp.concatenate([logits[k, rows, :] for k in ks], axis=1)
        prob = jnp.exp(part - log_total)
        row = lax.broadcasted_iota(jnp.int32, part.shape, 0)
        chosen = jnp.where(row == token_ids - start_row, advantage, 0.0)
        low = (chosen - prob * (level + ENTROPY_COEF * part)).astype(BF16)
        for j, k in enumerate(ks):
            tile = low[:, j * BLK:(j + 1) * BLK]
            grad[k, rows, :] = tile
            grad_t[pair, j * BLK:(j + 1) * BLK, rows] = tile.T

    def product_step(h, pair, n):
        c, m = lax.div(n, STEPS // 2), lax.rem(n, STEPS // 2)
        cols = pl.ds(pl.multiple_of(m * NC, NC), NC)
        part = jnp.dot(grad_t[pair], wall[:, pl.ds(pl.multiple_of(n * NC, NC), NC)], preferred_element_type=F32)
        one_0, one_1, two_0, two_1 = (part[i * HALF:(i + 1) * HALF] for i in range(4))
        if pair == 0:
            x1[h, c, 0, :, cols] = one_0.astype(BF16)
            x1[h, c, 2, :, cols] = one_1.astype(BF16)
            pm[h, c, 0, :, cols] = two_0
            x1[h, c, 1, :, cols] = two_1.astype(BF16)
        else:
            x1[h, c, 3, :, cols] = one_0.astype(BF16)
            pm[h, c, 1, :, cols] = one_1
            pm[h, c, 2, :, cols] = two_0
            pm[h, c, 3, :, cols] = two_1

    def each_step(*bodies):
        def step(n, carry):
            for body in bodies:
                body(n)
            return carry

        lax.fori_loop(0, STEPS, step, 0)

    def chunked(rows, body):
        def step(n, carry):
            body(pl.ds(pl.multiple_of(n * 32, 32), 32))
            return carry

        lax.fori_loop(0, rows // 32, step, 0)

    def slot(a):
        return pl.ds(pl.multiple_of(a * R, R), R)

    class Reduce:
        def __init__(self, h, c):
            self.at = h, c
            self.b = [remote(x1.at[h, c, i], y1.at[h, c, i], d)
                      for i, d in ((0, bm), (2, bp), (1, bm), (3, bp), (4, bm), (5, bp))]
            self.a = [remote(x2.at[h, c, i], y2.at[h, c, i], d) for i, d in enumerate(a_dev)]

        def send(self, *which):
            start(*[self.b[i] for i in which])

        def relay_b(self):
            h, c = self.at
            for i in range(2):
                arrive(self.b[i])

                def relay(rows):
                    x1[h, c, 4 + i, rows, :] = (
                        pm[h, c, i, rows, :] + y1[h, c, 2 * i, rows, :].astype(F32)).astype(BF16)

                chunked(HALF, relay)
                start(self.b[4 + i])

        def end_b(self):
            h, c = self.at
            arrive(*self.b[2:])
            for s, (one, two) in enumerate(((3, 4), (1, 5))):

                def total(rows):
                    r1[h, c, s, rows, :] = (pm[h, c, 2 + s, rows, :] + y1[h, c, one, rows, :].astype(F32)
                                            + y1[h, c, two, rows, :].astype(F32))

                chunked(HALF, total)
            for i in (1, 0, 2):
                for s in range(2):
                    x2[h, c, i, s] = r1[h, c, s, slot((a_p, a_2, a_m)[i]), :].astype(BF16)
                start(self.a[i])

        def end_a(self):
            h, c = self.at
            arrive(*self.a)
            for s in range(2):
                for f in range(DC // 128):
                    cols = slice(f * 128, f * 128 + 128)
                    zs[h, c * (NZ // 2) + f // 2, f % 2, s] = r1[h, c, s, slot(pa), cols] + sum(
                        y2[h, c, i, s, :, cols].astype(F32) for i in range(RING - 1))

    class Reduce_z:
        def __init__(self, h):
            self.h = h
            self.sibling = remote(zs.at[h, z, 1 - core], zr.at[h, core, 0], sibling, z_sem.at[h, 0, core])
            self.others = [[remote(zs.at[h, lax.rem(z + k, NZ), f], zr.at[h, core, k], z_both[k - 1][f],
                                   z_sem.at[h, k, core]) for f in range(2)] for k in range(1, NZ)]
            places = [(1 - core, 0)] + [(c, k) for k in range(1, NZ) for c in range(2)]
            self.arrivals = [pltpu.make_async_remote_copy(
                src_ref=zr.at[h, c, k], dst_ref=zr.at[h, c, k], send_sem=send_sem.at[0], recv_sem=z_sem.at[h, k, c],
                device_id=sibling, device_id_type=MESH) for c, k in places]

        def send(self, c):
            @pl.when(lax.div(z, NZ // 2) == c)
            def _():
                zr[self.h, core, 0] = zs[self.h, z, core]
                start(self.sibling)

            for k in range(1, NZ):

                @pl.when(lax.div(lax.rem(z + k, NZ), NZ // 2) == c)
                def _():
                    start(*self.others[k - 1])

        def end(self):
            h = self.h
            arrive(*self.arrivals)
            for c in range(2):
                total = zr[h, c, 0]
                for k in range(1, NZ):
                    total += zr[h, c, k]
                gh_out[c, h] = total

    d00, d01, d10, d11 = (Reduce(h, c) for h in range(H) for c in range(2))
    z0, z1 = Reduce_z(0), Reduce_z(1)

    weight_copies = [remote(gw_send.at[n], gw_recv.at[n], sibling) for n in range(D // NC)]

    def weight_part(side, n):
        rows = pl.ds(pl.multiple_of(side * ROWS, ROWS), ROWS)
        cols = pl.ds(pl.multiple_of(n * NC, NC), NC)
        lhs = jnp.concatenate([grad[k, rows, :] for k in range(NB)], axis=1)
        rhs = hall[:, :, :, :, cols].reshape(NB * BLK, NC)
        return jnp.dot(lhs, rhs, preferred_element_type=F32), cols

    def weight_other(n):
        gw_send[n] = weight_part(1 - core, n)[0].astype(BF16)

    def weight_own(n):
        part, cols = weight_part(core, n)
        gw_out[:, cols] = part + gw_recv[n].astype(F32)

    stat_copy = remote(stat_swap.at[0], stat_swap.at[1], sibling)

    def own_stats():
        for q in range(2):
            line = jnp.zeros((8, 128), F32)
            for h in range(H):
                k = h * RING + pb
                log_total, mean, target = (fin[2, k, pl.ds(i, 1), :] for i in range(3))
                row = jnp.broadcast_to(target - log_total if q == 0 else log_total - mean, (8, 128))
                for s in range(2):
                    group = (h * 2 + s) + core * 4
                    shift = lax.rem(group * R + 256 - (s * RING + pa) * R, 128)
                    line = jnp.where(lanes_of(group), pltpu.roll(row, shift, 1), line)
            stat_swap[0, q] = line
        start(stat_copy)

    def own_stats_store():
        arrive(stat_copy)
        mine = lax.div(lane, 64) == core
        for q, out in enumerate((lp_out, en_out)):
            out[...] = jnp.where(mine, stat_swap[0, q], stat_swap[1, q])[0:1]

    def staged(count, before, body):
        def step(i, carry):
            for j, action in before.items():
                pl.when(i == j)(action)
            body(i)
            return carry

        lax.fori_loop(0, count, step, 0)

    for c in small_in:
        c.wait()
    reorder(ids_in, ids_row)
    reorder(adv_in, adv_row)
    pl.semaphore_wait(barrier, len(peers))
    start(*g0.near, *g1.near)
    for c in [w_in] + own_in:
        c.wait()
    start(w_swap)
    g0.ring()
    g1.ring()
    g0.spread()
    g0.pass_on()
    g1.spread()
    arrive(w_swap, *g0.second)

    def unit(i):
        half = lax.rem(i, 2)
        k = lax.div(i, 2) * RING
        stats_blocks(k + lax.rem(pb + half, RING), k + lax.rem(pb + 3 - half, RING))

    def before_1():
        arrive(*g0.on)

    def before_2():
        s0.begin()
        g1.pass_on()
        s0.step(0)
        arrive(*g1.second)

    def before_3():
        s0.step(1)
        arrive(*g1.on)

    staged(4, {1: before_1, 2: before_2, 3: before_3}, unit)
    s1.begin()
    s0.step(2)

    def chunk_step(h):
        each_step(lambda v: grad_step(h, 0, v))
        pl.when(h == 1)(d01.relay_b)
        each_step(lambda n: product_step(h, 0, n), lambda v: grad_step(h, 1, v))

        @pl.when(h == 0)
        def _():
            d00.send(0, 1)
            d01.send(0, 1)
            d00.send(2)
            d01.send(2)
            s1.step(0)

        @pl.when(h == 1)
        def _():
            d10.send(0, 1)
            d11.send(0, 1)
            d10.send(2)
            d11.send(2)
            d00.end_b()

        each_step(lambda n: product_step(h, 1, n))

    def before_chunk_1():
        d00.send(3)
        d01.send(3)
        s1.step(1)
        d00.relay_b()
        s1.step(2)

    staged(H, {1: before_chunk_1}, chunk_step)
    d10.send(3)
    d11.send(3)
    own_stats()

    def weight_sent(n, *then):
        def action():
            start(weight_copies[n])
            for step in then:
                step()

        return action

    def weight_came(n, *then):
        def action():
            arrive(weight_copies[n])
            for step in then:
                step()

        return action

    staged(4, {1: weight_sent(0, d01.end_b), 2: weight_sent(1, d10.relay_b), 3: weight_sent(2)}, weight_other)
    start(weight_copies[3])
    d11.relay_b()

    def before_own_1():
        d00.end_a()
        z0.send(0)

    def before_own_2():
        d01.end_a()
        z0.send(1)

    staged(4, {0: weight_came(0), 1: weight_came(1, before_own_1), 2: weight_came(2, before_own_2),
               3: weight_came(3)}, weight_own)
    d10.end_b()
    d11.end_b()
    d10.end_a()
    z1.send(0)
    z0.end()
    own_stats_store()
    d11.end_a()
    z1.send(1)
    last = [z1.sibling] + [copy for both in z1.others for copy in both]
    for copy in copies:
        if not any(copy is other for other in last):
            copy.wait_send()
    z1.end()
    for copy in last:
        copy.wait_send()


def call(hid, w, ids, adv):
    vmem = pl.BlockSpec(memory_space=pltpu.VMEM)
    anywhere = pl.BlockSpec(memory_space=pl.ANY)
    scratch = [
        pltpu.VMEM((NB, 2, RING, R, D), BF16),
        pltpu.VMEM((V, D), BF16),
        pltpu.VMEM((NB, V, BLK), F32),
        pltpu.VMEM((NB, V, BLK), BF16),
        pltpu.VMEM((2, 2 * BLK, V), BF16),
        pltpu.VMEM((H, 2, 4, HALF, DC), F32),
        pltpu.VMEM((H, 2, 6, HALF, DC), BF16),
        pltpu.VMEM((H, 2, 6, HALF, DC), BF16),
        pltpu.VMEM((H, 2, 2, HALF, DC), F32),
        pltpu.VMEM((H, 2, RING - 1, 2, R, DC), BF16),
        pltpu.VMEM((H, 2, RING - 1, 2, R, DC), BF16),
        pltpu.VMEM((H, NZ, 2, 2, R, 128), F32),
        pltpu.VMEM((H, 2, NZ, 2, R, 128), F32),
        pltpu.VMEM((NB, 4, BLK), F32),
        pltpu.VMEM((H, RING - 1, RING, 4, BLK), F32),
        pltpu.VMEM((H, RING - 1, RING, 4, BLK), F32),
        pltpu.VMEM((H, NZ - 1, RING, 4, BLK), F32),
        pltpu.VMEM((3, NB, 4, BLK), F32),
        pltpu.VMEM((16, 128), jnp.int32),
        pltpu.VMEM((16, 128), F32),
        pltpu.VMEM((16, 128), F32),
        pltpu.VMEM((NB, 1, BLK), jnp.int32),
        pltpu.VMEM((NB, 1, BLK), F32),
        pltpu.VMEM((2, 2, 8, 128), F32),
        pltpu.VMEM((D // NC, ROWS, NC), BF16),
        pltpu.VMEM((D // NC, ROWS, NC), BF16),
        pltpu.SemaphoreType.DMA((NSEM,)),
        pltpu.SemaphoreType.DMA((NSEM,)),
        pltpu.SemaphoreType.DMA((H, NZ, 2)),
        pltpu.SemaphoreType.DMA((3 + H,)),
    ]
    return pl.pallas_call(
        kernel,
        out_shape=(
            pltpu.VMEM((ROWS, D), F32),
            pltpu.VMEM((2, H, 2, R, 128), F32),
            pltpu.VMEM((1, SHARD), F32),
            pltpu.VMEM((1, SHARD), F32),
        ),
        in_specs=[anywhere] * 4,
        out_specs=(vmem, vmem, vmem, vmem),
        scratch_shapes=scratch,
        compiler_params=pltpu.CompilerParams(
            collective_id=0, has_side_effects=True, vmem_limit_bytes=50 * 2**20),
    )(hid, w, ids, adv)


def store_kernel(*refs):
    count = len(refs) // 2
    moves = [pltpu.make_async_copy(refs[i], refs[count + i], refs[-1].at[i]) for i in range(count)]
    for move in moves:
        move.start()
    for move in moves:
        move.wait()


def store(*arrays):
    return pl.pallas_call(
        store_kernel,
        out_shape=[jax.ShapeDtypeStruct(a.shape, a.dtype) for a in arrays],
        in_specs=[pl.BlockSpec(memory_space=pltpu.VMEM)] * len(arrays),
        out_specs=[pl.BlockSpec(memory_space=pl.ANY)] * len(arrays),
        scratch_shapes=[pltpu.SemaphoreType.DMA((len(arrays),))],
        compiler_params=pltpu.CompilerParams(vmem_limit_bytes=4 * 2**20),
    )(*arrays)


def shards(hidden, head_weight, sampled_ids, advantage):
    hid = hidden.reshape(2, H, 2, R, D)
    grad_weight, grad_hidden, log_prob, entropy = store(*call(
        hid, head_weight, sampled_ids.reshape(16, 128), advantage.reshape(16, 128)))
    return (log_prob.reshape(SHARD), entropy.reshape(SHARD), grad_hidden.reshape(SHARD, 128), grad_weight)


def solution(mesh):
    placed = (P("dp", None), P(("dp", "vocab"), None), P(), P())
    return jax.shard_map(
        shards,
        mesh=mesh,
        in_specs=placed,
        out_specs=(P("dp"), P("dp"), P("dp", "vocab"), P(("dp", "vocab"), None)),
        check_vma=False,
    )
```
